32 devices in a mesh: dp: 8 (over y, x, core), sp: 4 (over z).
Axes of the slice: x: 2, y: 2, z: 4, core: 2. Of those that a mesh axis runs over, the one named last changes fastest.
Arguments:
- tokens: bfloat16 [16, 1024, 1024], P('dp', 'sp'), may hold values from -6 to 6
- timestep: int32 [16], P('dp'), may hold values from 0 to 4999
- segment_ids: int32 [16, 1024], P('dp', 'sp'), may hold values from 0 to 1023, as said below
- cotangent: bfloat16 [16, 1024, 1024], P('dp', 'sp'), may hold values from -6 to 6
- time_weight: bfloat16 [1024, 1024], P(('dp', 'sp')), may hold values from -0.1875 to 0.1875
- qkv_weight: bfloat16 [1024, 3072], P(('dp', 'sp')), may hold values from -0.1875 to 0.1875
- qv_bias: bfloat16 [2048], P(('dp', 'sp')), may hold values from -3 to 3
- out_weight: bfloat16 [1024, 1024], P(('dp', 'sp')), may hold values from -0.75 to 0.75
- out_bias: bfloat16 [1024], P(('dp', 'sp')), may hold values from -3 to 3
- norm_gain: bfloat16 [1024], P(('dp', 'sp')), may hold values from 0.099609375 to 1.8984375
- norm_bias: bfloat16 [1024], P(('dp', 'sp')), may hold values from -3 to 3
- up_weight: bfloat16 [1024, 4096], P(('dp', 'sp')), may hold values from -0.1875 to 0.1875
- up_bias: bfloat16 [4096], P(('dp', 'sp')), may hold values from -3 to 3
- down_weight: bfloat16 [4096, 1024], P(('dp', 'sp')), may hold values from -0.09375 to 0.09375
- down_bias: bfloat16 [1024], P(('dp', 'sp')), may hold values from -3 to 3
- final_gain: bfloat16 [1024], P(('dp', 'sp')), may hold values from 0.099609375 to 1.8984375
- final_bias: bfloat16 [1024], P(('dp', 'sp')), may hold values from -3 to 3
Outputs:
- output: bfloat16 [16, 1024, 1024], P('dp', 'sp')
- input_grad: bfloat16 [16, 1024, 1024], P('dp', 'sp')
- grad_time_weight: float32 [1024, 1024], P(('dp', 'sp'))
- grad_qkv_weight: float32 [1024, 3072], P(('dp', 'sp'))
- grad_qv_bias: float32 [2048], P(('dp', 'sp'))
- grad_out_weight: float32 [1024, 1024], P(('dp', 'sp'))
- grad_out_bias: float32 [1024], P(('dp', 'sp'))
- grad_norm_gain: float32 [1024], P(('dp', 'sp'))
- grad_norm_bias: float32 [1024], P(('dp', 'sp'))
- grad_up_weight: float32 [1024, 4096], P(('dp', 'sp'))
- grad_up_bias: float32 [4096], P(('dp', 'sp'))
- grad_down_weight: float32 [4096, 1024], P(('dp', 'sp'))
- grad_down_bias: float32 [1024], P(('dp', 'sp'))
- grad_final_gain: float32 [1024], P(('dp', 'sp'))
- grad_final_bias: float32 [1024], P(('dp', 'sp'))
The draws below stay inside these ranges and needn't reach their ends.
Inputs may be any that keep to these rules, and one draw needn't show every extreme that they name: `segment_ids`: each position's id is the position within its row at which its document begins; attention stays within one document of one row.
All inputs are finite; a program needn't handle non-finite values.
Results may differ from the reference program's by a relative error of at most 0.02.
Values may be sent and summed in bfloat16 or wider, within the bound.
No kernel may reach another device: no remote copies, remote signals or barrier semaphores. Data moves between devices by JAX's collectives and lax.ppermute only.
A program may use at most 256 MiB of HBM per device.

```python
import math
import jax
import jax.numpy as jnp
from jax import lax

D = 1024
HEADS = 16
HEAD_DIM = 64
FF = 4096
LEN = 1024
DOC = 128
TSTEPS = 5000
ROWS_DEV = 2
ROWS = 16
PIECE = 256


def draw_segment_ids(key, part):
    key = jax.random.fold_in(key, 11)
    start_key, chosen_key = jax.random.split(key)
    position = jnp.arange(LEN, dtype=jnp.int32)
    starts = jax.random.randint(start_key, (ROWS, LEN), 0, DOC) == 0
    starts = starts | (position == 0)[None, :]
    chosen = jax.random.randint(chosen_key, (ROWS // ROWS_DEV,), 0, ROWS_DEV)
    row_index = jnp.arange(ROWS, dtype=jnp.int32)
    spanning = row_index % ROWS_DEV == jnp.repeat(chosen, ROWS_DEV)
    inner = (position >= PIECE) & (position <= LEN - PIECE)
    starts = starts & jnp.logical_not(spanning[:, None] & inner[None, :])
    marked = jnp.where(starts, position[None, :], 0)
    return lax.cummax(marked, axis=1).astype(jnp.int32)


def place_ends(values, key, smallest, high):
    spot = [jax.random.randint(jax.random.fold_in(key, axis), (), 0, length) for axis, length in enumerate(values.shape)]
    longest = values.shape.index(max(values.shape))
    next_to = spot[:longest] + [(spot[longest] + 1) % values.shape[longest]] + spot[longest + 1:]
    return values.at[tuple(spot)].set(smallest).at[tuple(next_to)].set(high)


def with_spikes(values, stream_key, source, target, parts, factor):
    owner, partner = [(jnp.arange(values.shape[dim]) // (values.shape[dim] // parts)).reshape([-1 if axis == dim else 1 for axis in range(values.ndim)]) for dim in (source, target)]
    chosen = jax.random.permutation(stream_key, parts)[partner]
    strong = (owner == chosen) | (owner == (partner + parts // 2) % parts)
    return jnp.where(strong, factor * values, values)


def level_of(rng, dims, cuts, least, high):
    def one(axis_at, blocks):
        draws = jax.random.uniform(jax.random.fold_in(jax.random.fold_in(rng, 6), axis_at), (blocks,), jnp.float32, least / len(cuts), high / len(cuts))
        return jnp.repeat(jnp.exp(draws), dims[axis_at] // blocks).reshape((-1,) + (1,) * (len(dims) - axis_at - 1))

    factor_of = one(*cuts[0])
    for cut in cuts[1:]:
        factor_of = factor_of * one(*cut)
    return factor_of


def gaussian(rng, extent, deviation, limit, shards=(), kind=jnp.bfloat16):
    values = deviation * jax.random.normal(rng, extent, jnp.float32)
    if shards:
        values = values * level_of(rng, extent, shards, -0.22, 0.18)
    return jnp.clip(values, -limit, limit).astype(kind)


def heavy_noise(stream_key, extent, spread, bound, cuts, heavy, held_as=jnp.bfloat16):
    values = spread * jax.random.normal(stream_key, extent, jnp.float32)
    if cuts:
        values = values * level_of(stream_key, extent, cuts, -0.22, 0.18)
    return jnp.clip(with_spikes(values, jax.random.fold_in(stream_key, 3), *heavy), -bound, bound).astype(held_as)


def setup_inputs(seed: int = 0) -> dict:
    key_of = jax.random.split(jax.random.key(seed), 18)
    tokens = heavy_noise(key_of[0], (ROWS, LEN, D), 1.0, 6.0, ((0, 8), (1, 4)), (0, 2, 8, 2.0))
    timestep = place_ends(jax.random.randint(key_of[1], (ROWS,), 0, TSTEPS), jax.random.fold_in(key_of[1], 1), 0, TSTEPS - 1).astype(jnp.int32)
    segment_ids = draw_segment_ids(jax.random.fold_in(key_of[17], 71), 0)
    cotangent = gaussian(key_of[3], (ROWS, LEN, D), 1.0, 6.0, ((0, 8), (1, 4)))
    time_weight = gaussian(key_of[4], (D, D), D ** -0.5, 0.1875, ((0, 32),))
    qkv_weight = gaussian(key_of[5], (D, 3 * D), D ** -0.5, 0.1875, ((0, 32),))
    qv_bias = gaussian(key_of[6], (2 * D,), 0.5, 3.0, ((0, 32),))
    out_weight = gaussian(key_of[7], (D, D), (D // 16) ** -0.5, 0.75, ((0, 32),))
    out_bias = gaussian(key_of[8], (D,), 0.5, 3.0, ((0, 32),))
    norm_gain = jnp.clip(1.0 + 0.18 * jax.random.normal(key_of[9], (D,), jnp.float32), 0.099609375, 1.8984375).astype(jnp.bfloat16)
    norm_bias = gaussian(key_of[10], (D,), 0.5, 3.0, ((0, 32),))
    up_weight = gaussian(key_of[11], (D, FF), D ** -0.5, 0.1875, ((0, 32),))
    up_bias = gaussian(key_of[12], (FF,), 0.5, 3.0, ((0, 32),))
    down_weight = gaussian(key_of[13], (FF, D), FF ** -0.5, 0.09375, ((0, 32),))
    down_bias = gaussian(key_of[14], (D,), 0.5, 3.0, ((0, 32),))
    final_gain = jnp.clip(1.0 + 0.18 * jax.random.normal(key_of[15], (D,), jnp.float32), 0.099609375, 1.8984375).astype(jnp.bfloat16)
    final_bias = gaussian(key_of[16], (D,), 0.5, 3.0, ((0, 32),))
    return dict(tokens=tokens, timestep=timestep, segment_ids=segment_ids, cotangent=cotangent, time_weight=time_weight, qkv_weight=qkv_weight, qv_bias=qv_bias, out_weight=out_weight, out_bias=out_bias, norm_gain=norm_gain, norm_bias=norm_bias, up_weight=up_weight, up_bias=up_bias, down_weight=down_weight, down_bias=down_bias, final_gain=final_gain, final_bias=final_bias)


@jax.custom_vjp
def low(v):
    return lax.optimization_barrier(v.astype(jnp.bfloat16)).astype(jnp.float32)

@jax.custom_vjp
def low_back(v):
    return v

def low_keep(v):
    return (low(v), None)

def low_pass(kept, grad):
    return (grad,)

def back_keep(v):
    return (v, None)

def back_low(kept, grad):
    return (low(grad),)
low.defvjp(low_keep, low_pass)
low_back.defvjp(back_keep, back_low)
EPSILON = 1e-05
HIGHEST_PRECISION = lax.Precision.HIGHEST

def matmul(left, right):
    return jnp.dot(left, right, precision=HIGHEST_PRECISION)

def layer_norm(values, gain, offset):
    center = values - lax.optimization_barrier(jnp.mean(values, axis=-1, keepdims=True))
    variance = lax.optimization_barrier(jnp.mean(center * center, axis=-1, keepdims=True))
    return center * lax.rsqrt(variance + EPSILON) * gain + offset

def time_features(stamps, model_width):
    halfway = model_width // 2
    frequency = jnp.exp(-math.log(10000.0) * jnp.arange(halfway, dtype=jnp.float32) / halfway)
    phases = stamps.astype(jnp.float32)[:, None] * frequency[None, :]
    return jnp.concatenate([jnp.sin(phases), jnp.cos(phases)], axis=1)

def row_forward(params, row_tokens, features, segments):
    time_weight, qkv_weight, qv_bias, out_weight, out_bias, norm_gain, norm_bias, up_weight, up_bias, down_weight, down_bias, final_gain, final_bias = params
    hidden = row_tokens + matmul(low(features)[None, :], time_weight)
    qkv_shift = jnp.concatenate([qv_bias[:D], jnp.zeros((D,), jnp.float32), qv_bias[D:]])
    packed = low(low_back(matmul(low(hidden), qkv_weight) + qkv_shift))
    queries = packed[:, :D].reshape(LEN, HEADS, HEAD_DIM)
    keys_all = packed[:, D:2 * D].reshape(LEN, HEADS, HEAD_DIM)
    values_all = packed[:, 2 * D:].reshape(LEN, HEADS, HEAD_DIM)
    query_block = min(512, LEN)
    scale = 1.0 / math.sqrt(HEAD_DIM)

    def one_block(index):
        start = (index * query_block).astype(jnp.int32)
        query_part = lax.dynamic_slice_in_dim(queries, start, query_block, 0)
        segment_part = lax.dynamic_slice_in_dim(segments, start, query_block, 0)
        scores = low_back(jnp.einsum('qhd,khd->hqk', query_part, keys_all, precision=HIGHEST_PRECISION) * scale)
        allowed = segment_part[None, :, None] == segments[None, None, :]
        scores = jnp.where(allowed, scores, -1e+30)
        largest = lax.optimization_barrier(jnp.max(scores, axis=-1, keepdims=True))
        exponent = jnp.exp(scores - largest)
        probability = exponent / lax.optimization_barrier(jnp.sum(exponent, axis=-1, keepdims=True))
        return jnp.einsum('hqk,khd->qhd', low(probability), values_all, precision=HIGHEST_PRECISION)
    mixed = lax.map(jax.checkpoint(one_block), jnp.arange(LEN // query_block, dtype=jnp.int32))
    mixed = low(low_back(mixed.reshape(LEN, D)))
    attended = low_back(matmul(mixed, out_weight) + out_bias)
    normed = layer_norm(hidden + attended, norm_gain, norm_bias)
    upward = low_back(matmul(low(normed), up_weight) + up_bias)
    activated = low(jax.nn.gelu(upward, approximate=False))
    downward = low_back(matmul(activated, down_weight) + down_bias)
    return layer_norm(normed + downward, final_gain, final_bias)

def reference(tokens, timestep, segment_ids, cotangent, time_weight, qkv_weight, qv_bias, out_weight, out_bias, norm_gain, norm_bias, up_weight, up_bias, down_weight, down_bias, final_gain, final_bias):
    params = tuple((weight.astype(jnp.float32) for weight in (time_weight, qkv_weight, qv_bias, out_weight, out_bias, norm_gain, norm_bias, up_weight, up_bias, down_weight, down_bias, final_gain, final_bias)))

    def one_row(totals, row_inputs):
        row_tokens, stamp, segments, row_cotangent = row_inputs
        features = time_features(stamp[None], D)[0]
        result, pullback = jax.vjp(lambda weights, inputs: row_forward(weights, inputs, features, segments), params, row_tokens.astype(jnp.float32))
        weight_grads, token_grads = pullback(row_cotangent.astype(jnp.float32))
        totals = jax.tree.map(jnp.add, totals, weight_grads)
        return (totals, (result.astype(jnp.bfloat16), token_grads.astype(jnp.bfloat16)))
    starting = jax.tree.map(jnp.zeros_like, params)
    totals, (output, input_grad) = lax.scan(one_row, starting, (tokens, timestep, segment_ids, cotangent))
    return (output, input_grad, totals[0], totals[1], totals[2], totals[3], totals[4], totals[5], totals[6], totals[7], totals[8], totals[9], totals[10], totals[11], totals[12])
```

```python
import math

import jax
import jax.numpy as jnp
from jax import lax
from jax.experimental import pallas as pl
from jax.experimental.pallas import tpu as pltpu
from jax.sharding import PartitionSpec as P

HEADS = 16
HEAD_DIM = 64


EPSILON = 1e-05
INVERSE_ROOT_TWO = 1.0 / math.sqrt(2.0)
INVERSE_ROOT_TWO_PI = 1.0 / math.sqrt(2.0 * math.pi)


def time_features(stamps, model_width):
    halfway = model_width // 2
    frequency = jnp.exp(-math.log(10000.0) * jnp.arange(halfway, dtype=jnp.float32) / halfway)
    phases = stamps.astype(jnp.float32)[:, None] * frequency[None, :]
    return jnp.concatenate([jnp.sin(phases), jnp.cos(phases)], axis=1)


def layer_norm_parts(values, gain, offset):
    center = values - jnp.mean(values, axis=-1, keepdims=True)
    variance = jnp.mean(center * center, axis=-1, keepdims=True)
    inverse = lax.rsqrt(variance + EPSILON)
    normal_part = center * inverse
    return (normal_part * gain + offset, normal_part, inverse)


def layer_norm_back(upstream, normal_part, inverse, gain):
    scaled = upstream * gain
    return inverse * (
        scaled
        - jnp.mean(scaled, axis=-1, keepdims=True)
        - normal_part * jnp.mean(scaled * normal_part, axis=-1, keepdims=True)
    )


def gelu_slope(values):
    cumulative = 0.5 * (1.0 + lax.erf(values * INVERSE_ROOT_TWO))
    density = jnp.exp(-0.5 * values * values) * INVERSE_ROOT_TWO_PI
    return cumulative + values * density


def contract_rows(left, right):
    return lax.dot_general(
        left, right, (((0,), (0,)), ((), ())), preferred_element_type=jnp.float32
    )


def times_transposed(left, right):
    return lax.dot_general(
        left, right, (((1,), (1,)), ((), ())), preferred_element_type=jnp.float32
    )


def flatten_grads(grads):
    return tuple((grad.reshape(-1, 128) if grad.ndim == 2 else grad for grad in grads))


def restore_grads(shares, templates):
    return tuple((share.reshape(template.shape) for share, template in zip(shares, templates)))


def attention_forward(queries, keys_all, values_all, seg_full, query_block, scale):
    block_count = queries.shape[1] // query_block

    def one_block(index):
        start = index * query_block
        query_part = lax.dynamic_slice_in_dim(queries, start, query_block, 1)
        seg_part = lax.dynamic_slice_in_dim(seg_full, start, query_block, 1)
        scores = (
            jnp.einsum("rqhd,rkhd->rhqk", query_part, keys_all, preferred_element_type=jnp.float32)
            * scale
        )
        allowed = seg_part[:, None, :, None] == seg_full[:, None, None, :]
        scores = jnp.where(allowed, scores, -1e30)
        largest = jnp.max(scores, axis=-1, keepdims=True)
        exponent = jnp.exp(scores - largest)
        totals = jnp.sum(exponent, axis=-1, keepdims=True)
        probability = exponent / totals
        log_total = largest[..., 0] + jnp.log(totals[..., 0])
        mixed = jnp.einsum(
            "rhqk,rkhd->rqhd",
            probability.astype(jnp.bfloat16),
            values_all,
            preferred_element_type=jnp.float32,
        )
        return (mixed, log_total)

    mixed_blocks, log_totals = lax.map(one_block, jnp.arange(block_count, dtype=jnp.int32))
    mixed = jnp.moveaxis(mixed_blocks, 0, 1).reshape(queries.shape)
    return (mixed, log_totals)


def attention_backward(
    queries, keys_all, values_all, seg_full, grad_heads, log_totals, query_block, scale
):
    block_count = queries.shape[1] // query_block

    def one_block(carry, index):
        key_grad, value_grad = carry
        start = index * query_block
        query_part = lax.dynamic_slice_in_dim(queries, start, query_block, 1)
        seg_part = lax.dynamic_slice_in_dim(seg_full, start, query_block, 1)
        grad_part = lax.dynamic_slice_in_dim(grad_heads, start, query_block, 1)
        scores = (
            jnp.einsum("rqhd,rkhd->rhqk", query_part, keys_all, preferred_element_type=jnp.float32)
            * scale
        )
        allowed = seg_part[:, None, :, None] == seg_full[:, None, None, :]
        scores = jnp.where(allowed, scores, -1e30)
        probability = jnp.exp(scores - log_totals[index][..., None])
        dotted = jnp.einsum(
            "rqhd,rkhd->rhqk", grad_part, values_all, preferred_element_type=jnp.float32
        )
        center = jnp.sum(probability * dotted, axis=-1, keepdims=True)
        score_grad = (probability * (dotted - center)).astype(jnp.bfloat16)
        query_grad = (
            jnp.einsum("rhqk,rkhd->rqhd", score_grad, keys_all, preferred_element_type=jnp.float32)
            * scale
        )
        key_grad = (
            key_grad
            + jnp.einsum(
                "rhqk,rqhd->rkhd", score_grad, query_part, preferred_element_type=jnp.float32
            )
            * scale
        )
        value_grad = value_grad + jnp.einsum(
            "rhqk,rqhd->rkhd",
            probability.astype(jnp.bfloat16),
            grad_part,
            preferred_element_type=jnp.float32,
        )
        return ((key_grad, value_grad), query_grad)

    starting = (jnp.zeros(keys_all.shape, jnp.float32), jnp.zeros(values_all.shape, jnp.float32))
    (key_grad, value_grad), query_blocks = lax.scan(
        one_block, starting, jnp.arange(block_count, dtype=jnp.int32)
    )
    query_grad = jnp.moveaxis(query_blocks, 0, 1).reshape(queries.shape)
    return (query_grad, key_grad, value_grad)


def body(
    tokens,
    timestep,
    segment_ids,
    cotangent,
    time_weight,
    qkv_weight,
    qv_bias,
    out_weight,
    out_bias,
    norm_gain,
    norm_bias,
    up_weight,
    up_bias,
    down_weight,
    down_bias,
    final_gain,
    final_bias,
):
    shards = (
        time_weight,
        qkv_weight,
        qv_bias,
        out_weight,
        out_bias,
        norm_gain,
        norm_bias,
        up_weight,
        up_bias,
        down_weight,
        down_bias,
        final_gain,
        final_bias,
    )
    sp_count = lax.axis_size("sp")
    micro_count = max(2, sp_count // 2)
    rows_local, piece_len, model_width = tokens.shape
    rows_micro = rows_local // micro_count
    seq_len = piece_len * sp_count
    width_local = model_width // sp_count
    heads_local = HEADS // sp_count
    query_block = min(512, seq_len)
    scale = 1.0 / math.sqrt(HEAD_DIM)
    tok_count = rows_micro * piece_len
    owned = tuple((jnp.zeros(piece.shape, jnp.float32) for piece in shards))
    output_parts = []
    input_parts = []
    for micro in range(micro_count):
        first_row = micro * rows_micro
        block_tokens = tokens[first_row : first_row + rows_micro]
        block_cotangent = cotangent[first_row : first_row + rows_micro]
        block_segments = segment_ids[first_row : first_row + rows_micro]
        block_stamps = timestep[first_row : first_row + rows_micro]
        gathered = (
            lax.all_gather(shards[0], ("dp", "sp"), axis=0, tiled=True),
            lax.all_gather(shards[1], ("dp", "sp"), axis=0, tiled=True),
            lax.all_gather(shards[2], ("dp", "sp"), axis=0, tiled=True),
            lax.all_gather(shards[3], ("dp", "sp"), axis=0, tiled=True),
            lax.all_gather(shards[4], ("dp", "sp"), axis=0, tiled=True),
            lax.all_gather(shards[5], ("dp", "sp"), axis=0, tiled=True),
            lax.all_gather(shards[6], ("dp", "sp"), axis=0, tiled=True),
            lax.all_gather(shards[7], ("dp", "sp"), axis=0, tiled=True),
            lax.all_gather(shards[8], ("dp", "sp"), axis=0, tiled=True),
            lax.all_gather(shards[9], ("dp", "sp"), axis=0, tiled=True),
            lax.all_gather(shards[10], ("dp", "sp"), axis=0, tiled=True),
            lax.all_gather(shards[11], ("dp", "sp"), axis=0, tiled=True),
            lax.all_gather(shards[12], ("dp", "sp"), axis=0, tiled=True),
        )
        (
            time_full,
            qkv_full,
            qv_full,
            out_full,
            out_shift,
            first_gain,
            first_shift,
            up_full,
            up_shift,
            down_full,
            down_shift,
            second_gain,
            second_shift,
        ) = gathered
        features = time_features(block_stamps, model_width).astype(jnp.bfloat16)
        embedded = jnp.dot(features, time_full, preferred_element_type=jnp.float32)
        hidden = block_tokens.astype(jnp.float32) + embedded[:, None, :]
        hidden_flat = hidden.reshape(tok_count, model_width)
        hidden_low = hidden_flat.astype(jnp.bfloat16)
        qv_float = qv_full.astype(jnp.float32)
        qkv_shift = jnp.concatenate(
            [qv_float[:model_width], jnp.zeros((model_width,), jnp.float32), qv_float[model_width:]]
        )
        packed = jnp.dot(hidden_low, qkv_full, preferred_element_type=jnp.float32) + qkv_shift
        packed = packed.astype(jnp.bfloat16).reshape(rows_micro, piece_len, 3, model_width)
        seg_copies = jnp.broadcast_to(
            block_segments[:, :, None, None], (rows_micro, piece_len, 1, sp_count)
        )
        packed_heads, seg_heads = (
            lax.all_to_all(packed, "sp", split_axis=3, concat_axis=1, tiled=True),
            lax.all_to_all(seg_copies, "sp", split_axis=3, concat_axis=1, tiled=True),
        )
        seg_full = seg_heads[:, :, 0, 0]
        head_shape = (rows_micro, seq_len, heads_local, HEAD_DIM)
        queries = packed_heads[:, :, 0].reshape(head_shape)
        keys_all = packed_heads[:, :, 1].reshape(head_shape)
        values_all = packed_heads[:, :, 2].reshape(head_shape)
        mixed, log_totals = attention_forward(
            queries, keys_all, values_all, seg_full, query_block, scale
        )
        mixed_low = mixed.astype(jnp.bfloat16).reshape(rows_micro, seq_len, width_local)
        mixed_local = lax.all_to_all(mixed_low, "sp", split_axis=1, concat_axis=2, tiled=True)
        mixed_flat = mixed_local.reshape(tok_count, model_width)
        attended = jnp.dot(
            mixed_flat, out_full, preferred_element_type=jnp.float32
        ) + out_shift.astype(jnp.float32)
        first_gain_f = first_gain.astype(jnp.float32)
        normed, normal_one, inverse_one = layer_norm_parts(
            hidden_flat + attended, first_gain_f, first_shift.astype(jnp.float32)
        )
        normed_low = normed.astype(jnp.bfloat16)
        upward = jnp.dot(normed_low, up_full, preferred_element_type=jnp.float32) + up_shift.astype(
            jnp.float32
        )
        activated = jax.nn.gelu(upward, approximate=False).astype(jnp.bfloat16)
        downward = jnp.dot(
            activated, down_full, preferred_element_type=jnp.float32
        ) + down_shift.astype(jnp.float32)
        second_gain_f = second_gain.astype(jnp.float32)
        result, normal_two, inverse_two = layer_norm_parts(
            normed + downward, second_gain_f, second_shift.astype(jnp.float32)
        )
        output_parts.append(result.astype(jnp.bfloat16).reshape(rows_micro, piece_len, model_width))
        upstream = block_cotangent.reshape(tok_count, model_width).astype(jnp.float32)
        grad_second_gain = jnp.sum(upstream * normal_two, axis=0)
        grad_second_shift = jnp.sum(upstream, axis=0)
        resid_two = layer_norm_back(upstream, normal_two, inverse_two, second_gain_f)
        down_grad = resid_two.astype(jnp.bfloat16)
        grad_down_shift = jnp.sum(down_grad, axis=0, dtype=jnp.float32)
        grad_down_full = contract_rows(activated, down_grad)
        act_grad = times_transposed(down_grad, down_full)
        up_grad = (act_grad * gelu_slope(upward)).astype(jnp.bfloat16)
        grad_up_shift = jnp.sum(up_grad, axis=0, dtype=jnp.float32)
        grad_up_full = contract_rows(normed_low, up_grad)
        normed_grad = resid_two + times_transposed(up_grad, up_full)
        grad_first_gain = jnp.sum(normed_grad * normal_one, axis=0)
        grad_first_shift = jnp.sum(normed_grad, axis=0)
        resid_one = layer_norm_back(normed_grad, normal_one, inverse_one, first_gain_f)
        attended_grad = resid_one.astype(jnp.bfloat16)
        grad_out_shift = jnp.sum(attended_grad, axis=0, dtype=jnp.float32)
        grad_out_full = contract_rows(mixed_flat, attended_grad)
        mixed_grad = times_transposed(attended_grad, out_full).astype(jnp.bfloat16)
        mixed_grad = mixed_grad.reshape(rows_micro, piece_len, model_width)
        grad_heads = lax.all_to_all(
            mixed_grad, "sp", split_axis=2, concat_axis=1, tiled=True
        ).reshape(head_shape)
        query_grad, key_grad, value_grad = attention_backward(
            queries, keys_all, values_all, seg_full, grad_heads, log_totals, query_block, scale
        )
        packed_grad = jnp.stack([query_grad, key_grad, value_grad], axis=2)
        packed_grad = packed_grad.reshape(rows_micro, seq_len, 3, width_local).astype(jnp.bfloat16)
        packed_local = lax.all_to_all(packed_grad, "sp", split_axis=1, concat_axis=3, tiled=True)
        packed_flat = packed_local.reshape(tok_count, 3 * model_width)
        third_sums = jnp.sum(packed_flat, axis=0, dtype=jnp.float32)
        grad_qv_full = jnp.concatenate([third_sums[:model_width], third_sums[2 * model_width :]])
        grad_qkv_full = contract_rows(hidden_low, packed_flat)
        hidden_grad = resid_one + times_transposed(packed_flat, qkv_full)
        input_parts.append(
            hidden_grad.astype(jnp.bfloat16).reshape(rows_micro, piece_len, model_width)
        )
        embed_grad = jnp.sum(hidden_grad.reshape(rows_micro, piece_len, model_width), axis=1)
        grad_time_full = jnp.dot(
            features.astype(jnp.float32).T, embed_grad, precision=lax.Precision.HIGHEST
        )
        grads = (
            grad_time_full,
            grad_qkv_full,
            grad_qv_full,
            grad_out_full,
            grad_out_shift,
            grad_first_gain,
            grad_first_shift,
            grad_up_full,
            grad_up_shift,
            grad_down_full,
            grad_down_shift,
            grad_second_gain,
            grad_second_shift,
        )
        shares = lax.psum_scatter(
            flatten_grads(grads), ("dp", "sp"), scatter_dimension=0, tiled=True
        )
        owned = jax.tree.map(jnp.add, owned, restore_grads(shares, owned))
    output = jnp.concatenate(output_parts, axis=0)
    input_grad = jnp.concatenate(input_parts, axis=0)
    return (
        output,
        input_grad,
        owned[0],
        owned[1],
        owned[2],
        owned[3],
        owned[4],
        owned[5],
        owned[6],
        owned[7],
        owned[8],
        owned[9],
        owned[10],
        owned[11],
        owned[12],
    )


AXES = ("dp", "sp")
BF = jnp.bfloat16
F32 = jnp.float32
NT = (((1,), (1,)), ((), ()))
TN = (((0,), (0,)), ((), ()))
NN = (((1,), (0,)), ((), ()))
VMEM_LIMIT = 48 * 1024 * 1024
CHIP_SLOTS = ((0, 0, 0), (0, 0, 1), (0, 1, 0), (0, 1, 1), (1, 0, 0), (1, 0, 1), (1, 1, 0), (1, 1, 1))


def dot(left, right, dims=NN):
    return lax.dot_general(left, right, dims, preferred_element_type=F32)


def device_perm(target):
    pairs = []
    for y in range(2):
        for x in range(2):
            for c in range(2):
                for z in range(4):
                    ty, tx, tc, tz = target(y, x, c, z)
                    source = ((y * 2 + x) * 2 + c) * 4 + z
                    pairs.append((source, ((ty * 2 + tx) * 2 + tc) * 4 + tz))
    return pairs


PAIR = device_perm(lambda y, x, c, z: (y, x, 1 - c, z))
ALONG_X = device_perm(lambda y, x, c, z: (y, 1 - x, c, z))
ALONG_Y = device_perm(lambda y, x, c, z: (1 - y, x, c, z))
DIAGONAL = device_perm(lambda y, x, c, z: (1 - y, 1 - x, c, z))
SHIFT_Z = [device_perm(lambda y, x, c, z, k=k: (y, x, c, (z + k) % 4)) for k in range(4)]
ROW_OUT = [device_perm(lambda y, x, c, z, k=k: (y, x, z // 2, c * 2 + (z + k) % 2)) for k in range(2)]
ROW_BACK = [[(t, s) for s, t in pairs] for pairs in ROW_OUT]


def send(value, pairs):
    return lax.ppermute(value, AXES, pairs)


def gather_pieces(shard):
    near = [shard] + [send(shard, SHIFT_Z[k]) for k in (1, 2, 3)]
    first, second = jnp.stack(near[:2]), jnp.stack(near[2:])
    first_x, second_y = send(first, ALONG_X), send(second, ALONG_Y)
    first_y, second_x = send(first, ALONG_Y), send(second, ALONG_X)
    first_xy, second_xy = send(first_x, ALONG_Y), send(second_y, ALONG_X)
    return [first, first_x, first_y, first_xy, second, second_x, second_y, second_xy]


def scatter_pieces(first_keep, first_send, second_keep, second_send):
    add = lambda a, b: (a.astype(F32) + b.astype(F32)).astype(BF)
    from_y, from_x = send(first_send, ALONG_Y), send(second_send, ALONG_X)
    to_x = add(first_keep[1], from_y[1])
    to_y = add(second_keep[1], from_x[1])
    from_x, from_y, mine_first, mine_second = (
        send(to_x, ALONG_X),
        send(to_y, ALONG_Y),
        add(first_keep[0], from_y[0]),
        add(second_keep[0], from_x[0]),
    )
    far = [
        send(add(mine_first[1], from_x[1]), SHIFT_Z[1]),
        send(add(mine_second[0], from_y[0]), SHIFT_Z[2]),
        send(add(mine_second[1], from_y[1]), SHIFT_Z[3]),
    ]
    total = mine_first[0].astype(F32) + from_x[0].astype(F32)
    return total + far[0].astype(F32) + far[1].astype(F32) + far[2].astype(F32)


def place(meta, slot, j):
    half, y_rel, x_rel = CHIP_SLOTS[slot]
    y = lax.rem(meta[0] + y_rel, 2)
    x = lax.rem(meta[1] + x_rel, 2)
    z = lax.rem(meta[3] + 4 - (2 * half + j), 4)
    return y * 2 + x, z


def load_all(copies):
    for copy in copies:
        copy.start()
    for copy in copies:
        copy.wait()


def load_split_rows(meta, refs, base, blocks, weight, sem):
    copies = []
    for slot, ref in enumerate(refs):
        for j in range(2):
            chip, z = place(meta, slot, j)
            for other in range(2):
                core = lax.rem(meta[2] + other, 2)
                row = pl.multiple_of((chip * 2 + core) * 128 + z * 32, 32)
                copies.append(
                    pltpu.make_async_copy(
                        ref.at[j, pl.ds(base + other * blocks, blocks)],
                        weight.at[:, pl.ds(row, 32), :],
                        sem.at[(slot * 2 + j) * 2 + other],
                    )
                )
    return copies


def load_own_rows(meta, refs, base, blocks, rows, weight, sem):
    copies = []
    for slot, ref in enumerate(refs):
        for j in range(2):
            chip, z = place(meta, slot, j)
            row = pl.multiple_of((chip * 4 + z) * rows, 32)
            copies.append(
                pltpu.make_async_copy(
                    ref.at[j, pl.ds(base, blocks)],
                    weight.at[:, pl.ds(row, rows), :],
                    sem.at[slot * 2 + j],
                )
            )
    return copies


def kernel_call(kernel, meta, operands, in_specs, out_specs, out_shape, scratch=(), grid=(4,), flops=0, moved=0, exps=0):
    return pl.pallas_call(
        kernel,
        grid_spec=pltpu.PrefetchScalarGridSpec(
            num_scalar_prefetch=1,
            grid=grid,
            in_specs=in_specs,
            out_specs=out_specs,
            scratch_shapes=list(scratch),
        ),
        out_shape=out_shape,
        compiler_params=pltpu.CompilerParams(vmem_limit_bytes=VMEM_LIMIT),
        cost_estimate=pl.CostEstimate(flops=flops, bytes_accessed=moved, transcendentals=exps),
    )(meta, *operands)


HBM = pl.BlockSpec(memory_space=pl.ANY)


def spec(shape, index):
    return pl.BlockSpec(shape, index)


def whole(shape):
    return pl.BlockSpec(shape, lambda i, m: (0,) * len(shape))


def shaped(shape, kind):
    return jax.ShapeDtypeStruct(shape, kind)


def low_block(i):
    return jnp.minimum(i, 1)


def high_block(i):
    return jnp.maximum(i - 2, 0)


def turned(i):
    return lax.rem(i + 2, 4)


def project_qkv(meta, own, other, embedded, shift, pieces):
    def kernel(m, own_ref, other_ref, emb_ref, shift_ref, *rest):
        refs, (hidden_ref, out_ref, weight, sem) = rest[:8], rest[8:]
        i = pl.program_id(0)

        @pl.when(i == 0)
        def _():
            load_all(load_split_rows(m, refs, 0, 3, weight, sem))

        tokens = jnp.where(i < 2, own_ref[...].astype(F32), other_ref[...].astype(F32))
        hidden = (tokens + emb_ref[...]).astype(BF)
        hidden_ref[...] = hidden
        for t in range(3):
            out_ref[t] = (dot(hidden, weight[t]) + shift_ref[t : t + 1, :]).astype(BF)

    return kernel_call(
        kernel,
        meta,
        (own, other, embedded, shift, *pieces),
        [
            spec((256, 1024), lambda i, m: (low_block(i), 0)),
            spec((256, 1024), lambda i, m: (high_block(i), 0)),
            whole((1, 1024)),
            whole((3, 512)),
        ]
        + [HBM] * 8,
        [spec((256, 1024), lambda i, m: (i, 0)), spec((3, 256, 512), lambda i, m: (0, i, 0))],
        [shaped((1024, 1024), BF), shaped((3, 1024, 512), BF)],
        [pltpu.VMEM((3, 1024, 512), BF), pltpu.SemaphoreType.DMA((32,))],
        flops=2 * 1024 * 1024 * 1536,
        moved=10 << 20,
    )


def head_lanes(h, kind):
    lane = lax.broadcasted_iota(jnp.int32, (1, 128), 1)
    return jnp.where(lane // HEAD_DIM == h, 1.0, 0.0).astype(kind)


def attend(meta, qkv, seg_column, seg_row):
    def kernel(m, q_ref, k_ref, v_ref, column_ref, row_ref, out_ref, lse_ref):
        keys, values = k_ref[0], v_ref[0]
        for block in range(4):
            rows = pl.ds(block * 256, 256)
            queries = q_ref[0, rows, :] * jnp.asarray(0.125, BF)
            allowed = column_ref[rows, :] == row_ref[...]
            mixed = jnp.zeros((256, 128), F32)
            for h in range(2):
                lanes = head_lanes(h, BF)
                scores = jnp.where(allowed, dot(queries * lanes, keys, NT), -1e30)
                largest = jnp.max(scores, axis=1, keepdims=True)
                exponent = jnp.exp(scores - largest)
                total = jnp.sum(exponent, axis=1, keepdims=True)
                mixed += dot(exponent.astype(BF), values * lanes) / total
                lse = jnp.broadcast_to(largest + jnp.log(total), (256, 128))
                lse_ref[0, h : h + 1, rows] = jnp.transpose(lse)[0:1, :]
            out_ref[rows, :] = mixed.astype(BF)

    part = lambda t: spec((1, 1024, 128), lambda i, m: (t, 0, i))
    return kernel_call(
        kernel,
        meta,
        (qkv, qkv, qkv, seg_column, seg_row),
        [part(0), part(1), part(2), whole((1024, 1)), whole((1, 1024))],
        [spec((1024, 128), lambda i, m: (0, i)), spec((1, 8, 1024), lambda i, m: (i, 0, 0))],
        [shaped((1024, 512), BF), shaped((4, 8, 1024), F32)],
        flops=8 * 4 * 1024 * 1024 * 256,
        moved=5 << 20,
        exps=8 << 20,
    )


def attend_back(meta, qkv, out, grad, lse, seg_column, seg_row):
    def kernel(m, q_ref, k_ref, v_ref, out_ref, grad_ref, lse_ref, column_ref, row_ref, d_ref, sum_ref, dq):
        queries, upstream = q_ref[0], grad_ref[...]
        product = out_ref[...].astype(F32) * upstream.astype(F32)
        row = lax.broadcasted_iota(jnp.int32, (8, 128), 0)
        lane = lax.broadcasted_iota(jnp.int32, (8, 128), 1)
        picked = jnp.where(lane // HEAD_DIM == row, 1.0, 0.0).astype(F32)
        center = lax.dot_general(picked, product, NT, precision=lax.Precision.HIGHEST, preferred_element_type=F32)
        dq[...] = jnp.zeros_like(dq)
        value_sum = jnp.zeros((1, 128), F32)
        for block in range(4):
            rows = pl.ds(block * 256, 256)
            keys, values = k_ref[0, rows, :], v_ref[0, rows, :]
            allowed = column_ref[rows, :] == row_ref[...]
            dk = jnp.zeros((256, 128), F32)
            dv = jnp.zeros((256, 128), F32)
            for h in range(2):
                lanes = head_lanes(h, BF)
                keys_h = keys * lanes
                scores = dot(keys_h * jnp.asarray(0.125, BF), queries, NT)
                prob = jnp.where(allowed, jnp.exp(scores - lse_ref[0, h : h + 1, :]), 0.0)
                dp = dot(values * lanes, upstream, NT)
                ds = (prob * (dp - center[h : h + 1, :])).astype(BF)
                dv += dot(prob.astype(BF), upstream * lanes)
                dk += dot(ds, queries * lanes)
                dq[...] += dot(ds, keys_h, TN)
            dv = dv.astype(BF)
            d_ref[1, rows, :] = (dk * 0.125).astype(BF)
            d_ref[2, rows, :] = dv
            value_sum += jnp.sum(dv.astype(F32), axis=0, keepdims=True)
        final = (dq[...] * 0.125).astype(BF)
        d_ref[0] = final
        sum_ref[0:1, :] = jnp.sum(final.astype(F32), axis=0, keepdims=True)
        sum_ref[1:2, :] = value_sum

    part = lambda t: spec((1, 1024, 128), lambda i, m: (t, 0, i))
    heads = spec((1024, 128), lambda i, m: (0, i))
    return kernel_call(
        kernel,
        meta,
        (qkv, qkv, qkv, out, grad, lse, seg_column, seg_row),
        [part(0), part(1), part(2), heads, heads, spec((1, 8, 1024), lambda i, m: (i, 0, 0)), whole((1024, 1)), whole((1, 1024))],
        [spec((3, 1024, 128), lambda i, m: (0, 0, i)), spec((8, 128), lambda i, m: (0, i))],
        [shaped((3, 1024, 512), BF), shaped((8, 512), F32)],
        [pltpu.VMEM((1024, 128), F32)],
        flops=8 * 10 * 1024 * 1024 * 256,
        moved=8 << 20,
        exps=8 << 20,
    )


def project_out(meta, mixed, pieces):
    def kernel(m, x_ref, *rest):
        refs, (send_ref, own_ref, weight, sem) = rest[:8], rest[8:]
        i = pl.program_id(0)

        @pl.when(i == 0)
        def _():
            load_all(load_own_rows(m, refs, 0, 2, 32, weight, sem))

        for b in range(2):
            columns = pl.ds(b * 512, 512)
            result = dot(x_ref[...], weight[b])

            @pl.when(i < 2)
            def _():
                send_ref[:, columns] = result.astype(BF)

            @pl.when(i >= 2)
            def _():
                own_ref[:, columns] = result

    return kernel_call(
        kernel,
        meta,
        (mixed, *pieces),
        [spec((256, 512), lambda i, m: (turned(i), 0))] + [HBM] * 8,
        [spec((256, 1024), lambda i, m: (low_block(i), 0)), spec((256, 1024), lambda i, m: (high_block(i), 0))],
        [shaped((512, 1024), BF), shaped((512, 1024), F32)],
        [pltpu.VMEM((2, 512, 512), BF), pltpu.SemaphoreType.DMA((16,))],
        flops=2 * 1024 * 1024 * 512,
        moved=6 << 20,
    )


def normal_parts(values):
    center = values - jnp.mean(values, axis=-1, keepdims=True)
    inverse = lax.rsqrt(jnp.mean(center * center, axis=-1, keepdims=True) + EPSILON)
    return center * inverse, inverse


def normal_back(upstream, normal_part, inverse, gain):
    scaled = upstream * gain
    return inverse * (
        scaled
        - jnp.mean(scaled, axis=-1, keepdims=True)
        - normal_part * jnp.mean(scaled * normal_part, axis=-1, keepdims=True)
    )


ROWS128 = lambda i, m: (i, 0)


def first_norm(meta, tokens, embedded, own, received, vectors):
    def kernel(m, tok_ref, emb_ref, own_ref, recv_ref, vec_ref, normal_ref, inverse_ref, low_ref):
        hidden = tok_ref[...].astype(F32) + emb_ref[...]
        attended = own_ref[...] + recv_ref[...].astype(F32) + vec_ref[0:1, :]
        normal_part, inverse = normal_parts(hidden + attended)
        normal_ref[...] = normal_part
        inverse_ref[...] = jnp.broadcast_to(inverse, (128, 128))
        low_ref[...] = (normal_part * vec_ref[1:2, :] + vec_ref[2:3, :]).astype(BF)

    block = spec((128, 1024), ROWS128)
    return kernel_call(
        kernel,
        meta,
        (tokens, embedded, own, received, vectors),
        [block, whole((1, 1024)), block, block, whole((8, 1024))],
        [block, spec((128, 128), ROWS128), block],
        [shaped((512, 1024), F32), shaped((512, 128), F32), shaped((512, 1024), BF)],
        flops=512 * 1024 * 12,
        moved=8 << 20,
    )


def expand(meta, own, other, shift, pieces):
    def kernel(m, own_ref, other_ref, shift_ref, *rest):
        refs, (act_ref, slope_ref, weight, sem) = rest[:8], rest[8:]
        i = pl.program_id(0)

        @pl.when(i == 0)
        def _():
            load_all(load_split_rows(m, refs, 2, 4, weight, sem))

        x = jnp.where(i < 2, own_ref[...].astype(F32), other_ref[...].astype(F32)).astype(BF)
        for b in range(4):
            columns = pl.ds(b * 512, 512)
            u = dot(x, weight[b]) + shift_ref[:, columns]
            cumulative = 0.5 * (1.0 + lax.erf(u * INVERSE_ROOT_TWO))
            act_ref[:, columns] = (u * cumulative).astype(BF)
            density = jnp.exp(-0.5 * u * u) * INVERSE_ROOT_TWO_PI
            slope_ref[:, columns] = (cumulative + u * density).astype(BF)

    return kernel_call(
        kernel,
        meta,
        (own, other, shift, *pieces),
        [
            spec((256, 1024), lambda i, m: (low_block(i), 0)),
            spec((256, 1024), lambda i, m: (high_block(i), 0)),
            whole((1, 2048)),
        ]
        + [HBM] * 8,
        [spec((256, 2048), ROWS128), spec((256, 2048), ROWS128)],
        [shaped((1024, 2048), BF), shaped((1024, 2048), BF)],
        [pltpu.VMEM((4, 1024, 512), BF), pltpu.SemaphoreType.DMA((32,))],
        flops=2 * 1024 * 1024 * 2048,
        moved=14 << 20,
        exps=4 << 20,
    )


def contract(meta, activated, pieces):
    def kernel(m, x_ref, *rest):
        refs, (send_ref, own_ref, weight, sem) = rest[:8], rest[8:]
        i = pl.program_id(0)

        @pl.when(i == 0)
        def _():
            load_all(load_own_rows(m, refs, 0, 2, 128, weight, sem))

        for b in range(2):
            columns = pl.ds(b * 512, 512)
            result = dot(x_ref[...], weight[b])

            @pl.when(i < 2)
            def _():
                send_ref[:, columns] = result.astype(BF)

            @pl.when(i >= 2)
            def _():
                own_ref[:, columns] = result

    return kernel_call(
        kernel,
        meta,
        (activated, *pieces),
        [spec((256, 2048), lambda i, m: (turned(i), 0))] + [HBM] * 8,
        [spec((256, 1024), lambda i, m: (low_block(i), 0)), spec((256, 1024), lambda i, m: (high_block(i), 0))],
        [shaped((512, 1024), BF), shaped((512, 1024), F32)],
        [pltpu.VMEM((2, 2048, 512), BF), pltpu.SemaphoreType.DMA((16,))],
        flops=2 * 1024 * 1024 * 2048,
        moved=11 << 20,
    )


def row_sums(sum_ref, i, rows):
    @pl.when(i == 0)
    def _():
        sum_ref[...] = jnp.zeros_like(sum_ref)

    for n, value in enumerate(rows):
        sum_ref[n : n + 1, :] += jnp.sum(value, axis=0, keepdims=True)


def second_norm(meta, normal_one, own, received, cotangent, vectors):
    def kernel(m, normal_ref, own_ref, recv_ref, cot_ref, vec_ref, out_ref, resid_ref, low_ref, sum_ref):
        normed = normal_ref[...] * vec_ref[1:2, :] + vec_ref[2:3, :]
        downward = own_ref[...] + recv_ref[...].astype(F32) + vec_ref[3:4, :]
        normal_part, inverse = normal_parts(normed + downward)
        out_ref[...] = (normal_part * vec_ref[4:5, :] + vec_ref[5:6, :]).astype(BF)
        upstream = cot_ref[...].astype(F32)
        resid = normal_back(upstream, normal_part, inverse, vec_ref[4:5, :])
        resid_ref[...] = resid
        low = resid.astype(BF)
        low_ref[...] = low
        row_sums(sum_ref, pl.program_id(0), (upstream * normal_part, upstream, low.astype(F32)))

    block = spec((128, 1024), ROWS128)
    return kernel_call(
        kernel,
        meta,
        (normal_one, own, received, cotangent, vectors),
        [block, block, block, block, whole((8, 1024))],
        [block, block, block, whole((8, 1024))],
        [shaped((512, 1024), BF), shaped((512, 1024), F32), shaped((512, 1024), BF), shaped((8, 1024), F32)],
        flops=512 * 1024 * 30,
        moved=10 << 20,
    )


def feed_back(meta, own, other, slope, down_pieces, up_pieces):
    def kernel(m, own_ref, other_ref, slope_ref, *rest):
        down_refs, up_refs = rest[:8], rest[8:16]
        du_ref, send_ref, mine_ref, sum_ref, down, up, down_sem, up_sem = rest[16:]
        i = pl.program_id(0)

        @pl.when(i == 0)
        def _():
            load_all(
                load_own_rows(m, down_refs, 0, 2, 128, down, down_sem)
                + load_split_rows(m, up_refs, 2, 4, up, up_sem)
            )
            sum_ref[...] = jnp.zeros_like(sum_ref)

        df = jnp.where(i < 2, other_ref[...].astype(F32), own_ref[...].astype(F32)).astype(BF)
        total = jnp.zeros((256, 1024), F32)
        for b in range(4):
            rows = pl.ds(b * 512, 512)
            act = dot(df[:, :512], down[0, rows, :], NT) + dot(df[:, 512:], down[1, rows, :], NT)
            du = (act * slope_ref[:, rows].astype(F32)).astype(BF)
            du_ref[:, rows] = du
            sum_ref[0:1, rows] += jnp.sum(du.astype(F32), axis=0, keepdims=True)
            total += dot(du, up[b], NT)

        @pl.when(i < 2)
        def _():
            send_ref[...] = total.astype(BF)

        @pl.when(i >= 2)
        def _():
            mine_ref[...] = total

    return kernel_call(
        kernel,
        meta,
        (own, other, slope, *down_pieces, *up_pieces),
        [
            spec((256, 1024), lambda i, m: (high_block(i), 0)),
            spec((256, 1024), lambda i, m: (low_block(i), 0)),
            spec((256, 2048), lambda i, m: (turned(i), 0)),
        ]
        + [HBM] * 16,
        [
            spec((256, 2048), lambda i, m: (turned(i), 0)),
            spec((256, 1024), lambda i, m: (low_block(i), 0)),
            spec((256, 1024), lambda i, m: (high_block(i), 0)),
            whole((8, 2048)),
        ],
        [shaped((1024, 2048), BF), shaped((512, 1024), BF), shaped((512, 1024), F32), shaped((8, 2048), F32)],
        [
            pltpu.VMEM((2, 2048, 512), BF),
            pltpu.VMEM((4, 1024, 512), BF),
            pltpu.SemaphoreType.DMA((16,)),
            pltpu.SemaphoreType.DMA((32,)),
        ],
        flops=4 * 1024 * 1024 * 2048,
        moved=22 << 20,
    )


def first_norm_back(meta, resid, own, received, normal_one, inverse_one, vectors):
    def kernel(m, resid_ref, own_ref, recv_ref, normal_ref, inverse_ref, vec_ref, out_ref, low_ref, sum_ref):
        upstream = resid_ref[...] + own_ref[...] + recv_ref[...].astype(F32)
        normal_part = normal_ref[...]
        resid_one = normal_back(upstream, normal_part, inverse_ref[:, 0:1], vec_ref[1:2, :])
        out_ref[...] = resid_one
        low = resid_one.astype(BF)
        low_ref[...] = low
        row_sums(sum_ref, pl.program_id(0), (upstream * normal_part, upstream, low.astype(F32)))

    block = spec((128, 1024), ROWS128)
    return kernel_call(
        kernel,
        meta,
        (resid, own, received, normal_one, inverse_one, vectors),
        [block, block, block, block, spec((128, 128), ROWS128), whole((8, 1024))],
        [block, block, whole((8, 1024))],
        [shaped((512, 1024), F32), shaped((512, 1024), BF), shaped((8, 1024), F32)],
        flops=512 * 1024 * 20,
        moved=10 << 20,
    )


def output_back(meta, own, other, pieces):
    def kernel(m, own_ref, other_ref, *rest):
        refs, (out_ref, weight, sem) = rest[:8], rest[8:]
        i = pl.program_id(0)

        @pl.when(i == 0)
        def _():
            load_all(load_own_rows(m, refs, 0, 2, 32, weight, sem))

        da = jnp.where(i < 2, own_ref[...].astype(F32), other_ref[...].astype(F32)).astype(BF)
        out_ref[...] = (dot(da[:, :512], weight[0], NT) + dot(da[:, 512:], weight[1], NT)).astype(BF)

    return kernel_call(
        kernel,
        meta,
        (own, other, *pieces),
        [
            spec((256, 1024), lambda i, m: (low_block(i), 0)),
            spec((256, 1024), lambda i, m: (high_block(i), 0)),
        ]
        + [HBM] * 8,
        spec((256, 512), ROWS128),
        shaped((1024, 512), BF),
        [pltpu.VMEM((2, 512, 512), BF), pltpu.SemaphoreType.DMA((16,))],
        flops=2 * 1024 * 1024 * 512,
        moved=4 << 20,
    )


def rel_chip(s, m):
    return lax.rem(m[0] + s // 2, 2) * 2 + lax.rem(m[1] + lax.rem(s, 2), 2)


def piece_outputs(blocks, rows):
    shape = (2, 2, blocks, rows, 512)
    return [HBM] * 4, [shaped(shape, BF)] * 4


def push(s, outs, copy_for):
    first_keep, first_send, second_keep, second_send = outs
    slots = (
        ((first_keep, 0), (second_keep, 0)),
        ((first_keep, 1), (second_send, 0)),
        ((first_send, 0), (second_keep, 1)),
        ((first_send, 1), (second_send, 1)),
    )
    for n, (first, second) in enumerate(slots):

        @pl.when(s == n)
        def _(n=n, first=first, second=second):
            for k in range(4):
                ref, at = (first, second)[k // 2]
                for copy in copy_for(n, k, ref.at[at, k % 2]):
                    copy.start()

    @pl.when(s == 3)
    def _():
        for n, (first, second) in enumerate(slots):
            for k in range(4):
                ref, at = (first, second)[k // 2]
                for copy in copy_for(n, k, ref.at[at, k % 2]):
                    copy.wait()


def weigh_down(meta, activated, own, other):
    def kernel(m, x_ref, own_ref, other_ref, *rest):
        outs, (stage, sem) = rest[:4], rest[4:]
        s = pl.program_id(0)
        x = x_ref[...]
        for b in range(2):
            columns = pl.ds(b * 512, 512)
            stage[s, b] = (dot(x[:512], own_ref[:, columns], TN) + dot(x[512:], other_ref[:, columns], TN)).astype(BF)

        def copy_for(n, k, target):
            row = pl.multiple_of(lax.rem(m[3] + k, 4) * 128, 128)
            return [pltpu.make_async_copy(stage.at[n, :, pl.ds(row, 128), :], target, sem.at[n * 4 + k])]

        push(s, outs, copy_for)

    out_specs, out_shape = piece_outputs(2, 128)
    return kernel_call(
        kernel,
        meta,
        (activated, own, other),
        [spec((1024, 512), lambda s, m: (0, rel_chip(s, m))), whole((512, 1024)), whole((512, 1024))],
        out_specs,
        out_shape,
        [pltpu.VMEM((4, 2, 512, 512), BF), pltpu.SemaphoreType.DMA((16,))],
        flops=2 * 1024 * 1024 * 2048,
        moved=10 << 20,
    )


def weigh_up_out(meta, normed_own, normed_other, du, mixed, da_own, da_other):
    def kernel(m, own_ref, other_ref, du_ref, mixed_ref, da_own_ref, da_other_ref, *rest):
        outs, (up, out, sem) = rest[:4], rest[4:]
        s = pl.program_id(0)
        x = mixed_ref[...]
        for b in range(2):
            columns = pl.ds(b * 512, 512)
            out[s, b] = (dot(x[:512], da_own_ref[:, columns], TN) + dot(x[512:], da_other_ref[:, columns], TN)).astype(BF)
        for b in range(4):
            columns = pl.ds(b * 512, 512)
            up[s, b] = (dot(own_ref[...], du_ref[:512, columns], TN) + dot(other_ref[...], du_ref[512:, columns], TN)).astype(BF)

        def copy_for(n, k, target):
            z = lax.rem(m[3] + k, 4)
            copies = [
                pltpu.make_async_copy(
                    out.at[n, :, pl.ds(pl.multiple_of(z * 32, 32), 32), :],
                    target.at[pl.ds(0, 2)],
                    sem.at[(n * 4 + k) * 3],
                )
            ]
            for rel in range(2):
                row = pl.multiple_of(lax.rem(m[2] + rel, 2) * 128 + z * 32, 32)
                copies.append(
                    pltpu.make_async_copy(
                        up.at[n, :, pl.ds(row, 32), :],
                        target.at[pl.ds(2 + rel * 4, 4)],
                        sem.at[(n * 4 + k) * 3 + 1 + rel],
                    )
                )
            return copies

        push(s, outs, copy_for)

    out_specs, out_shape = piece_outputs(10, 32)
    return kernel_call(
        kernel,
        meta,
        (normed_own, normed_other, du, mixed, da_own, da_other),
        [
            spec((512, 256), lambda s, m: (0, rel_chip(s, m))),
            spec((512, 256), lambda s, m: (0, rel_chip(s, m))),
            whole((1024, 2048)),
            spec((1024, 128), lambda s, m: (0, rel_chip(s, m))),
            whole((512, 1024)),
            whole((512, 1024)),
        ],
        out_specs,
        out_shape,
        [pltpu.VMEM((4, 4, 256, 512), BF), pltpu.VMEM((4, 2, 128, 512), BF), pltpu.SemaphoreType.DMA((48,))],
        flops=2 * 1024 * 1024 * 2560,
        moved=15 << 20,
    )


def weigh_qkv(meta, hidden, dqkv):
    def kernel(m, x_ref, d_ref, *rest):
        outs, (stage, sem) = rest[:4], rest[4:]
        s = pl.program_id(0)
        for t in range(3):
            stage[s, t] = dot(x_ref[...], d_ref[t], TN).astype(BF)

        def copy_for(n, k, target):
            copies = []
            for rel in range(2):
                row = pl.multiple_of(lax.rem(m[2] + rel, 2) * 128 + lax.rem(m[3] + k, 4) * 32, 32)
                copies.append(
                    pltpu.make_async_copy(
                        stage.at[n, :, pl.ds(row, 32), :],
                        target.at[pl.ds(rel * 3, 3)],
                        sem.at[(n * 4 + k) * 2 + rel],
                    )
                )
            return copies

        push(s, outs, copy_for)

    out_specs, out_shape = piece_outputs(6, 32)
    return kernel_call(
        kernel,
        meta,
        (hidden, dqkv),
        [spec((1024, 256), lambda s, m: (0, rel_chip(s, m))), whole((3, 1024, 512))],
        out_specs,
        out_shape,
        [pltpu.VMEM((4, 3, 256, 512), BF), pltpu.SemaphoreType.DMA((32,))],
        flops=2 * 1024 * 1024 * 1536,
        moved=8 << 20,
    )


def qkv_back(meta, dqkv, pieces):
    def kernel(m, d_ref, *rest):
        refs, (send_ref, own_ref, weight, sem) = rest[:8], rest[8:]
        i = pl.program_id(0)

        @pl.when(i == 0)
        def _():
            load_all(load_split_rows(m, refs, 0, 3, weight, sem))

        total = dot(d_ref[0], weight[0], NT) + dot(d_ref[1], weight[1], NT) + dot(d_ref[2], weight[2], NT)

        @pl.when(i < 2)
        def _():
            send_ref[...] = total.astype(BF)

        @pl.when(i >= 2)
        def _():
            own_ref[...] = total

    return kernel_call(
        kernel,
        meta,
        (dqkv, *pieces),
        [spec((3, 256, 512), lambda i, m: (0, turned(i), 0))] + [HBM] * 8,
        [spec((256, 1024), lambda i, m: (low_block(i), 0)), spec((256, 1024), lambda i, m: (high_block(i), 0))],
        [shaped((512, 1024), BF), shaped((512, 1024), F32)],
        [pltpu.VMEM((3, 1024, 512), BF), pltpu.SemaphoreType.DMA((32,))],
        flops=2 * 1024 * 1024 * 1536,
        moved=9 << 20,
    )


def last_sum(meta, resid, own, received):
    def kernel(m, resid_ref, own_ref, recv_ref, out_ref, sum_ref):
        total = resid_ref[...] + own_ref[...] + recv_ref[...].astype(F32)
        out_ref[...] = total.astype(BF)
        row_sums(sum_ref, pl.program_id(0), (total,))

    block = spec((128, 1024), ROWS128)
    return kernel_call(
        kernel,
        meta,
        (resid, own, received),
        [block, block, block],
        [block, whole((8, 1024))],
        [shaped((512, 1024), BF), shaped((8, 1024), F32)],
        flops=512 * 1024 * 4,
        moved=6 << 20,
    )


VECTOR_SIZES = (64, 32, 32, 32, 128, 32, 32, 32)


def split_vectors(packed):
    parts, start = [], 0
    for size in VECTOR_SIZES:
        parts.append(packed[:, start : start + size])
        start += size
    return parts


def chip_body(
    tokens,
    timestep,
    segment_ids,
    cotangent,
    time_weight,
    qkv_weight,
    qv_bias,
    out_weight,
    out_bias,
    norm_gain,
    norm_bias,
    up_weight,
    up_bias,
    down_weight,
    down_bias,
    final_gain,
    final_bias,
):
    dp, z = lax.axis_index("dp"), lax.axis_index("sp")
    y, x, c = dp // 4, (dp // 2) % 2, dp % 2
    meta = jnp.stack([y, x, c, z]).astype(jnp.int32)
    pick = lambda value, index, axis: lax.dynamic_index_in_dim(value, index, axis, keepdims=False)

    qkv_split = qkv_weight.reshape(32, 3, 4, 2, 128)
    up_split = up_weight.reshape(32, 4, 2, 512)
    qkv_half = lambda core: pick(qkv_split, core, 3).reshape(32, 3, 512).transpose(1, 0, 2)
    up_half = lambda core: pick(up_split, core, 2).transpose(1, 0, 2)
    qkv_shard = jnp.concatenate([qkv_half(c), send(qkv_half(1 - c), PAIR)])
    out_shard = out_weight.reshape(32, 2, 512).transpose(1, 0, 2)
    mid_shard = jnp.concatenate([out_shard, up_half(c), send(up_half(1 - c), PAIR)])
    down_shard = down_weight.reshape(128, 2, 512).transpose(1, 0, 2)
    qkv_pieces = gather_pieces(qkv_shard)
    mid_pieces = gather_pieces(mid_shard)
    down_pieces = gather_pieces(down_shard)

    stamps = timestep.astype(jnp.int32)
    small = jnp.concatenate(
        [qv_bias, out_bias, norm_gain, norm_bias, up_bias, down_bias, final_gain, final_bias]
        + [(stamps // 64).astype(BF), (stamps % 64).astype(BF)]
    )[None]
    small = jnp.concatenate([small, send(small, PAIR)])
    small = jnp.stack([small] + [send(small, SHIFT_Z[k]) for k in (1, 2, 3)])
    small = jnp.stack([small] + [send(small, pairs) for pairs in (ALONG_X, ALONG_Y, DIAGONAL)])
    small = small.reshape(32, -1)
    natural = jnp.arange(32, dtype=jnp.int32)
    ny, nx, nc, nz = natural // 16, (natural // 8) % 2, (natural // 4) % 2, natural % 4
    source = (((ny ^ y) * 2 + (nx ^ x)) * 4 + (z + 4 - nz) % 4) * 2 + (nc ^ c)
    order = (source[:, None] == natural[None, :]).astype(BF)
    small = jnp.dot(order, small, preferred_element_type=F32)
    full = [part.reshape(1, -1) for part in split_vectors(small)]
    qv_full, out_shift, first_gain, first_shift, up_full, down_shift, second_gain, second_shift = full
    blank = jnp.zeros((2, 1024), F32)
    vectors = jnp.concatenate([out_shift, first_gain, first_shift, down_shift, second_gain, second_shift, blank])
    qv_mine = pick(qv_full.reshape(2, 4, 2, 128), c, 2).reshape(2, 512)
    qkv_shift = jnp.stack([qv_mine[0], jnp.zeros((512,), F32), qv_mine[1]])
    up_shift = pick(up_full.reshape(4, 2, 512), c, 1).reshape(1, 2048)

    all_stamps = (small[::4, 384:386] * 64.0 + small[::4, 386:388]).reshape(16)
    column = (dp * 4 + z) * 32 + jnp.arange(32, dtype=jnp.int32)
    frequency = jnp.exp(-math.log(10000.0) * (column % 512).astype(F32) / 512)
    rel = jnp.arange(16, dtype=jnp.int32)
    rel_row = ((rel // 8) ^ y) * 8 + (((rel // 4) % 2) ^ x) * 4

    def features_for(rows):
        phases = all_stamps[rows][:, None] * frequency[None, :]
        return jnp.where(column[None, :] < 512, jnp.sin(phases), jnp.cos(phases)).astype(BF)

    terms = jnp.dot(features_for(rel_row + (rel + z) % 4), time_weight, preferred_element_type=F32)
    terms = (terms + send(terms, PAIR)).reshape(4, 4, 1024)
    terms = terms[0] + send(terms[1], ALONG_X) + send(terms[2], ALONG_Y) + send(terms[3], DIAGONAL)
    embedded = terms[0:1]
    for k in (1, 2, 3):
        embedded = embedded + send(terms[k : k + 1], SHIFT_Z[k])

    def take_rows(value):
        return jnp.concatenate([send(pick(value, (z + k) % 2, 0), ROW_OUT[k]) for k in range(2)])

    def give_rows(value):
        parts = [send(value[k * 256 : (k + 1) * 256], ROW_BACK[k]) for k in range(2)]
        swapped = (z % 2) == 1
        return jnp.stack([jnp.where(swapped, parts[1], parts[0]), jnp.where(swapped, parts[0], parts[1])])

    own_tokens = take_rows(tokens)
    own_segments = take_rows(segment_ids)
    other_tokens = send(own_tokens, PAIR)
    segments = jnp.concatenate([own_segments, send(own_segments, PAIR)])
    seg_column, seg_row = segments[:, None], segments[None, :]
    own_cotangent = take_rows(cotangent)

    hidden, qkv = project_qkv(meta, own_tokens, other_tokens, embedded, qkv_shift, qkv_pieces)
    mixed, lse = attend(meta, qkv, seg_column, seg_row)
    away, mine = project_out(meta, mixed, mid_pieces)
    normal_one, inverse_one, normed = first_norm(meta, own_tokens, embedded, mine, send(away, PAIR), vectors)
    normed_other = send(normed, PAIR)
    activated, slope = expand(meta, normed, normed_other, up_shift, mid_pieces)
    away, mine = contract(meta, activated, down_pieces)
    result, resid_two, df, sums_two = second_norm(meta, normal_one, mine, send(away, PAIR), own_cotangent, vectors)
    output = give_rows(result)

    df_other = send(df, PAIR)
    down_share = scatter_pieces(*weigh_down(meta, activated, df, df_other))
    du, away, mine, up_sums = feed_back(meta, df, df_other, slope, down_pieces, mid_pieces)
    resid_one, da, sums_one = first_norm_back(meta, resid_two, mine, send(away, PAIR), normal_one, inverse_one, vectors)
    da_other = send(da, PAIR)
    dout = output_back(meta, da, da_other, mid_pieces)
    mid_share = scatter_pieces(*weigh_up_out(meta, normed, normed_other, du, mixed, da, da_other))
    dqkv, qv_sums = attend_back(meta, qkv, mixed, dout, lse, seg_column, seg_row)
    qkv_share = scatter_pieces(*weigh_qkv(meta, hidden, dqkv))
    away, mine = qkv_back(meta, dqkv, qkv_pieces)
    input_low, embed_sums = last_sum(meta, resid_one, mine, send(away, PAIR))
    input_grad = give_rows(input_low)

    def both_halves(own, received):
        return jnp.where(c == 0, jnp.stack([own, received], axis=-2), jnp.stack([received, own], axis=-2))

    grad_down = down_share.transpose(1, 0, 2).reshape(128, 1024)
    grad_out = mid_share[:2].transpose(1, 0, 2).reshape(32, 1024)
    grad_up = both_halves(mid_share[2:6], send(mid_share[6:], PAIR))
    grad_up = grad_up.transpose(1, 0, 2, 3).reshape(32, 4096)
    split = lambda share: share.reshape(3, 32, 4, 128)
    grad_qkv = both_halves(split(qkv_share[:3]), split(send(qkv_share[3:], PAIR)))
    grad_qkv = grad_qkv.transpose(1, 0, 2, 3, 4).reshape(32, 3072)

    core_lane = (jnp.arange(2) == c).astype(F32)
    spread = lambda sums, width: (sums.reshape(-1, 1, width) * core_lane[None, :, None]).reshape(32, -1)
    grads = jnp.concatenate(
        [
            spread(qv_sums[0:2], 128),
            sums_one[2].reshape(32, 32),
            sums_one[0].reshape(32, 32),
            sums_one[1].reshape(32, 32),
            spread(up_sums[0:1], 512),
            sums_two[2].reshape(32, 32),
            sums_two[0].reshape(32, 32),
            sums_two[1].reshape(32, 32),
        ],
        axis=1,
    ).reshape(4, 2, 4, 384)
    grads = pick(grads, c, 1) + send(pick(grads, 1 - c, 1), PAIR)
    rel_order = ((rel_row + (rel + z) % 4)[:, None] == rel[None, :]).astype(F32)
    grads = jnp.dot(rel_order, grads.reshape(16, 384), precision=lax.Precision.HIGHEST).reshape(4, 4, 384)
    grads = grads[0] + send(grads[1], ALONG_X) + send(grads[2], ALONG_Y) + send(grads[3], DIAGONAL)
    total = grads[0:1]
    for k in (1, 2, 3):
        total = total + send(grads[k : k + 1], SHIFT_Z[k])
    small_grads = [part.reshape(-1) for part in split_vectors(total)]

    sums = embed_sums[0:1]
    sums = sums + send(sums, PAIR)
    sums = jnp.concatenate([sums] + [send(sums, SHIFT_Z[k]) for k in (1, 2, 3)])
    sums = jnp.concatenate([sums] + [send(sums, pairs) for pairs in (ALONG_X, ALONG_Y, DIAGONAL)])
    features = features_for(rel_row + (z + 4 - rel % 4) % 4).astype(F32)
    grad_time = jnp.dot(features.T, sums, precision=lax.Precision.HIGHEST)

    return (
        output,
        input_grad,
        grad_time,
        grad_qkv,
        small_grads[0],
        grad_out,
        *small_grads[1:4],
        grad_up,
        small_grads[4],
        grad_down,
        *small_grads[5:],
    )


def solution(mesh):
    in_specs = (
        P("dp", "sp", None),
        P("dp"),
        P("dp", "sp"),
        P("dp", "sp", None),
        P(("dp", "sp"), None),
        P(("dp", "sp"), None),
        P(("dp", "sp")),
        P(("dp", "sp"), None),
        P(("dp", "sp")),
        P(("dp", "sp")),
        P(("dp", "sp")),
        P(("dp", "sp"), None),
        P(("dp", "sp")),
        P(("dp", "sp"), None),
        P(("dp", "sp")),
        P(("dp", "sp")),
        P(("dp", "sp")),
    )
    out_specs = (
        P("dp", "sp", None),
        P("dp", "sp", None),
        P(("dp", "sp"), None),
        P(("dp", "sp"), None),
        P(("dp", "sp")),
        P(("dp", "sp"), None),
        P(("dp", "sp")),
        P(("dp", "sp")),
        P(("dp", "sp")),
        P(("dp", "sp"), None),
        P(("dp", "sp")),
        P(("dp", "sp"), None),
        P(("dp", "sp")),
        P(("dp", "sp")),
        P(("dp", "sp")),
    )
    plan = chip_body if dict(mesh.shape) == {"dp": 8, "sp": 4} else body
    return jax.shard_map(plan, mesh=mesh, in_specs=in_specs, out_specs=out_specs, check_vma=False)
```

```python
import math

import jax
import jax.numpy as jnp
from jax import lax
from jax.experimental import pallas as pl
from jax.experimental.pallas import tpu as pltpu
from jax.sharding import PartitionSpec as P

HEADS = 16
HEAD_DIM = 64


EPSILON = 1e-05
INVERSE_ROOT_TWO = 1.0 / math.sqrt(2.0)
INVERSE_ROOT_TWO_PI = 1.0 / math.sqrt(2.0 * math.pi)


def time_features(stamps, model_width):
    halfway = model_width // 2
    frequency = jnp.exp(-math.log(10000.0) * jnp.arange(halfway, dtype=jnp.float32) / halfway)
    phases = stamps.astype(jnp.float32)[:, None] * frequency[None, :]
    return jnp.concatenate([jnp.sin(phases), jnp.cos(phases)], axis=1)


def layer_norm_parts(values, gain, offset):
    center = values - jnp.mean(values, axis=-1, keepdims=True)
    variance = jnp.mean(center * center, axis=-1, keepdims=True)
    inverse = lax.rsqrt(variance + EPSILON)
    normal_part = center * inverse
    return (normal_part * gain + offset, normal_part, inverse)


def layer_norm_back(upstream, normal_part, inverse, gain):
    scaled = upstream * gain
    return inverse * (
        scaled
        - jnp.mean(scaled, axis=-1, keepdims=True)
        - normal_part * jnp.mean(scaled * normal_part, axis=-1, keepdims=True)
    )


def gelu_slope(values):
    cumulative = 0.5 * (1.0 + lax.erf(values * INVERSE_ROOT_TWO))
    density = jnp.exp(-0.5 * values * values) * INVERSE_ROOT_TWO_PI
    return cumulative + values * density


def contract_rows(left, right):
    return lax.dot_general(
        left, right, (((0,), (0,)), ((), ())), preferred_element_type=jnp.float32
    )


def times_transposed(left, right):
    return lax.dot_general(
        left, right, (((1,), (1,)), ((), ())), preferred_element_type=jnp.float32
    )


def flatten_grads(grads):
    return tuple((grad.reshape(-1, 128) if grad.ndim == 2 else grad for grad in grads))


def restore_grads(shares, templates):
    return tuple((share.reshape(template.shape) for share, template in zip(shares, templates)))


def attention_forward(queries, keys_all, values_all, seg_full, query_block, scale):
    block_count = queries.shape[1] // query_block

    def one_block(index):
        start = index * query_block
        query_part = lax.dynamic_slice_in_dim(queries, start, query_block, 1)
        seg_part = lax.dynamic_slice_in_dim(seg_full, start, query_block, 1)
        scores = (
            jnp.einsum("rqhd,rkhd->rhqk", query_part, keys_all, preferred_element_type=jnp.float32)
            * scale
        )
        allowed = seg_part[:, None, :, None] == seg_full[:, None, None, :]
        scores = jnp.where(allowed, scores, -1e30)
        largest = jnp.max(scores, axis=-1, keepdims=True)
        exponent = jnp.exp(scores - largest)
        totals = jnp.sum(exponent, axis=-1, keepdims=True)
        probability = exponent / totals
        log_total = largest[..., 0] + jnp.log(totals[..., 0])
        mixed = jnp.einsum(
            "rhqk,rkhd->rqhd",
            probability.astype(jnp.bfloat16),
            values_all,
            preferred_element_type=jnp.float32,
        )
        return (mixed, log_total)

    mixed_blocks, log_totals = lax.map(one_block, jnp.arange(block_count, dtype=jnp.int32))
    mixed = jnp.moveaxis(mixed_blocks, 0, 1).reshape(queries.shape)
    return (mixed, log_totals)


def attention_backward(
    queries, keys_all, values_all, seg_full, grad_heads, log_totals, query_block, scale
):
    block_count = queries.shape[1] // query_block

    def one_block(carry, index):
        key_grad, value_grad = carry
        start = index * query_block
        query_part = lax.dynamic_slice_in_dim(queries, start, query_block, 1)
        seg_part = lax.dynamic_slice_in_dim(seg_full, start, query_block, 1)
        grad_part = lax.dynamic_slice_in_dim(grad_heads, start, query_block, 1)
        scores = (
            jnp.einsum("rqhd,rkhd->rhqk", query_part, keys_all, preferred_element_type=jnp.float32)
            * scale
        )
        allowed = seg_part[:, None, :, None] == seg_full[:, None, None, :]
        scores = jnp.where(allowed, scores, -1e30)
        probability = jnp.exp(scores - log_totals[index][..., None])
        dotted = jnp.einsum(
            "rqhd,rkhd->rhqk", grad_part, values_all, preferred_element_type=jnp.float32
        )
        center = jnp.sum(probability * dotted, axis=-1, keepdims=True)
        score_grad = (probability * (dotted - center)).astype(jnp.bfloat16)
        query_grad = (
            jnp.einsum("rhqk,rkhd->rqhd", score_grad, keys_all, preferred_element_type=jnp.float32)
            * scale
        )
        key_grad = (
            key_grad
            + jnp.einsum(
                "rhqk,rqhd->rkhd", score_grad, query_part, preferred_element_type=jnp.float32
            )
            * scale
        )
        value_grad = value_grad + jnp.einsum(
            "rhqk,rqhd->rkhd",
            probability.astype(jnp.bfloat16),
            grad_part,
            preferred_element_type=jnp.float32,
        )
        return ((key_grad, value_grad), query_grad)

    starting = (jnp.zeros(keys_all.shape, jnp.float32), jnp.zeros(values_all.shape, jnp.float32))
    (key_grad, value_grad), query_blocks = lax.scan(
        one_block, starting, jnp.arange(block_count, dtype=jnp.int32)
    )
    query_grad = jnp.moveaxis(query_blocks, 0, 1).reshape(queries.shape)
    return (query_grad, key_grad, value_grad)


def body(
    tokens,
    timestep,
    segment_ids,
    cotangent,
    time_weight,
    qkv_weight,
    qv_bias,
    out_weight,
    out_bias,
    norm_gain,
    norm_bias,
    up_weight,
    up_bias,
    down_weight,
    down_bias,
    final_gain,
    final_bias,
):
    shards = (
        time_weight,
        qkv_weight,
        qv_bias,
        out_weight,
        out_bias,
        norm_gain,
        norm_bias,
        up_weight,
        up_bias,
        down_weight,
        down_bias,
        final_gain,
        final_bias,
    )
    sp_count = lax.axis_size("sp")
    micro_count = max(2, sp_count // 2)
    rows_local, piece_len, model_width = tokens.shape
    rows_micro = rows_local // micro_count
    seq_len = piece_len * sp_count
    width_local = model_width // sp_count
    heads_local = HEADS // sp_count
    query_block = min(512, seq_len)
    scale = 1.0 / math.sqrt(HEAD_DIM)
    tok_count = rows_micro * piece_len
    owned = tuple((jnp.zeros(piece.shape, jnp.float32) for piece in shards))
    output_parts = []
    input_parts = []
    for micro in range(micro_count):
        first_row = micro * rows_micro
        block_tokens = tokens[first_row : first_row + rows_micro]
        block_cotangent = cotangent[first_row : first_row + rows_micro]
        block_segments = segment_ids[first_row : first_row + rows_micro]
        block_stamps = timestep[first_row : first_row + rows_micro]
        gathered = (
            lax.all_gather(shards[0], ("dp", "sp"), axis=0, tiled=True),
            lax.all_gather(shards[1], ("dp", "sp"), axis=0, tiled=True),
            lax.all_gather(shards[2], ("dp", "sp"), axis=0, tiled=True),
            lax.all_gather(shards[3], ("dp", "sp"), axis=0, tiled=True),
            lax.all_gather(shards[4], ("dp", "sp"), axis=0, tiled=True),
            lax.all_gather(shards[5], ("dp", "sp"), axis=0, tiled=True),
            lax.all_gather(shards[6], ("dp", "sp"), axis=0, tiled=True),
            lax.all_gather(shards[7], ("dp", "sp"), axis=0, tiled=True),
            lax.all_gather(shards[8], ("dp", "sp"), axis=0, tiled=True),
            lax.all_gather(shards[9], ("dp", "sp"), axis=0, tiled=True),
            lax.all_gather(shards[10], ("dp", "sp"), axis=0, tiled=True),
            lax.all_gather(shards[11], ("dp", "sp"), axis=0, tiled=True),
            lax.all_gather(shards[12], ("dp", "sp"), axis=0, tiled=True),
        )
        (
            time_full,
            qkv_full,
            qv_full,
            out_full,
            out_shift,
            first_gain,
            first_shift,
            up_full,
            up_shift,
            down_full,
            down_shift,
            second_gain,
            second_shift,
        ) = gathered
        features = time_features(block_stamps, model_width).astype(jnp.bfloat16)
        embedded = jnp.dot(features, time_full, preferred_element_type=jnp.float32)
        hidden = block_tokens.astype(jnp.float32) + embedded[:, None, :]
        hidden_flat = hidden.reshape(tok_count, model_width)
        hidden_low = hidden_flat.astype(jnp.bfloat16)
        qv_float = qv_full.astype(jnp.float32)
        qkv_shift = jnp.concatenate(
            [qv_float[:model_width], jnp.zeros((model_width,), jnp.float32), qv_float[model_width:]]
        )
        packed = jnp.dot(hidden_low, qkv_full, preferred_element_type=jnp.float32) + qkv_shift
        packed = packed.astype(jnp.bfloat16).reshape(rows_micro, piece_len, 3, model_width)
        seg_copies = jnp.broadcast_to(
            block_segments[:, :, None, None], (rows_micro, piece_len, 1, sp_count)
        )
        packed_heads, seg_heads = (
            lax.all_to_all(packed, "sp", split_axis=3, concat_axis=1, tiled=True),
            lax.all_to_all(seg_copies, "sp", split_axis=3, concat_axis=1, tiled=True),
        )
        seg_full = seg_heads[:, :, 0, 0]
        head_shape = (rows_micro, seq_len, heads_local, HEAD_DIM)
        queries = packed_heads[:, :, 0].reshape(head_shape)
        keys_all = packed_heads[:, :, 1].reshape(head_shape)
        values_all = packed_heads[:, :, 2].reshape(head_shape)
        mixed, log_totals = attention_forward(
            queries, keys_all, values_all, seg_full, query_block, scale
        )
        mixed_low = mixed.astype(jnp.bfloat16).reshape(rows_micro, seq_len, width_local)
        mixed_local = lax.all_to_all(mixed_low, "sp", split_axis=1, concat_axis=2, tiled=True)
        mixed_flat = mixed_local.reshape(tok_count, model_width)
        attended = jnp.dot(
            mixed_flat, out_full, preferred_element_type=jnp.float32
        ) + out_shift.astype(jnp.float32)
        first_gain_f = first_gain.astype(jnp.float32)
        normed, normal_one, inverse_one = layer_norm_parts(
            hidden_flat + attended, first_gain_f, first_shift.astype(jnp.float32)
        )
        normed_low = normed.astype(jnp.bfloat16)
        upward = jnp.dot(normed_low, up_full, preferred_element_type=jnp.float32) + up_shift.astype(
            jnp.float32
        )
        activated = jax.nn.gelu(upward, approximate=False).astype(jnp.bfloat16)
        downward = jnp.dot(
            activated, down_full, preferred_element_type=jnp.float32
        ) + down_shift.astype(jnp.float32)
        second_gain_f = second_gain.astype(jnp.float32)
        result, normal_two, inverse_two = layer_norm_parts(
            normed + downward, second_gain_f, second_shift.astype(jnp.float32)
        )
        output_parts.append(result.astype(jnp.bfloat16).reshape(rows_micro, piece_len, model_width))
        upstream = block_cotangent.reshape(tok_count, model_width).astype(jnp.float32)
        grad_second_gain = jnp.sum(upstream * normal_two, axis=0)
        grad_second_shift = jnp.sum(upstream, axis=0)
        resid_two = layer_norm_back(upstream, normal_two, inverse_two, second_gain_f)
        down_grad = resid_two.astype(jnp.bfloat16)
        grad_down_shift = jnp.sum(down_grad, axis=0, dtype=jnp.float32)
        grad_down_full = contract_rows(activated, down_grad)
        act_grad = times_transposed(down_grad, down_full)
        up_grad = (act_grad * gelu_slope(upward)).astype(jnp.bfloat16)
        grad_up_shift = jnp.sum(up_grad, axis=0, dtype=jnp.float32)
        grad_up_full = contract_rows(normed_low, up_grad)
        normed_grad = resid_two + times_transposed(up_grad, up_full)
        grad_first_gain = jnp.sum(normed_grad * normal_one, axis=0)
        grad_first_shift = jnp.sum(normed_grad, axis=0)
        resid_one = layer_norm_back(normed_grad, normal_one, inverse_one, first_gain_f)
        attended_grad = resid_one.astype(jnp.bfloat16)
        grad_out_shift = jnp.sum(attended_grad, axis=0, dtype=jnp.float32)
        grad_out_full = contract_rows(mixed_flat, attended_grad)
        mixed_grad = times_transposed(attended_grad, out_full).astype(jnp.bfloat16)
        mixed_grad = mixed_grad.reshape(rows_micro, piece_len, model_width)
        grad_heads = lax.all_to_all(
            mixed_grad, "sp", split_axis=2, concat_axis=1, tiled=True
        ).reshape(head_shape)
        query_grad, key_grad, value_grad = attention_backward(
            queries, keys_all, values_all, seg_full, grad_heads, log_totals, query_block, scale
        )
        packed_grad = jnp.stack([query_grad, key_grad, value_grad], axis=2)
        packed_grad = packed_grad.reshape(rows_micro, seq_len, 3, width_local).astype(jnp.bfloat16)
        packed_local = lax.all_to_all(packed_grad, "sp", split_axis=1, concat_axis=3, tiled=True)
        packed_flat = packed_local.reshape(tok_count, 3 * model_width)
        third_sums = jnp.sum(packed_flat, axis=0, dtype=jnp.float32)
        grad_qv_full = jnp.concatenate([third_sums[:model_width], third_sums[2 * model_width :]])
        grad_qkv_full = contract_rows(hidden_low, packed_flat)
        hidden_grad = resid_one + times_transposed(packed_flat, qkv_full)
        input_parts.append(
            hidden_grad.astype(jnp.bfloat16).reshape(rows_micro, piece_len, model_width)
        )
        embed_grad = jnp.sum(hidden_grad.reshape(rows_micro, piece_len, model_width), axis=1)
        grad_time_full = jnp.dot(
            features.astype(jnp.float32).T, embed_grad, precision=lax.Precision.HIGHEST
        )
        grads = (
            grad_time_full,
            grad_qkv_full,
            grad_qv_full,
            grad_out_full,
            grad_out_shift,
            grad_first_gain,
            grad_first_shift,
            grad_up_full,
            grad_up_shift,
            grad_down_full,
            grad_down_shift,
            grad_second_gain,
            grad_second_shift,
        )
        shares = lax.psum_scatter(
            flatten_grads(grads), ("dp", "sp"), scatter_dimension=0, tiled=True
        )
        owned = jax.tree.map(jnp.add, owned, restore_grads(shares, owned))
    output = jnp.concatenate(output_parts, axis=0)
    input_grad = jnp.concatenate(input_parts, axis=0)
    return (
        output,
        input_grad,
        owned[0],
        owned[1],
        owned[2],
        owned[3],
        owned[4],
        owned[5],
        owned[6],
        owned[7],
        owned[8],
        owned[9],
        owned[10],
        owned[11],
        owned[12],
    )


AXES = ("dp", "sp")
BF = jnp.bfloat16
F32 = jnp.float32
NT = (((1,), (1,)), ((), ()))
TN = (((0,), (0,)), ((), ()))
NN = (((1,), (0,)), ((), ()))
VMEM_LIMIT = 58 * 1024 * 1024
CHIP_SLOTS = (
    ((0, 0, 0), (0, 0, 1)),
    ((0, 1, 0), (0, 1, 1)),
    ((1, 0, 0), (1, 1, 0)),
    ((1, 0, 1), (1, 1, 1)),
)


def dot(left, right, dims=NN):
    return lax.dot_general(left, right, dims, preferred_element_type=F32)


def device_perm(target):
    pairs = []
    for y in range(2):
        for x in range(2):
            for c in range(2):
                for z in range(4):
                    ty, tx, tc, tz = target(y, x, c, z)
                    source = ((y * 2 + x) * 2 + c) * 4 + z
                    pairs.append((source, ((ty * 2 + tx) * 2 + tc) * 4 + tz))
    return pairs


PAIR = device_perm(lambda y, x, c, z: (y, x, 1 - c, z))
ALONG_X = device_perm(lambda y, x, c, z: (y, 1 - x, c, z))
ALONG_Y = device_perm(lambda y, x, c, z: (1 - y, x, c, z))
ALONG_Z = [device_perm(lambda y, x, c, z, k=k: (y, x, c, z ^ k)) for k in range(3)]
ROW_OUT = [device_perm(lambda y, x, c, z, k=k: (y, x, z // 2, c * 2 + (z + k) % 2)) for k in range(2)]
ROW_BACK = [[(t, s) for s, t in pairs] for pairs in ROW_OUT]


def send(value, pairs):
    return lax.ppermute(value, AXES, pairs)


def after(value, *earlier):
    return lax.optimization_barrier((value, earlier))[0]


def gather_line(shard):
    first = jnp.stack([shard, send(shard, ALONG_Z[2])])
    return first, send(first, ALONG_Z[1])


def gather_plane(first, second, *earlier):
    first_x, second_y = lax.optimization_barrier((send(first, ALONG_X), send(second, ALONG_Y)))
    first, second = jnp.stack([after(first, earlier), first_x]), jnp.stack([after(second, earlier), second_y])
    return [first, send(first, ALONG_Y), second, send(second, ALONG_X)]


def add_low(a, b):
    return (a.astype(F32) + b.astype(F32)).astype(BF)


def scatter_one(first_keep, first_send, second_keep, second_send):
    return first_keep, send(first_send, ALONG_Y), second_keep, send(second_send, ALONG_X)


def add_one(first_keep, from_y, second_keep, from_x, *earlier):
    first_keep, second_keep = after((first_keep, second_keep), earlier)
    to_x, to_y = add_low(first_keep[1], from_y[1]), add_low(second_keep[1], from_x[1])
    return add_low(first_keep[0], from_y[0]), to_x, add_low(second_keep[0], from_x[0]), to_y


def scatter_two(first, to_x, second, to_y):
    return first, send(to_x, ALONG_X), second, send(to_y, ALONG_Y)


def add_two(first, from_x, second, from_y, *earlier):
    first, second = after((first, second), earlier)
    return add_low(first, from_x), add_low(second, from_y)


def scatter_three(first, second):
    return first, send(second, ALONG_Z[1])


def add_three(first, received, *earlier):
    first = after(first, earlier)
    return add_low(first[0], received[0]), add_low(first[1], received[1])


def scatter_four(near, far, *earlier):
    return after(near, earlier).astype(F32) + send(far, ALONG_Z[2]).astype(F32)


def z_relative(half, j):
    return 2 * j + half


def place(meta, slot, at, j):
    half, y_rel, x_rel = CHIP_SLOTS[slot][at]
    chip = (meta[0] ^ y_rel) * 2 + (meta[1] ^ x_rel)
    return chip, meta[3] ^ z_relative(half, j)


def load_all(copies):
    for copy in copies:
        copy.start()
    for copy in copies:
        copy.wait()


def load_qkv(meta, refs, weight, sem):
    copies = []
    for slot, ref in enumerate(refs):
        for at in range(2):
            for j in range(2):
                chip, z = place(meta, slot, at, j)
                for other in range(2):
                    row = pl.multiple_of((chip * 2 + (meta[2] ^ other)) * 128 + z * 32, 32)
                    for t in range(3):
                        copies.append(
                            pltpu.make_async_copy(
                                ref.at[at, j, pl.ds((other * 3 + t) * 32, 32)],
                                weight.at[t, pl.ds(row, 32), :],
                                sem.at[len(copies)],
                            )
                        )
    return copies


def load_split_rows(meta, refs, base, blocks, weight, sem):
    copies = []
    for slot, ref in enumerate(refs):
        for at in range(2):
            for j in range(2):
                chip, z = place(meta, slot, at, j)
                for other in range(2):
                    row = pl.multiple_of((chip * 2 + (meta[2] ^ other)) * 128 + z * 32, 32)
                    copies.append(
                        pltpu.make_async_copy(
                            ref.at[at, j, pl.ds(base + other * blocks, blocks)],
                            weight.at[:, pl.ds(row, 32), :],
                            sem.at[len(copies)],
                        )
                    )
    return copies


def load_own_rows(meta, refs, base, blocks, rows, weight, sem):
    copies = []
    for slot, ref in enumerate(refs):
        for at in range(2):
            for j in range(2):
                chip, z = place(meta, slot, at, j)
                row = pl.multiple_of((chip * 4 + z) * rows, 32)
                copies.append(
                    pltpu.make_async_copy(
                        ref.at[at, j, pl.ds(base, blocks)],
                        weight.at[:, pl.ds(row, rows), :],
                        sem.at[len(copies)],
                    )
                )
    return copies


def kernel_call(kernel, meta, operands, in_specs, out_specs, out_shape, scratch=(), grid=(4,), flops=0, moved=0, exps=0):
    return pl.pallas_call(
        kernel,
        grid_spec=pltpu.PrefetchScalarGridSpec(
            num_scalar_prefetch=1,
            grid=grid,
            in_specs=in_specs,
            out_specs=out_specs,
            scratch_shapes=list(scratch),
        ),
        out_shape=out_shape,
        compiler_params=pltpu.CompilerParams(vmem_limit_bytes=VMEM_LIMIT),
        cost_estimate=pl.CostEstimate(flops=1000, bytes_accessed=1000, transcendentals=0),
    )(meta, *operands)


HBM = pl.BlockSpec(memory_space=pl.ANY)


def spec(shape, index):
    return pl.BlockSpec(shape, index)


def whole(shape):
    return pl.BlockSpec(shape, lambda i, m: (0,) * len(shape))


def shaped(shape, kind):
    return jax.ShapeDtypeStruct(shape, kind)


def low_block(i):
    return jnp.minimum(i, 1)


def high_block(i):
    return jnp.maximum(i - 2, 0)


def turned(i):
    return lax.rem(i + 2, 4)


def project_qkv(meta, own, other, embedded, shift, pieces):
    def kernel(m, own_ref, other_ref, emb_ref, shift_ref, *rest):
        refs, (hidden_ref, out_ref, weight, sem) = rest[:4], rest[4:]
        i = pl.program_id(0)

        @pl.when(i == 0)
        def _():
            load_all(load_qkv(m, refs, weight, sem))

        tokens = jnp.where(i < 2, own_ref[0].astype(F32), other_ref[0].astype(F32))
        hidden = (tokens + emb_ref[...]).astype(BF)
        hidden_ref[...] = hidden
        for t in range(3):
            out_ref[t] = (dot(hidden, weight[t]) + shift_ref[t : t + 1, :]).astype(BF)

    return kernel_call(
        kernel,
        meta,
        (own, other, embedded, shift, *pieces),
        [
            spec((1, 256, 1024), lambda i, m: (low_block(i), 0, 0)),
            spec((1, 256, 1024), lambda i, m: (high_block(i), 0, 0)),
            whole((1, 1024)),
            whole((3, 512)),
        ]
        + [HBM] * 4,
        [spec((256, 1024), lambda i, m: (i, 0)), spec((3, 256, 512), lambda i, m: (0, i, 0))],
        [shaped((1024, 1024), BF), shaped((3, 1024, 512), BF)],
        [pltpu.VMEM((3, 1024, 512), BF), pltpu.SemaphoreType.DMA((96,))],
        flops=2 * 1024 * 1024 * 1536,
        moved=10 << 20,
    )


def head_lanes(h, kind):
    lane = lax.broadcasted_iota(jnp.int32, (1, 128), 1)
    return jnp.where(lane // HEAD_DIM == h, 1.0, 0.0).astype(kind)


def attend(meta, part, qkv, seg_column, seg_row):
    def kernel(m, q_ref, k_ref, v_ref, column_ref, row_ref, out_ref, lse_ref):
        keys, values = k_ref[0], v_ref[0]
        for block in range(4):
            rows = pl.ds(block * 256, 256)
            queries = q_ref[0, rows, :] * jnp.asarray(0.125, BF)
            allowed = column_ref[rows, :] == row_ref[...]
            mixed = jnp.zeros((256, 128), F32)
            for h in range(2):
                lanes = head_lanes(h, BF)
                scores = jnp.where(allowed, dot(queries * lanes, keys, NT), -1e30)
                largest = jnp.max(scores, axis=1, keepdims=True)
                exponent = jnp.exp(scores - largest)
                total = jnp.sum(exponent, axis=1, keepdims=True)
                mixed += dot(exponent.astype(BF), values * lanes) / total
                lse = jnp.broadcast_to(largest + jnp.log(total), (256, 128))
                lse_ref[0, h : h + 1, rows] = jnp.transpose(lse)[0:1, :]
            out_ref[rows, :] = mixed.astype(BF)

    base = part * 2
    third = lambda t: spec((1, 1024, 128), lambda i, m: (t, 0, base + i))
    return kernel_call(
        kernel,
        meta,
        (qkv, qkv, qkv, seg_column, seg_row),
        [third(0), third(1), third(2), whole((1024, 1)), whole((1, 1024))],
        [spec((1024, 128), lambda i, m: (0, i)), spec((1, 8, 1024), lambda i, m: (i, 0, 0))],
        [shaped((1024, 256), BF), shaped((2, 8, 1024), F32)],
        grid=(2,),
        flops=8 * 4 * 1024 * 1024 * 256,
        moved=5 << 20,
        exps=8 << 20,
    )


def attend_back(meta, part, qkv, out, grad, lse, seg_column, seg_row):
    def kernel(m, q_ref, k_ref, v_ref, out_ref, grad_ref, lse_ref, column_ref, row_ref, d_ref, sum_ref, dq):
        queries, upstream = q_ref[0], grad_ref[...]
        product = out_ref[...].astype(F32) * upstream.astype(F32)
        row = lax.broadcasted_iota(jnp.int32, (8, 128), 0)
        lane = lax.broadcasted_iota(jnp.int32, (8, 128), 1)
        picked = jnp.where(lane // HEAD_DIM == row, 1.0, 0.0).astype(F32)
        center = lax.dot_general(picked, product, NT, precision=lax.Precision.HIGHEST, preferred_element_type=F32)
        dq[...] = jnp.zeros_like(dq)
        value_sum = jnp.zeros((1, 128), F32)
        for block in range(4):
            rows = pl.ds(block * 256, 256)
            keys, values = k_ref[0, rows, :], v_ref[0, rows, :]
            allowed = column_ref[rows, :] == row_ref[...]
            dk = jnp.zeros((256, 128), F32)
            dv = jnp.zeros((256, 128), F32)
            for h in range(2):
                lanes = head_lanes(h, BF)
                keys_h = keys * lanes
                scores = dot(keys_h * jnp.asarray(0.125, BF), queries, NT)
                prob = jnp.where(allowed, jnp.exp(scores - lse_ref[0, h : h + 1, :]), 0.0)
                dp = dot(values * lanes, upstream, NT)
                ds = (prob * (dp - center[h : h + 1, :])).astype(BF)
                dv += dot(prob.astype(BF), upstream * lanes)
                dk += dot(ds, queries * lanes)
                dq[...] += dot(ds, keys_h, TN)
            dv = dv.astype(BF)
            d_ref[1, rows, :] = (dk * 0.125).astype(BF)
            d_ref[2, rows, :] = dv
            value_sum += jnp.sum(dv.astype(F32), axis=0, keepdims=True)
        final = (dq[...] * 0.125).astype(BF)
        d_ref[0] = final
        sum_ref[0:1, :] = jnp.sum(final.astype(F32), axis=0, keepdims=True)
        sum_ref[1:2, :] = value_sum

    base = part * 2
    third = lambda t: spec((1, 1024, 128), lambda i, m: (t, 0, base + i))
    heads = lambda first: spec((1024, 128), lambda i, m: (0, first + i))
    return kernel_call(
        kernel,
        meta,
        (qkv, qkv, qkv, out, grad, lse, seg_column, seg_row),
        [third(0), third(1), third(2), heads(0), heads(base), spec((1, 8, 1024), lambda i, m: (i, 0, 0)), whole((1024, 1)), whole((1, 1024))],
        [spec((3, 1024, 128), lambda i, m: (0, 0, i)), spec((8, 128), lambda i, m: (0, i))],
        [shaped((3, 1024, 256), BF), shaped((8, 256), F32)],
        [pltpu.VMEM((1024, 128), F32)],
        grid=(2,),
        flops=8 * 10 * 1024 * 1024 * 256,
        moved=8 << 20,
        exps=8 << 20,
    )


def project_out(meta, mixed, pieces):
    def kernel(m, x_ref, w_ref, *rest):
        refs, (send_ref, own_ref, weight, sem) = rest[:4], rest[4:]
        i = pl.program_id(0)

        @pl.when(i == 0)
        def _():
            load_all(load_own_rows(m, refs, 0, 2, 32, weight, sem))

        for b in range(2):
            columns = pl.ds(b * 512, 512)
            result = dot(x_ref[...], weight[b, :256, :]) + dot(w_ref[...], weight[b, 256:, :])

            @pl.when(i < 2)
            def _():
                send_ref[:, columns] = result.astype(BF)

            @pl.when(i >= 2)
            def _():
                own_ref[:, columns] = result

    return kernel_call(
        kernel,
        meta,
        (*mixed, *pieces),
        [spec((256, 256), lambda i, m: (turned(i), 0))] * 2 + [HBM] * 4,
        [spec((256, 1024), lambda i, m: (low_block(i), 0)), spec((256, 1024), lambda i, m: (high_block(i), 0))],
        [shaped((512, 1024), BF), shaped((512, 1024), F32)],
        [pltpu.VMEM((2, 512, 512), BF), pltpu.SemaphoreType.DMA((16,))],
        flops=2 * 1024 * 1024 * 512,
        moved=6 << 20,
    )


def normal_parts(values):
    center = values - jnp.mean(values, axis=-1, keepdims=True)
    inverse = lax.rsqrt(jnp.mean(center * center, axis=-1, keepdims=True) + EPSILON)
    return center * inverse, inverse


def normal_back(upstream, normal_part, inverse, gain):
    scaled = upstream * gain
    return inverse * (
        scaled
        - jnp.mean(scaled, axis=-1, keepdims=True)
        - normal_part * jnp.mean(scaled * normal_part, axis=-1, keepdims=True)
    )


BY_ROWS = lambda i, m: (i, 0)


def first_norm(meta, tokens, embedded, own, received, vectors):
    def kernel(m, tok_ref, emb_ref, own_ref, recv_ref, vec_ref, normal_ref, inverse_ref, low_ref):
        hidden = tok_ref[0].astype(F32) + emb_ref[...]
        attended = own_ref[...] + recv_ref[...].astype(F32) + vec_ref[0:1, :]
        normal_part, inverse = normal_parts(hidden + attended)
        normal_ref[...] = normal_part
        inverse_ref[...] = jnp.broadcast_to(inverse, (256, 128))
        low_ref[...] = (normal_part * vec_ref[1:2, :] + vec_ref[2:3, :]).astype(BF)

    block = spec((256, 1024), BY_ROWS)
    return kernel_call(
        kernel,
        meta,
        (tokens, embedded, own, received, vectors),
        [spec((1, 256, 1024), lambda i, m: (i, 0, 0)), whole((1, 1024)), block, block, whole((8, 1024))],
        [block, spec((256, 128), BY_ROWS), block],
        [shaped((512, 1024), F32), shaped((512, 128), F32), shaped((512, 1024), BF)],
        grid=(2,),
        flops=512 * 1024 * 12,
        moved=8 << 20,
    )


def expand(meta, own, other, shift, pieces):
    def kernel(m, own_ref, other_ref, shift_ref, *rest):
        refs, (act_ref, slope_ref, weight, sem) = rest[:4], rest[4:]
        i = pl.program_id(0)

        @pl.when(i == 0)
        def _():
            load_all(load_split_rows(m, refs, 2, 4, weight, sem))

        x = jnp.where(i < 2, own_ref[...].astype(F32), other_ref[...].astype(F32)).astype(BF)
        for b in range(4):
            columns = pl.ds(b * 512, 512)
            u = dot(x, weight[b]) + shift_ref[:, columns]
            cumulative = 0.5 * (1.0 + lax.erf(u * INVERSE_ROOT_TWO))
            act_ref[:, columns] = (u * cumulative).astype(BF)
            density = jnp.exp(-0.5 * u * u) * INVERSE_ROOT_TWO_PI
            slope_ref[:, columns] = (cumulative + u * density).astype(BF)

    return kernel_call(
        kernel,
        meta,
        (own, other, shift, *pieces),
        [
            spec((256, 1024), lambda i, m: (low_block(i), 0)),
            spec((256, 1024), lambda i, m: (high_block(i), 0)),
            whole((1, 2048)),
        ]
        + [HBM] * 4,
        [spec((256, 2048), BY_ROWS), spec((256, 2048), BY_ROWS)],
        [shaped((1024, 2048), BF), shaped((1024, 2048), BF)],
        [pltpu.VMEM((4, 1024, 512), BF), pltpu.SemaphoreType.DMA((32,))],
        flops=2 * 1024 * 1024 * 2048,
        moved=14 << 20,
        exps=4 << 20,
    )


def contract(meta, activated, pieces):
    def kernel(m, x_ref, *rest):
        refs, (send_ref, own_ref, weight, sem) = rest[:4], rest[4:]
        i = pl.program_id(0)

        @pl.when(i == 0)
        def _():
            load_all(load_own_rows(m, refs, 0, 2, 128, weight, sem))

        for b in range(2):
            columns = pl.ds(b * 512, 512)
            result = dot(x_ref[...], weight[b])

            @pl.when(i < 2)
            def _():
                send_ref[:, columns] = result.astype(BF)

            @pl.when(i >= 2)
            def _():
                own_ref[:, columns] = result

    return kernel_call(
        kernel,
        meta,
        (activated, *pieces),
        [spec((256, 2048), lambda i, m: (turned(i), 0))] + [HBM] * 4,
        [spec((256, 1024), lambda i, m: (low_block(i), 0)), spec((256, 1024), lambda i, m: (high_block(i), 0))],
        [shaped((512, 1024), BF), shaped((512, 1024), F32)],
        [pltpu.VMEM((2, 2048, 512), BF), pltpu.SemaphoreType.DMA((16,))],
        flops=2 * 1024 * 1024 * 2048,
        moved=11 << 20,
    )


def row_sums(sum_ref, i, rows):
    @pl.when(i == 0)
    def _():
        sum_ref[...] = jnp.zeros_like(sum_ref)

    for n, value in enumerate(rows):
        sum_ref[n : n + 1, :] += jnp.sum(value, axis=0, keepdims=True)


def second_norm(meta, normal_one, own, received, cotangent, vectors):
    def kernel(m, normal_ref, own_ref, recv_ref, cot_ref, vec_ref, out_ref, resid_ref, low_ref, sum_ref):
        normed = normal_ref[...] * vec_ref[1:2, :] + vec_ref[2:3, :]
        downward = own_ref[...] + recv_ref[...].astype(F32) + vec_ref[3:4, :]
        normal_part, inverse = normal_parts(normed + downward)
        out_ref[...] = (normal_part * vec_ref[4:5, :] + vec_ref[5:6, :]).astype(BF)
        upstream = cot_ref[...].astype(F32)
        resid = normal_back(upstream, normal_part, inverse, vec_ref[4:5, :])
        resid_ref[...] = resid
        low = resid.astype(BF)
        low_ref[...] = low
        row_sums(sum_ref, pl.program_id(0), (upstream * normal_part, upstream, low.astype(F32)))

    block = spec((256, 1024), BY_ROWS)
    return kernel_call(
        kernel,
        meta,
        (normal_one, own, received, cotangent, vectors),
        [block, block, block, block, whole((8, 1024))],
        [block, block, block, whole((8, 1024))],
        [shaped((512, 1024), BF), shaped((512, 1024), F32), shaped((512, 1024), BF), shaped((8, 1024), F32)],
        grid=(2,),
        flops=512 * 1024 * 30,
        moved=10 << 20,
    )


def feed_back(meta, own, other, slope, down_pieces, up_pieces):
    def kernel(m, own_ref, other_ref, slope_ref, *rest):
        down_refs, up_refs = rest[:4], rest[4:8]
        du_ref, send_ref, mine_ref, sum_ref, down, up, down_sem, up_sem = rest[8:]
        i = pl.program_id(0)

        @pl.when(i == 0)
        def _():
            load_all(
                load_own_rows(m, down_refs, 0, 2, 128, down, down_sem)
                + load_split_rows(m, up_refs, 2, 4, up, up_sem)
            )
            sum_ref[...] = jnp.zeros_like(sum_ref)

        df = jnp.where(i < 2, other_ref[...].astype(F32), own_ref[...].astype(F32)).astype(BF)
        total = jnp.zeros((256, 1024), F32)
        for b in range(4):
            rows = pl.ds(b * 512, 512)
            act = dot(df[:, :512], down[0, rows, :], NT) + dot(df[:, 512:], down[1, rows, :], NT)
            du = (act * slope_ref[:, rows].astype(F32)).astype(BF)
            du_ref[:, rows] = du
            sum_ref[0:1, rows] += jnp.sum(du.astype(F32), axis=0, keepdims=True)
            total += dot(du, up[b], NT)

        @pl.when(i < 2)
        def _():
            send_ref[...] = total.astype(BF)

        @pl.when(i >= 2)
        def _():
            mine_ref[...] = total

    return kernel_call(
        kernel,
        meta,
        (own, other, slope, *down_pieces, *up_pieces),
        [
            spec((256, 1024), lambda i, m: (high_block(i), 0)),
            spec((256, 1024), lambda i, m: (low_block(i), 0)),
            spec((256, 2048), lambda i, m: (turned(i), 0)),
        ]
        + [HBM] * 8,
        [
            spec((256, 2048), lambda i, m: (turned(i), 0)),
            spec((256, 1024), lambda i, m: (low_block(i), 0)),
            spec((256, 1024), lambda i, m: (high_block(i), 0)),
            whole((8, 2048)),
        ],
        [shaped((1024, 2048), BF), shaped((512, 1024), BF), shaped((512, 1024), F32), shaped((8, 2048), F32)],
        [
            pltpu.VMEM((2, 2048, 512), BF),
            pltpu.VMEM((4, 1024, 512), BF),
            pltpu.SemaphoreType.DMA((16,)),
            pltpu.SemaphoreType.DMA((32,)),
        ],
        flops=4 * 1024 * 1024 * 2048,
        moved=22 << 20,
    )


def first_norm_back(meta, resid, own, received, normal_one, inverse_one, vectors):
    def kernel(m, resid_ref, own_ref, recv_ref, normal_ref, inverse_ref, vec_ref, out_ref, low_ref, sum_ref):
        upstream = resid_ref[...] + own_ref[...] + recv_ref[...].astype(F32)
        normal_part = normal_ref[...]
        resid_one = normal_back(upstream, normal_part, inverse_ref[:, 0:1], vec_ref[1:2, :])
        out_ref[...] = resid_one
        low = resid_one.astype(BF)
        low_ref[...] = low
        row_sums(sum_ref, pl.program_id(0), (upstream * normal_part, upstream, low.astype(F32)))

    block = spec((256, 1024), BY_ROWS)
    return kernel_call(
        kernel,
        meta,
        (resid, own, received, normal_one, inverse_one, vectors),
        [block, block, block, block, spec((256, 128), BY_ROWS), whole((8, 1024))],
        [block, block, whole((8, 1024))],
        [shaped((512, 1024), F32), shaped((512, 1024), BF), shaped((8, 1024), F32)],
        grid=(2,),
        flops=512 * 1024 * 20,
        moved=10 << 20,
    )


def output_back(meta, own, other, pieces):
    def kernel(m, own_ref, other_ref, *rest):
        refs, (out_ref, weight, sem) = rest[:4], rest[4:]
        i = pl.program_id(0)

        @pl.when(i == 0)
        def _():
            load_all(load_own_rows(m, refs, 0, 2, 32, weight, sem))

        da = jnp.where(i < 2, own_ref[...].astype(F32), other_ref[...].astype(F32)).astype(BF)
        out_ref[...] = (dot(da[:, :512], weight[0], NT) + dot(da[:, 512:], weight[1], NT)).astype(BF)

    return kernel_call(
        kernel,
        meta,
        (own, other, *pieces),
        [
            spec((256, 1024), lambda i, m: (low_block(i), 0)),
            spec((256, 1024), lambda i, m: (high_block(i), 0)),
        ]
        + [HBM] * 4,
        spec((256, 512), BY_ROWS),
        shaped((1024, 512), BF),
        [pltpu.VMEM((2, 512, 512), BF), pltpu.SemaphoreType.DMA((16,))],
        flops=2 * 1024 * 1024 * 512,
        moved=4 << 20,
    )


def rel_chip(s, m):
    return (m[0] ^ (s // 2)) * 2 + (m[1] ^ lax.rem(s, 2))


def piece_outputs(blocks, rows, columns=512):
    shape = (2, 2, blocks, rows, columns)
    return [HBM] * 4, [shaped(shape, BF)] * 4


def push(s, outs, copy_for):
    first_keep, first_send, second_keep, second_send = outs
    slots = (
        ((first_keep, 0), (second_keep, 0)),
        ((first_keep, 1), (second_send, 0)),
        ((first_send, 0), (second_keep, 1)),
        ((first_send, 1), (second_send, 1)),
    )
    for n, (first, second) in enumerate(slots):

        @pl.when(s == n)
        def _(n=n, first=first, second=second):
            for k in range(4):
                ref, at = (first, second)[k // 2]
                for copy in copy_for(n, k, ref.at[at, k % 2]):
                    copy.start()

    @pl.when(s == 3)
    def _():
        for n, (first, second) in enumerate(slots):
            for k in range(4):
                ref, at = (first, second)[k // 2]
                for copy in copy_for(n, k, ref.at[at, k % 2]):
                    copy.wait()


def weigh_down(meta, activated, own, other):
    def kernel(m, x_ref, own_ref, other_ref, *rest):
        outs, (stage, sem) = rest[:4], rest[4:]
        s = pl.program_id(0)
        x = x_ref[...]
        for b in range(2):
            columns = pl.ds(b * 512, 512)
            stage[s, b] = (dot(x[:512], own_ref[:, columns], TN) + dot(x[512:], other_ref[:, columns], TN)).astype(BF)

        def copy_for(n, k, target):
            row = pl.multiple_of((m[3] ^ z_relative(k // 2, k % 2)) * 128, 128)
            return [pltpu.make_async_copy(stage.at[n, :, pl.ds(row, 128), :], target, sem.at[n * 4 + k])]

        push(s, outs, copy_for)

    out_specs, out_shape = piece_outputs(2, 128)
    return kernel_call(
        kernel,
        meta,
        (activated, own, other),
        [spec((1024, 512), lambda s, m: (0, rel_chip(s, m))), whole((512, 1024)), whole((512, 1024))],
        out_specs,
        out_shape,
        [pltpu.VMEM((4, 2, 512, 512), BF), pltpu.SemaphoreType.DMA((16,))],
        flops=2 * 1024 * 1024 * 2048,
        moved=10 << 20,
    )


def weigh_up(meta, normed_own, normed_other, du):
    def kernel(m, own_ref, other_ref, du_ref, *rest):
        outs, (up, sem) = rest[:4], rest[4:]
        s = pl.program_id(0)
        for b in range(4):
            columns = pl.ds(b * 512, 512)
            up[s, b] = (dot(own_ref[...], du_ref[:512, columns], TN) + dot(other_ref[...], du_ref[512:, columns], TN)).astype(BF)

        def copy_for(n, k, target):
            z = m[3] ^ z_relative(k // 2, k % 2)
            copies = []
            for rel in range(2):
                row = pl.multiple_of((m[2] ^ rel) * 128 + z * 32, 32)
                copies.append(
                    pltpu.make_async_copy(
                        up.at[n, :, pl.ds(row, 32), :],
                        target.at[pl.ds(rel * 4, 4)],
                        sem.at[(n * 4 + k) * 2 + rel],
                    )
                )
            return copies

        push(s, outs, copy_for)

    out_specs, out_shape = piece_outputs(8, 32)
    return kernel_call(
        kernel,
        meta,
        (normed_own, normed_other, du),
        [
            spec((512, 256), lambda s, m: (0, rel_chip(s, m))),
            spec((512, 256), lambda s, m: (0, rel_chip(s, m))),
            whole((1024, 2048)),
        ],
        out_specs,
        out_shape,
        [pltpu.VMEM((4, 4, 256, 512), BF), pltpu.SemaphoreType.DMA((32,))],
        flops=2 * 1024 * 1024 * 2048,
        moved=15 << 20,
    )


def weigh_qkv(meta, hidden, dqkv, out_terms=()):
    def kernel(m, x_ref, d_ref, *rest):
        s = pl.program_id(0)
        if out_terms:
            mixed_ref, more_ref, own_ref, other_ref = rest[:4]
            rest = rest[4:]
        outs, stage, sem = rest[:4], rest[4], rest[5]
        for t in range(3):
            stage[s, t] = dot(x_ref[...], d_ref[t], TN).astype(BF)
        if out_terms:
            stage_out, sem_out = rest[6:]
            x = jnp.where(rel_chip(s, m) < 2, mixed_ref[...].astype(F32), more_ref[...].astype(F32)).astype(BF)
            for b in range(4):
                columns = pl.ds(b * 256, 256)
                stage_out[s, b] = (
                    dot(x[:512], own_ref[:, columns], TN) + dot(x[512:], other_ref[:, columns], TN)
                ).astype(BF)

        def copy_for(n, k, target):
            z = m[3] ^ z_relative(k // 2, k % 2)
            copies = []
            for rel in range(2):
                row = pl.multiple_of((m[2] ^ rel) * 128 + z * 32, 32)
                copies.append(
                    pltpu.make_async_copy(
                        stage.at[n, :, pl.ds(row, 32), :],
                        target.at[pl.ds(rel * 3, 3)],
                        sem.at[(n * 4 + k) * 2 + rel],
                    )
                )
            if out_terms:
                copies.append(
                    pltpu.make_async_copy(
                        stage_out.at[n, :, pl.ds(pl.multiple_of(z * 32, 32), 32), :],
                        target.at[pl.ds(6, 4)],
                        sem_out.at[n * 4 + k],
                    )
                )
            return copies

        push(s, outs, copy_for)

    out_specs, out_shape = piece_outputs(10 if out_terms else 6, 32, 256)
    in_specs = [spec((1024, 256), lambda s, m: (0, rel_chip(s, m))), whole((3, 1024, 256))]
    scratch = [pltpu.VMEM((4, 3, 256, 256), BF), pltpu.SemaphoreType.DMA((32,))]
    if out_terms:
        in_specs += [spec((1024, 128), lambda s, m: (0, rel_chip(s, m) % 2))] * 2 + [whole((512, 1024))] * 2
        scratch += [pltpu.VMEM((4, 4, 128, 256), BF), pltpu.SemaphoreType.DMA((16,))]
    return kernel_call(
        kernel,
        meta,
        (hidden, dqkv, *out_terms),
        in_specs,
        out_specs,
        out_shape,
        scratch,
        flops=2 * 1024 * 1024 * 1024,
        moved=8 << 20,
    )


def qkv_back(meta, dqkv, pieces):
    def kernel(m, d_ref, e_ref, *rest):
        refs, (send_ref, own_ref, weight, sem) = rest[:4], rest[4:]
        i = pl.program_id(0)

        @pl.when(i == 0)
        def _():
            load_all(load_qkv(m, refs, weight, sem))

        total = jnp.zeros((256, 1024), F32)
        for t in range(3):
            total += dot(d_ref[t], weight[t, :, :256], NT) + dot(e_ref[t], weight[t, :, 256:], NT)

        @pl.when(i < 2)
        def _():
            send_ref[...] = total.astype(BF)

        @pl.when(i >= 2)
        def _():
            own_ref[...] = total

    return kernel_call(
        kernel,
        meta,
        (*dqkv, *pieces),
        [spec((3, 256, 256), lambda i, m: (0, turned(i), 0))] * 2 + [HBM] * 4,
        [spec((256, 1024), lambda i, m: (low_block(i), 0)), spec((256, 1024), lambda i, m: (high_block(i), 0))],
        [shaped((512, 1024), BF), shaped((512, 1024), F32)],
        [pltpu.VMEM((3, 1024, 512), BF), pltpu.SemaphoreType.DMA((96,))],
        flops=2 * 1024 * 1024 * 1536,
        moved=9 << 20,
    )


def last_sum(meta, resid, own, received):
    def kernel(m, resid_ref, own_ref, recv_ref, out_ref, sum_ref):
        total = resid_ref[...] + own_ref[...] + recv_ref[...].astype(F32)
        out_ref[...] = total.astype(BF)
        row_sums(sum_ref, pl.program_id(0), (total,))

    block = spec((256, 1024), BY_ROWS)
    return kernel_call(
        kernel,
        meta,
        (resid, own, received),
        [block, block, block],
        [block, whole((8, 1024))],
        [shaped((512, 1024), BF), shaped((8, 1024), F32)],
        grid=(2,),
        flops=512 * 1024 * 4,
        moved=6 << 20,
    )


VECTOR_SIZES = (64, 32, 32, 32, 128, 32, 32, 32)


def split_vectors(packed):
    parts, start = [], 0
    for size in VECTOR_SIZES:
        parts.append(packed[:, start : start + size])
        start += size
    return parts


def chip_body(
    tokens,
    timestep,
    segment_ids,
    cotangent,
    time_weight,
    qkv_weight,
    qv_bias,
    out_weight,
    out_bias,
    norm_gain,
    norm_bias,
    up_weight,
    up_bias,
    down_weight,
    down_bias,
    final_gain,
    final_bias,
):
    dp, z = lax.axis_index("dp"), lax.axis_index("sp")
    y, x, c = dp // 4, (dp // 2) % 2, dp % 2
    meta = jnp.stack([y, x, c, z]).astype(jnp.int32)
    pick = lambda value, index, axis: lax.dynamic_index_in_dim(value, index, axis, keepdims=False)

    me = dp * 4 + z

    qkv_split = qkv_weight.reshape(32, 3, 4, 2, 128)
    up_split = up_weight.reshape(32, 4, 2, 512)
    qkv_half = lambda core: pick(qkv_split, core, 3).reshape(32, 3, 512).transpose(1, 0, 2).reshape(96, 512)
    up_half = lambda core: pick(up_split, core, 2).transpose(1, 0, 2)
    small = jnp.concatenate([qv_bias, out_bias, norm_gain, norm_bias, up_bias, down_bias, final_gain, final_bias])
    small = jnp.pad(small[None], ((0, 15), (0, 128)))
    received = send(jnp.concatenate([qkv_half(1 - c), small]), PAIR)
    small = jnp.concatenate([small[:1], received[96:97], small[2:]])
    qkv_shard = jnp.concatenate([qkv_half(c), received[:96], small])
    out_shard = out_weight.reshape(32, 2, 512).transpose(1, 0, 2)
    mid_shard = jnp.concatenate([out_shard, up_half(c), send(up_half(1 - c), PAIR)])
    down_shard = down_weight.reshape(128, 2, 512).transpose(1, 0, 2)
    qkv_line = gather_line(qkv_shard)

    stamps = after(timestep.astype(jnp.int32), received)[:, None]
    stamps = jnp.concatenate([stamps // 64, stamps % 64], axis=1).astype(BF)
    for pairs in (PAIR, ALONG_X, ALONG_Y):
        stamps = jnp.concatenate([stamps, send(stamps, pairs)])
    stamps = stamps.astype(F32)
    stamps = (stamps[:, 0] * 64.0 + stamps[:, 1]).reshape(4, 4)
    sums_order = jnp.arange(4, dtype=jnp.int32) ^ z
    from_pair = (sums_order // 2) ^ c
    stamps = jnp.take_along_axis(stamps, jnp.broadcast_to(from_pair * 2 + sums_order % 2, (4, 4)), axis=1).reshape(16, 1)
    column = me * 32 + jnp.arange(32, dtype=jnp.int32)
    frequency = jnp.exp(-math.log(10000.0) * (column % 512).astype(F32) / 512)
    phases = stamps * frequency[None, :]
    features = jnp.where(column[None, :] < 512, jnp.sin(phases), jnp.cos(phases)).astype(BF)
    features = after(features, qkv_line[0])
    embedded = jnp.dot(features, time_weight, preferred_element_type=F32)
    embedded = embedded + send(embedded, PAIR)
    for width, pairs in ((8, ALONG_Y), (4, ALONG_X), (2, ALONG_Z[2]), (1, ALONG_Z[1])):
        embedded = embedded[:width] + send(embedded[width:], pairs)

    mid_line = gather_line(after(mid_shard, qkv_line))
    qkv_pieces = gather_plane(*qkv_line)

    def take_rows(value):
        return jnp.stack([send(pick(value, (z + k) % 2, 0), ROW_OUT[k]) for k in range(2)])

    def give_rows(value):
        parts = [send(value[k * 256 : (k + 1) * 256], ROW_BACK[k]) for k in range(2)]
        swapped = (z % 2) == 1
        return jnp.stack([jnp.where(swapped, parts[1], parts[0]), jnp.where(swapped, parts[0], parts[1])])

    documents = jnp.concatenate([segment_ids // 32, segment_ids % 32], axis=1).astype(BF)
    documents = jnp.pad(documents[:, None, :], ((0, 0), (0, 15), (0, 512)))
    own_tokens = take_rows(after(jnp.concatenate([tokens, documents], axis=1), mid_line))
    other_tokens = send(own_tokens, PAIR)
    codes = jnp.concatenate([own_tokens[:, 256], other_tokens[:, 256]]).astype(F32)
    segments = (codes[:, :256] * 32.0 + codes[:, 256:512]).reshape(1024)
    seg_column, seg_row = segments[:, None], segments[None, :]

    mid_pieces = gather_plane(*mid_line)

    natural = jnp.arange(32, dtype=jnp.int32)
    order = (natural[:, None] ^ me) == natural[None, :]
    small = jnp.stack([piece[:, :, 192:194, :384] for piece in qkv_pieces])
    small = jnp.stack(
        [
            small[half * 2 + (x_rel if half else y_rel), y_rel if half else x_rel, j, rel]
            for y_rel in range(2)
            for x_rel in range(2)
            for rel in range(2)
            for j in range(2)
            for half in range(2)
        ]
    )
    small = jnp.dot(order.astype(BF), small, preferred_element_type=F32)
    full = [part.reshape(1, -1) for part in split_vectors(small)]
    qv_full, out_shift, first_gain, first_shift, up_full, down_shift, second_gain, second_shift = full
    blank = jnp.zeros((2, 1024), F32)
    vectors = jnp.concatenate([out_shift, first_gain, first_shift, down_shift, second_gain, second_shift, blank])
    qv_mine = pick(qv_full.reshape(2, 4, 2, 128), c, 2).reshape(2, 512)
    qkv_shift = jnp.stack([qv_mine[0], jnp.zeros((512,), F32), qv_mine[1]])
    up_shift = pick(up_full.reshape(4, 2, 512), c, 1).reshape(1, 2048)

    hidden, qkv = project_qkv(meta, own_tokens, other_tokens, embedded, qkv_shift, qkv_pieces)
    mixed_one, lse_one = attend(meta, 0, qkv, seg_column, seg_row)
    down_first = jnp.stack([after(down_shard, mixed_one), send(after(down_shard, qkv), ALONG_Z[2])])
    mixed_two, lse_two = attend(meta, 1, after(qkv, down_first), seg_column, seg_row)
    down_second = after(send(down_first, ALONG_Z[1]), mixed_two)
    mixed = mixed_one, after(mixed_two, down_second)
    away, mine = project_out(meta, mixed, mid_pieces)
    own_cotangent = take_rows(after(cotangent, down_second))
    down_pieces = gather_plane(down_first, down_second, mine)
    normal_one, inverse_one, normed = first_norm(meta, own_tokens, embedded, mine, send(away, PAIR), vectors)
    normed_other = send(normed, PAIR)
    activated, slope = expand(meta, normed, after(normed_other, own_cotangent, down_pieces[0], down_pieces[2]), up_shift, mid_pieces)
    away, mine = contract(meta, activated, down_pieces)
    own_cotangent = after(own_cotangent, mine).reshape(512, 1024)
    result, resid_two, df, sums_two = second_norm(meta, normal_one, mine, send(away, PAIR), own_cotangent, vectors)

    df_other = send(df, PAIR)
    down_terms = weigh_down(meta, activated, df, df_other)
    du, away, mine, up_sums = feed_back(meta, after(df, down_terms), df_other, slope, down_pieces, mid_pieces)
    received = send(away, PAIR)
    up_terms = weigh_up(meta, normed, normed_other, du)
    down_sums = add_one(*scatter_one(*down_terms), up_terms)
    resid_one, da, sums_one = first_norm_back(
        meta, after(resid_two, down_sums), mine, received, normal_one, inverse_one, vectors
    )
    da_other = send(da, PAIR)
    dout = output_back(meta, da, da_other, mid_pieces)
    down_sums = add_two(*scatter_two(*down_sums), dout)
    output = give_rows(after(result, dout))
    grad = after(dout, down_sums)
    dqkv_one, qv_sums_one = attend_back(meta, 0, qkv, mixed_one, grad, lse_one, seg_column, seg_row)
    output = after(output, dqkv_one)
    qkv_terms_one = weigh_qkv(meta, hidden, after(dqkv_one, output), (mixed_one, mixed_two, da, da_other))
    up_sums_one = add_one(*scatter_one(*up_terms), qkv_terms_one)
    down_sums = add_three(*scatter_three(*down_sums), qkv_terms_one)
    grad = after(dout, up_sums_one, down_sums)
    dqkv_two, qv_sums_two = attend_back(meta, 1, qkv, mixed_two, grad, lse_two, seg_column, seg_row)
    up_sums_two = add_two(*scatter_two(*up_sums_one), dqkv_two)
    down_share = scatter_four(*down_sums, dqkv_two)
    qkv_terms_two = weigh_qkv(meta, hidden, after(dqkv_two, up_sums_two, down_share))
    qkv_sums_one = add_one(*scatter_one(*qkv_terms_one), qkv_terms_two)
    away, mine = qkv_back(meta, (dqkv_one, after(dqkv_two, qkv_terms_two, qkv_sums_one)), qkv_pieces)
    up_sums_three = add_three(*scatter_three(*up_sums_two), mine)
    qkv_sums_two = add_one(*scatter_one(*qkv_terms_two), mine)
    qkv_sums_one = add_two(*scatter_two(*qkv_sums_one), mine)
    input_low, embed_sums = last_sum(meta, resid_one, mine, send(away, PAIR))
    input_grad = give_rows(input_low)
    qkv_sums_two = add_two(*scatter_two(*qkv_sums_two), input_low)
    qkv_sums_one = add_three(*scatter_three(*qkv_sums_one), input_low)
    up_share = scatter_four(*up_sums_three, input_low)
    qkv_share_one = scatter_four(*qkv_sums_one)
    qkv_share_two = scatter_four(*add_three(*scatter_three(*qkv_sums_two)))
    qkv_share = jnp.concatenate([qkv_share_one[:6], qkv_share_two], axis=2)
    qv_sums = jnp.concatenate([qv_sums_one[0:2], qv_sums_two[0:2]], axis=1)

    def both_halves(own, received):
        return jnp.where(c == 0, jnp.stack([own, received], axis=-2), jnp.stack([received, own], axis=-2))

    grad_down = down_share.transpose(1, 0, 2).reshape(128, 1024)
    grad_out = qkv_share_one[6:].transpose(1, 0, 2).reshape(32, 1024)
    grad_up = both_halves(up_share[:4], send(up_share[4:], PAIR))
    grad_up = grad_up.transpose(1, 0, 2, 3).reshape(32, 4096)
    split = lambda share: share.reshape(3, 32, 4, 128)
    grad_qkv = both_halves(split(qkv_share[:3]), split(send(qkv_share[3:], PAIR)))
    grad_qkv = grad_qkv.transpose(1, 0, 2, 3, 4).reshape(32, 3072)

    core_lane = (jnp.arange(2) == c).astype(F32)
    spread = lambda sums, width: (sums.reshape(-1, 1, width) * core_lane[None, :, None]).reshape(32, -1)
    grads = jnp.concatenate(
        [
            spread(qv_sums, 128),
            sums_one[2].reshape(32, 32),
            sums_one[0].reshape(32, 32),
            sums_one[1].reshape(32, 32),
            spread(up_sums[0:1], 512),
            sums_two[2].reshape(32, 32),
            sums_two[0].reshape(32, 32),
            sums_two[1].reshape(32, 32),
        ],
        axis=1,
    )
    total = jnp.dot(order.astype(F32), after(grads, embed_sums), precision=lax.Precision.HIGHEST)
    total = total.reshape(2, 2, 2, 4, 3, 128).transpose(2, 3, 1, 0, 4, 5).reshape(96, 128)
    sums = embed_sums[0:1].reshape(8, 128)
    received = send(jnp.concatenate([total[48:], sums]), PAIR)
    total, sums = total[:48] + received[:48], sums + received[48:]
    for width, pairs in ((24, ALONG_Z[2]), (12, ALONG_Z[1]), (6, ALONG_X), (3, ALONG_Y)):
        received = send(jnp.concatenate([total[width:], sums]), pairs)
        total, sums = total[:width] + received[:width], jnp.concatenate([sums, received[width:]])
    small_grads = [part.reshape(-1) for part in split_vectors(total.reshape(1, 384))]
    sums = sums.reshape(2, 2, 2, 2, 1024).transpose(0, 1, 3, 2, 4).reshape(16, 1024)
    grad_time = jnp.dot(features.astype(F32).T, sums, precision=lax.Precision.HIGHEST)

    return (
        output,
        input_grad,
        grad_time,
        grad_qkv,
        small_grads[0],
        grad_out,
        *small_grads[1:4],
        grad_up,
        small_grads[4],
        grad_down,
        *small_grads[5:],
    )


def solution(mesh):
    in_specs = (
        P("dp", "sp", None),
        P("dp"),
        P("dp", "sp"),
        P("dp", "sp", None),
        P(("dp", "sp"), None),
        P(("dp", "sp"), None),
        P(("dp", "sp")),
        P(("dp", "sp"), None),
        P(("dp", "sp")),
        P(("dp", "sp")),
        P(("dp", "sp")),
        P(("dp", "sp"), None),
        P(("dp", "sp")),
        P(("dp", "sp"), None),
        P(("dp", "sp")),
        P(("dp", "sp")),
        P(("dp", "sp")),
    )
    out_specs = (
        P("dp", "sp", None),
        P("dp", "sp", None),
        P(("dp", "sp"), None),
        P(("dp", "sp"), None),
        P(("dp", "sp")),
        P(("dp", "sp"), None),
        P(("dp", "sp")),
        P(("dp", "sp")),
        P(("dp", "sp")),
        P(("dp", "sp"), None),
        P(("dp", "sp")),
        P(("dp", "sp"), None),
        P(("dp", "sp")),
        P(("dp", "sp")),
        P(("dp", "sp")),
    )
    plan = chip_body if dict(mesh.shape) == {"dp": 8, "sp": 4} else body
    return jax.shard_map(plan, mesh=mesh, in_specs=in_specs, out_specs=out_specs, check_vma=False)
```

```python
import math

import jax
import jax.numpy as jnp
from jax import lax
from jax.experimental import pallas as pl
from jax.experimental.pallas import tpu as pltpu
from jax.sharding import PartitionSpec as P

HEADS = 16
HEAD_DIM = 64


EPSILON = 1e-05
INVERSE_ROOT_TWO = 1.0 / math.sqrt(2.0)
INVERSE_ROOT_TWO_PI = 1.0 / math.sqrt(2.0 * math.pi)


def time_features(stamps, model_width):
    halfway = model_width // 2
    frequency = jnp.exp(-math.log(10000.0) * jnp.arange(halfway, dtype=jnp.float32) / halfway)
    phases = stamps.astype(jnp.float32)[:, None] * frequency[None, :]
    return jnp.concatenate([jnp.sin(phases), jnp.cos(phases)], axis=1)


def layer_norm_parts(values, gain, offset):
    center = values - jnp.mean(values, axis=-1, keepdims=True)
    variance = jnp.mean(center * center, axis=-1, keepdims=True)
    inverse = lax.rsqrt(variance + EPSILON)
    normal_part = center * inverse
    return (normal_part * gain + offset, normal_part, inverse)


def layer_norm_back(upstream, normal_part, inverse, gain):
    scaled = upstream * gain
    return inverse * (
        scaled
        - jnp.mean(scaled, axis=-1, keepdims=True)
        - normal_part * jnp.mean(scaled * normal_part, axis=-1, keepdims=True)
    )


def gelu_slope(values):
    cumulative = 0.5 * (1.0 + lax.erf(values * INVERSE_ROOT_TWO))
    density = jnp.exp(-0.5 * values * values) * INVERSE_ROOT_TWO_PI
    return cumulative + values * density


def contract_rows(left, right):
    return lax.dot_general(
        left, right, (((0,), (0,)), ((), ())), preferred_element_type=jnp.float32
    )


def times_transposed(left, right):
    return lax.dot_general(
        left, right, (((1,), (1,)), ((), ())), preferred_element_type=jnp.float32
    )


def flatten_grads(grads):
    return tuple((grad.reshape(-1, 128) if grad.ndim == 2 else grad for grad in grads))


def restore_grads(shares, templates):
    return tuple((share.reshape(template.shape) for share, template in zip(shares, templates)))


def attention_forward(queries, keys_all, values_all, seg_full, query_block, scale):
    block_count = queries.shape[1] // query_block

    def one_block(index):
        start = index * query_block
        query_part = lax.dynamic_slice_in_dim(queries, start, query_block, 1)
        seg_part = lax.dynamic_slice_in_dim(seg_full, start, query_block, 1)
        scores = (
            jnp.einsum("rqhd,rkhd->rhqk", query_part, keys_all, preferred_element_type=jnp.float32)
            * scale
        )
        allowed = seg_part[:, None, :, None] == seg_full[:, None, None, :]
        scores = jnp.where(allowed, scores, -1e30)
        largest = jnp.max(scores, axis=-1, keepdims=True)
        exponent = jnp.exp(scores - largest)
        totals = jnp.sum(exponent, axis=-1, keepdims=True)
        probability = exponent / totals
        log_total = largest[..., 0] + jnp.log(totals[..., 0])
        mixed = jnp.einsum(
            "rhqk,rkhd->rqhd",
            probability.astype(jnp.bfloat16),
            values_all,
            preferred_element_type=jnp.float32,
        )
        return (mixed, log_total)

    mixed_blocks, log_totals = lax.map(one_block, jnp.arange(block_count, dtype=jnp.int32))
    mixed = jnp.moveaxis(mixed_blocks, 0, 1).reshape(queries.shape)
    return (mixed, log_totals)


def attention_backward(
    queries, keys_all, values_all, seg_full, grad_heads, log_totals, query_block, scale
):
    block_count = queries.shape[1] // query_block

    def one_block(carry, index):
        key_grad, value_grad = carry
        start = index * query_block
        query_part = lax.dynamic_slice_in_dim(queries, start, query_block, 1)
        seg_part = lax.dynamic_slice_in_dim(seg_full, start, query_block, 1)
        grad_part = lax.dynamic_slice_in_dim(grad_heads, start, query_block, 1)
        scores = (
            jnp.einsum("rqhd,rkhd->rhqk", query_part, keys_all, preferred_element_type=jnp.float32)
            * scale
        )
        allowed = seg_part[:, None, :, None] == seg_full[:, None, None, :]
        scores = jnp.where(allowed, scores, -1e30)
        probability = jnp.exp(scores - log_totals[index][..., None])
        dotted = jnp.einsum(
            "rqhd,rkhd->rhqk", grad_part, values_all, preferred_element_type=jnp.float32
        )
        center = jnp.sum(probability * dotted, axis=-1, keepdims=True)
        score_grad = (probability * (dotted - center)).astype(jnp.bfloat16)
        query_grad = (
            jnp.einsum("rhqk,rkhd->rqhd", score_grad, keys_all, preferred_element_type=jnp.float32)
            * scale
        )
        key_grad = (
            key_grad
            + jnp.einsum(
                "rhqk,rqhd->rkhd", score_grad, query_part, preferred_element_type=jnp.float32
            )
            * scale
        )
        value_grad = value_grad + jnp.einsum(
            "rhqk,rqhd->rkhd",
            probability.astype(jnp.bfloat16),
            grad_part,
            preferred_element_type=jnp.float32,
        )
        return ((key_grad, value_grad), query_grad)

    starting = (jnp.zeros(keys_all.shape, jnp.float32), jnp.zeros(values_all.shape, jnp.float32))
    (key_grad, value_grad), query_blocks = lax.scan(
        one_block, starting, jnp.arange(block_count, dtype=jnp.int32)
    )
    query_grad = jnp.moveaxis(query_blocks, 0, 1).reshape(queries.shape)
    return (query_grad, key_grad, value_grad)


def body(
    tokens,
    timestep,
    segment_ids,
    cotangent,
    time_weight,
    qkv_weight,
    qv_bias,
    out_weight,
    out_bias,
    norm_gain,
    norm_bias,
    up_weight,
    up_bias,
    down_weight,
    down_bias,
    final_gain,
    final_bias,
):
    shards = (
        time_weight,
        qkv_weight,
        qv_bias,
        out_weight,
        out_bias,
        norm_gain,
        norm_bias,
        up_weight,
        up_bias,
        down_weight,
        down_bias,
        final_gain,
        final_bias,
    )
    sp_count = lax.axis_size("sp")
    micro_count = max(2, sp_count // 2)
    rows_local, piece_len, model_width = tokens.shape
    rows_micro = rows_local // micro_count
    seq_len = piece_len * sp_count
    width_local = model_width // sp_count
    heads_local = HEADS // sp_count
    query_block = min(512, seq_len)
    scale = 1.0 / math.sqrt(HEAD_DIM)
    tok_count = rows_micro * piece_len
    owned = tuple((jnp.zeros(piece.shape, jnp.float32) for piece in shards))
    output_parts = []
    input_parts = []
    for micro in range(micro_count):
        first_row = micro * rows_micro
        block_tokens = tokens[first_row : first_row + rows_micro]
        block_cotangent = cotangent[first_row : first_row + rows_micro]
        block_segments = segment_ids[first_row : first_row + rows_micro]
        block_stamps = timestep[first_row : first_row + rows_micro]
        gathered = (
            lax.all_gather(shards[0], ("dp", "sp"), axis=0, tiled=True),
            lax.all_gather(shards[1], ("dp", "sp"), axis=0, tiled=True),
            lax.all_gather(shards[2], ("dp", "sp"), axis=0, tiled=True),
            lax.all_gather(shards[3], ("dp", "sp"), axis=0, tiled=True),
            lax.all_gather(shards[4], ("dp", "sp"), axis=0, tiled=True),
            lax.all_gather(shards[5], ("dp", "sp"), axis=0, tiled=True),
            lax.all_gather(shards[6], ("dp", "sp"), axis=0, tiled=True),
            lax.all_gather(shards[7], ("dp", "sp"), axis=0, tiled=True),
            lax.all_gather(shards[8], ("dp", "sp"), axis=0, tiled=True),
            lax.all_gather(shards[9], ("dp", "sp"), axis=0, tiled=True),
            lax.all_gather(shards[10], ("dp", "sp"), axis=0, tiled=True),
            lax.all_gather(shards[11], ("dp", "sp"), axis=0, tiled=True),
            lax.all_gather(shards[12], ("dp", "sp"), axis=0, tiled=True),
        )
        (
            time_full,
            qkv_full,
            qv_full,
            out_full,
            out_shift,
            first_gain,
            first_shift,
            up_full,
            up_shift,
            down_full,
            down_shift,
            second_gain,
            second_shift,
        ) = gathered
        features = time_features(block_stamps, model_width).astype(jnp.bfloat16)
        embedded = jnp.dot(features, time_full, preferred_element_type=jnp.float32)
        hidden = block_tokens.astype(jnp.float32) + embedded[:, None, :]
        hidden_flat = hidden.reshape(tok_count, model_width)
        hidden_low = hidden_flat.astype(jnp.bfloat16)
        qv_float = qv_full.astype(jnp.float32)
        qkv_shift = jnp.concatenate(
            [qv_float[:model_width], jnp.zeros((model_width,), jnp.float32), qv_float[model_width:]]
        )
        packed = jnp.dot(hidden_low, qkv_full, preferred_element_type=jnp.float32) + qkv_shift
        packed = packed.astype(jnp.bfloat16).reshape(rows_micro, piece_len, 3, model_width)
        seg_copies = jnp.broadcast_to(
            block_segments[:, :, None, None], (rows_micro, piece_len, 1, sp_count)
        )
        packed_heads, seg_heads = (
            lax.all_to_all(packed, "sp", split_axis=3, concat_axis=1, tiled=True),
            lax.all_to_all(seg_copies, "sp", split_axis=3, concat_axis=1, tiled=True),
        )
        seg_full = seg_heads[:, :, 0, 0]
        head_shape = (rows_micro, seq_len, heads_local, HEAD_DIM)
        queries = packed_heads[:, :, 0].reshape(head_shape)
        keys_all = packed_heads[:, :, 1].reshape(head_shape)
        values_all = packed_heads[:, :, 2].reshape(head_shape)
        mixed, log_totals = attention_forward(
            queries, keys_all, values_all, seg_full, query_block, scale
        )
        mixed_low = mixed.astype(jnp.bfloat16).reshape(rows_micro, seq_len, width_local)
        mixed_local = lax.all_to_all(mixed_low, "sp", split_axis=1, concat_axis=2, tiled=True)
        mixed_flat = mixed_local.reshape(tok_count, model_width)
        attended = jnp.dot(
            mixed_flat, out_full, preferred_element_type=jnp.float32
        ) + out_shift.astype(jnp.float32)
        first_gain_f = first_gain.astype(jnp.float32)
        normed, normal_one, inverse_one = layer_norm_parts(
            hidden_flat + attended, first_gain_f, first_shift.astype(jnp.float32)
        )
        normed_low = normed.astype(jnp.bfloat16)
        upward = jnp.dot(normed_low, up_full, preferred_element_type=jnp.float32) + up_shift.astype(
            jnp.float32
        )
        activated = jax.nn.gelu(upward, approximate=False).astype(jnp.bfloat16)
        downward = jnp.dot(
            activated, down_full, preferred_element_type=jnp.float32
        ) + down_shift.astype(jnp.float32)
        second_gain_f = second_gain.astype(jnp.float32)
        result, normal_two, inverse_two = layer_norm_parts(
            normed + downward, second_gain_f, second_shift.astype(jnp.float32)
        )
        output_parts.append(result.astype(jnp.bfloat16).reshape(rows_micro, piece_len, model_width))
        upstream = block_cotangent.reshape(tok_count, model_width).astype(jnp.float32)
        grad_second_gain = jnp.sum(upstream * normal_two, axis=0)
        grad_second_shift = jnp.sum(upstream, axis=0)
        resid_two = layer_norm_back(upstream, normal_two, inverse_two, second_gain_f)
        down_grad = resid_two.astype(jnp.bfloat16)
        grad_down_shift = jnp.sum(down_grad, axis=0, dtype=jnp.float32)
        grad_down_full = contract_rows(activated, down_grad)
        act_grad = times_transposed(down_grad, down_full)
        up_grad = (act_grad * gelu_slope(upward)).astype(jnp.bfloat16)
        grad_up_shift = jnp.sum(up_grad, axis=0, dtype=jnp.float32)
        grad_up_full = contract_rows(normed_low, up_grad)
        normed_grad = resid_two + times_transposed(up_grad, up_full)
        grad_first_gain = jnp.sum(normed_grad * normal_one, axis=0)
        grad_first_shift = jnp.sum(normed_grad, axis=0)
        resid_one = layer_norm_back(normed_grad, normal_one, inverse_one, first_gain_f)
        attended_grad = resid_one.astype(jnp.bfloat16)
        grad_out_shift = jnp.sum(attended_grad, axis=0, dtype=jnp.float32)
        grad_out_full = contract_rows(mixed_flat, attended_grad)
        mixed_grad = times_transposed(attended_grad, out_full).astype(jnp.bfloat16)
        mixed_grad = mixed_grad.reshape(rows_micro, piece_len, model_width)
        grad_heads = lax.all_to_all(
            mixed_grad, "sp", split_axis=2, concat_axis=1, tiled=True
        ).reshape(head_shape)
        query_grad, key_grad, value_grad = attention_backward(
            queries, keys_all, values_all, seg_full, grad_heads, log_totals, query_block, scale
        )
        packed_grad = jnp.stack([query_grad, key_grad, value_grad], axis=2)
        packed_grad = packed_grad.reshape(rows_micro, seq_len, 3, width_local).astype(jnp.bfloat16)
        packed_local = lax.all_to_all(packed_grad, "sp", split_axis=1, concat_axis=3, tiled=True)
        packed_flat = packed_local.reshape(tok_count, 3 * model_width)
        third_sums = jnp.sum(packed_flat, axis=0, dtype=jnp.float32)
        grad_qv_full = jnp.concatenate([third_sums[:model_width], third_sums[2 * model_width :]])
        grad_qkv_full = contract_rows(hidden_low, packed_flat)
        hidden_grad = resid_one + times_transposed(packed_flat, qkv_full)
        input_parts.append(
            hidden_grad.astype(jnp.bfloat16).reshape(rows_micro, piece_len, model_width)
        )
        embed_grad = jnp.sum(hidden_grad.reshape(rows_micro, piece_len, model_width), axis=1)
        grad_time_full = jnp.dot(
            features.astype(jnp.float32).T, embed_grad, precision=lax.Precision.HIGHEST
        )
        grads = (
            grad_time_full,
            grad_qkv_full,
            grad_qv_full,
            grad_out_full,
            grad_out_shift,
            grad_first_gain,
            grad_first_shift,
            grad_up_full,
            grad_up_shift,
            grad_down_full,
            grad_down_shift,
            grad_second_gain,
            grad_second_shift,
        )
        shares = lax.psum_scatter(
            flatten_grads(grads), ("dp", "sp"), scatter_dimension=0, tiled=True
        )
        owned = jax.tree.map(jnp.add, owned, restore_grads(shares, owned))
    output = jnp.concatenate(output_parts, axis=0)
    input_grad = jnp.concatenate(input_parts, axis=0)
    return (
        output,
        input_grad,
        owned[0],
        owned[1],
        owned[2],
        owned[3],
        owned[4],
        owned[5],
        owned[6],
        owned[7],
        owned[8],
        owned[9],
        owned[10],
        owned[11],
        owned[12],
    )


AXES = ("dp", "sp")
BF = jnp.bfloat16
F32 = jnp.float32
NT = (((1,), (1,)), ((), ()))
TN = (((0,), (0,)), ((), ()))
NN = (((1,), (0,)), ((), ()))
VMEM_LIMIT = 58 * 1024 * 1024
CHIP_SLOTS = (
    ((0, 0, 0), (0, 0, 1)),
    ((0, 1, 0), (0, 1, 1)),
    ((1, 0, 0), (1, 1, 0)),
    ((1, 0, 1), (1, 1, 1)),
)


def dot(left, right, dims=NN):
    return lax.dot_general(left, right, dims, preferred_element_type=F32)


def device_perm(target):
    pairs = []
    for y in range(2):
        for x in range(2):
            for c in range(2):
                for z in range(4):
                    ty, tx, tc, tz = target(y, x, c, z)
                    source = ((y * 2 + x) * 2 + c) * 4 + z
                    pairs.append((source, ((ty * 2 + tx) * 2 + tc) * 4 + tz))
    return pairs


PAIR = device_perm(lambda y, x, c, z: (y, x, 1 - c, z))
ALONG_X = device_perm(lambda y, x, c, z: (y, 1 - x, c, z))
ALONG_Y = device_perm(lambda y, x, c, z: (1 - y, x, c, z))
ALONG_Z = [device_perm(lambda y, x, c, z, k=k: (y, x, c, z ^ k)) for k in range(3)]
ROW_OUT = [device_perm(lambda y, x, c, z, k=k: (y, x, z // 2, c * 2 + (z + k) % 2)) for k in range(2)]
ROW_BACK = [[(t, s) for s, t in pairs] for pairs in ROW_OUT]


def send(value, pairs):
    return lax.ppermute(value, AXES, pairs)


def after(value, *earlier):
    return lax.optimization_barrier((value, earlier))[0]


def gather_line(shard):
    first = jnp.stack([shard, send(shard, ALONG_Z[2])])
    return first, send(first, ALONG_Z[1])


def gather_plane(first, second, *earlier):
    first_x, second_y = lax.optimization_barrier((send(first, ALONG_X), send(second, ALONG_Y)))
    first, second = jnp.stack([after(first, earlier), first_x]), jnp.stack([after(second, earlier), second_y])
    return [first, send(first, ALONG_Y), second, send(second, ALONG_X)]


def add_low(a, b):
    return (a.astype(F32) + b.astype(F32)).astype(BF)


def scatter_one(first_keep, first_send, second_keep, second_send):
    return first_keep, send(first_send, ALONG_Y), second_keep, send(second_send, ALONG_X)


def add_one(first_keep, from_y, second_keep, from_x, *earlier):
    first_keep, second_keep = after((first_keep, second_keep), earlier)
    to_x, to_y = add_low(first_keep[1], from_y[1]), add_low(second_keep[1], from_x[1])
    return add_low(first_keep[0], from_y[0]), to_x, add_low(second_keep[0], from_x[0]), to_y


def scatter_two(first, to_x, second, to_y):
    return first, send(to_x, ALONG_X), second, send(to_y, ALONG_Y)


def add_two(first, from_x, second, from_y, *earlier):
    first, second = after((first, second), earlier)
    return add_low(first, from_x), add_low(second, from_y)


def scatter_three(first, second):
    return first, send(second, ALONG_Z[1])


def add_three(first, received, *earlier):
    first = after(first, earlier)
    return add_low(first[0], received[0]), add_low(first[1], received[1])


def scatter_four(near, far, *earlier):
    return after(near, earlier).astype(F32) + send(far, ALONG_Z[2]).astype(F32)


def z_relative(half, j):
    return 2 * j + half


def place(meta, slot, at, j):
    half, y_rel, x_rel = CHIP_SLOTS[slot][at]
    chip = (meta[0] ^ y_rel) * 2 + (meta[1] ^ x_rel)
    return chip, meta[3] ^ z_relative(half, j)


def load_all(copies):
    for copy in copies:
        copy.start()
    for copy in copies:
        copy.wait()


def load_qkv(meta, refs, weight, sem):
    copies = []
    for slot, ref in enumerate(refs):
        for at in range(2):
            for j in range(2):
                chip, z = place(meta, slot, at, j)
                for other in range(2):
                    row = pl.multiple_of((chip * 2 + (meta[2] ^ other)) * 128 + z * 32, 32)
                    for t in range(3):
                        copies.append(
                            pltpu.make_async_copy(
                                ref.at[at, j, pl.ds((other * 3 + t) * 32, 32)],
                                weight.at[t, pl.ds(row, 32), :],
                                sem.at[len(copies)],
                            )
                        )
    return copies


def load_split_rows(meta, refs, base, blocks, weight, sem):
    copies = []
    for slot, ref in enumerate(refs):
        for at in range(2):
            for j in range(2):
                chip, z = place(meta, slot, at, j)
                for other in range(2):
                    row = pl.multiple_of((chip * 2 + (meta[2] ^ other)) * 128 + z * 32, 32)
                    copies.append(
                        pltpu.make_async_copy(
                            ref.at[at, j, pl.ds(base + other * blocks, blocks)],
                            weight.at[:, pl.ds(row, 32), :],
                            sem.at[len(copies)],
                        )
                    )
    return copies


def load_own_rows(meta, refs, base, blocks, rows, weight, sem):
    copies = []
    for slot, ref in enumerate(refs):
        for at in range(2):
            for j in range(2):
                chip, z = place(meta, slot, at, j)
                row = pl.multiple_of((chip * 4 + z) * rows, 32)
                copies.append(
                    pltpu.make_async_copy(
                        ref.at[at, j, pl.ds(base, blocks)],
                        weight.at[:, pl.ds(row, rows), :],
                        sem.at[len(copies)],
                    )
                )
    return copies


def kernel_call(kernel, meta, operands, in_specs, out_specs, out_shape, scratch=(), grid=(4,), flops=0, moved=0, exps=0):
    return pl.pallas_call(
        kernel,
        grid_spec=pltpu.PrefetchScalarGridSpec(
            num_scalar_prefetch=1,
            grid=grid,
            in_specs=in_specs,
            out_specs=out_specs,
            scratch_shapes=list(scratch),
        ),
        out_shape=out_shape,
        compiler_params=pltpu.CompilerParams(vmem_limit_bytes=VMEM_LIMIT),
        cost_estimate=pl.CostEstimate(
            flops=int(flops * 1.5), bytes_accessed=int(moved * 1.5), transcendentals=int(exps * 1.5)
        ),
    )(meta, *operands)


HBM = pl.BlockSpec(memory_space=pl.ANY)


def spec(shape, index):
    return pl.BlockSpec(shape, index)


def whole(shape):
    return pl.BlockSpec(shape, lambda i, m: (0,) * len(shape))


def shaped(shape, kind):
    return jax.ShapeDtypeStruct(shape, kind)


def low_block(i):
    return jnp.minimum(i, 1)


def high_block(i):
    return jnp.maximum(i - 2, 0)


def turned(i):
    return lax.rem(i + 2, 4)


def project_qkv(meta, own, other, embedded, shift, pieces):
    def kernel(m, own_ref, other_ref, emb_ref, shift_ref, *rest):
        refs, (hidden_ref, out_ref, weight, sem) = rest[:4], rest[4:]
        i = pl.program_id(0)

        @pl.when(i == 0)
        def _():
            load_all(load_qkv(m, refs, weight, sem))

        tokens = jnp.where(i < 2, own_ref[0].astype(F32), other_ref[0].astype(F32))
        hidden = (tokens + emb_ref[...]).astype(BF)
        hidden_ref[...] = hidden
        for t in range(3):
            out_ref[t] = (dot(hidden, weight[t]) + shift_ref[t : t + 1, :]).astype(BF)

    return kernel_call(
        kernel,
        meta,
        (own, other, embedded, shift, *pieces),
        [
            spec((1, 256, 1024), lambda i, m: (low_block(i), 0, 0)),
            spec((1, 256, 1024), lambda i, m: (high_block(i), 0, 0)),
            whole((1, 1024)),
            whole((3, 512)),
        ]
        + [HBM] * 4,
        [spec((256, 1024), lambda i, m: (i, 0)), spec((3, 256, 512), lambda i, m: (0, i, 0))],
        [shaped((1024, 1024), BF), shaped((3, 1024, 512), BF)],
        [pltpu.VMEM((3, 1024, 512), BF), pltpu.SemaphoreType.DMA((96,))],
        flops=2 * 1024 * 1024 * 1536,
        moved=10 << 20,
    )


def head_lanes(h, kind):
    lane = lax.broadcasted_iota(jnp.int32, (1, 128), 1)
    return jnp.where(lane // HEAD_DIM == h, 1.0, 0.0).astype(kind)


def attend(meta, part, qkv, seg_column, seg_row):
    def kernel(m, q_ref, k_ref, v_ref, column_ref, row_ref, out_ref, lse_ref):
        keys, values = k_ref[0], v_ref[0]
        for block in range(4):
            rows = pl.ds(block * 256, 256)
            queries = q_ref[0, rows, :] * jnp.asarray(0.125, BF)
            allowed = column_ref[rows, :] == row_ref[...]
            mixed = jnp.zeros((256, 128), F32)
            for h in range(2):
                lanes = head_lanes(h, BF)
                scores = jnp.where(allowed, dot(queries * lanes, keys, NT), -1e30)
                largest = jnp.max(scores, axis=1, keepdims=True)
                exponent = jnp.exp(scores - largest)
                total = jnp.sum(exponent, axis=1, keepdims=True)
                mixed += dot(exponent.astype(BF), values * lanes) / total
                lse = jnp.broadcast_to(largest + jnp.log(total), (256, 128))
                lse_ref[0, h : h + 1, rows] = jnp.transpose(lse)[0:1, :]
            out_ref[rows, :] = mixed.astype(BF)

    base = part * 2
    third = lambda t: spec((1, 1024, 128), lambda i, m: (t, 0, base + i))
    return kernel_call(
        kernel,
        meta,
        (qkv, qkv, qkv, seg_column, seg_row),
        [third(0), third(1), third(2), whole((1024, 1)), whole((1, 1024))],
        [spec((1024, 128), lambda i, m: (0, i)), spec((1, 8, 1024), lambda i, m: (i, 0, 0))],
        [shaped((1024, 256), BF), shaped((2, 8, 1024), F32)],
        grid=(2,),
        flops=8 * 4 * 1024 * 1024 * 256,
        moved=5 << 20,
        exps=8 << 20,
    )


def attend_back(meta, part, qkv, out, grad, lse, seg_column, seg_row):
    def kernel(m, q_ref, k_ref, v_ref, out_ref, grad_ref, lse_ref, column_ref, row_ref, d_ref, sum_ref, dq):
        queries, upstream = q_ref[0], grad_ref[...]
        product = out_ref[...].astype(F32) * upstream.astype(F32)
        row = lax.broadcasted_iota(jnp.int32, (8, 128), 0)
        lane = lax.broadcasted_iota(jnp.int32, (8, 128), 1)
        picked = jnp.where(lane // HEAD_DIM == row, 1.0, 0.0).astype(F32)
        center = lax.dot_general(picked, product, NT, precision=lax.Precision.HIGHEST, preferred_element_type=F32)
        dq[...] = jnp.zeros_like(dq)
        value_sum = jnp.zeros((1, 128), F32)
        for block in range(4):
            rows = pl.ds(block * 256, 256)
            keys, values = k_ref[0, rows, :], v_ref[0, rows, :]
            allowed = column_ref[rows, :] == row_ref[...]
            dk = jnp.zeros((256, 128), F32)
            dv = jnp.zeros((256, 128), F32)
            for h in range(2):
                lanes = head_lanes(h, BF)
                keys_h = keys * lanes
                scores = dot(keys_h * jnp.asarray(0.125, BF), queries, NT)
                prob = jnp.where(allowed, jnp.exp(scores - lse_ref[0, h : h + 1, :]), 0.0)
                dp = dot(values * lanes, upstream, NT)
                ds = (prob * (dp - center[h : h + 1, :])).astype(BF)
                dv += dot(prob.astype(BF), upstream * lanes)
                dk += dot(ds, queries * lanes)
                dq[...] += dot(ds, keys_h, TN)
            dv = dv.astype(BF)
            d_ref[1, rows, :] = (dk * 0.125).astype(BF)
            d_ref[2, rows, :] = dv
            value_sum += jnp.sum(dv.astype(F32), axis=0, keepdims=True)
        final = (dq[...] * 0.125).astype(BF)
        d_ref[0] = final
        sum_ref[0:1, :] = jnp.sum(final.astype(F32), axis=0, keepdims=True)
        sum_ref[1:2, :] = value_sum

    base = part * 2
    third = lambda t: spec((1, 1024, 128), lambda i, m: (t, 0, base + i))
    heads = lambda first: spec((1024, 128), lambda i, m: (0, first + i))
    return kernel_call(
        kernel,
        meta,
        (qkv, qkv, qkv, out, grad, lse, seg_column, seg_row),
        [third(0), third(1), third(2), heads(0), heads(base), spec((1, 8, 1024), lambda i, m: (i, 0, 0)), whole((1024, 1)), whole((1, 1024))],
        [spec((3, 1024, 128), lambda i, m: (0, 0, i)), spec((8, 128), lambda i, m: (0, i))],
        [shaped((3, 1024, 256), BF), shaped((8, 256), F32)],
        [pltpu.VMEM((1024, 128), F32)],
        grid=(2,),
        flops=8 * 10 * 1024 * 1024 * 256,
        moved=8 << 20,
        exps=8 << 20,
    )


def project_out(meta, mixed, pieces):
    def kernel(m, x_ref, w_ref, *rest):
        refs, (send_ref, own_ref, weight, sem) = rest[:4], rest[4:]
        i = pl.program_id(0)

        @pl.when(i == 0)
        def _():
            load_all(load_own_rows(m, refs, 0, 2, 32, weight, sem))

        for b in range(2):
            columns = pl.ds(b * 512, 512)
            result = dot(x_ref[...], weight[b, :256, :]) + dot(w_ref[...], weight[b, 256:, :])

            @pl.when(i < 2)
            def _():
                send_ref[:, columns] = result.astype(BF)

            @pl.when(i >= 2)
            def _():
                own_ref[:, columns] = result

    return kernel_call(
        kernel,
        meta,
        (*mixed, *pieces),
        [spec((256, 256), lambda i, m: (turned(i), 0))] * 2 + [HBM] * 4,
        [spec((256, 1024), lambda i, m: (low_block(i), 0)), spec((256, 1024), lambda i, m: (high_block(i), 0))],
        [shaped((512, 1024), BF), shaped((512, 1024), F32)],
        [pltpu.VMEM((2, 512, 512), BF), pltpu.SemaphoreType.DMA((16,))],
        flops=2 * 1024 * 1024 * 512,
        moved=6 << 20,
    )


def normal_parts(values):
    center = values - jnp.mean(values, axis=-1, keepdims=True)
    inverse = lax.rsqrt(jnp.mean(center * center, axis=-1, keepdims=True) + EPSILON)
    return center * inverse, inverse


def normal_back(upstream, normal_part, inverse, gain):
    scaled = upstream * gain
    return inverse * (
        scaled
        - jnp.mean(scaled, axis=-1, keepdims=True)
        - normal_part * jnp.mean(scaled * normal_part, axis=-1, keepdims=True)
    )


BY_ROWS = lambda i, m: (i, 0)


def first_norm(meta, tokens, embedded, own, received, vectors):
    def kernel(m, tok_ref, emb_ref, own_ref, recv_ref, vec_ref, normal_ref, inverse_ref, low_ref):
        hidden = tok_ref[0].astype(F32) + emb_ref[...]
        attended = own_ref[...] + recv_ref[...].astype(F32) + vec_ref[0:1, :]
        normal_part, inverse = normal_parts(hidden + attended)
        normal_ref[...] = normal_part
        inverse_ref[...] = jnp.broadcast_to(inverse, (256, 128))
        low_ref[...] = (normal_part * vec_ref[1:2, :] + vec_ref[2:3, :]).astype(BF)

    block = spec((256, 1024), BY_ROWS)
    return kernel_call(
        kernel,
        meta,
        (tokens, embedded, own, received, vectors),
        [spec((1, 256, 1024), lambda i, m: (i, 0, 0)), whole((1, 1024)), block, block, whole((8, 1024))],
        [block, spec((256, 128), BY_ROWS), block],
        [shaped((512, 1024), F32), shaped((512, 128), F32), shaped((512, 1024), BF)],
        grid=(2,),
        flops=512 * 1024 * 12,
        moved=8 << 20,
    )


def expand(meta, own, other, shift, pieces):
    def kernel(m, own_ref, other_ref, shift_ref, *rest):
        refs, (act_ref, slope_ref, weight, sem) = rest[:4], rest[4:]
        i = pl.program_id(0)

        @pl.when(i == 0)
        def _():
            load_all(load_split_rows(m, refs, 2, 4, weight, sem))

        x = jnp.where(i < 2, own_ref[...].astype(F32), other_ref[...].astype(F32)).astype(BF)
        for b in range(4):
            columns = pl.ds(b * 512, 512)
            u = dot(x, weight[b]) + shift_ref[:, columns]
            cumulative = 0.5 * (1.0 + lax.erf(u * INVERSE_ROOT_TWO))
            act_ref[:, columns] = (u * cumulative).astype(BF)
            density = jnp.exp(-0.5 * u * u) * INVERSE_ROOT_TWO_PI
            slope_ref[:, columns] = (cumulative + u * density).astype(BF)

    return kernel_call(
        kernel,
        meta,
        (own, other, shift, *pieces),
        [
            spec((256, 1024), lambda i, m: (low_block(i), 0)),
            spec((256, 1024), lambda i, m: (high_block(i), 0)),
            whole((1, 2048)),
        ]
        + [HBM] * 4,
        [spec((256, 2048), BY_ROWS), spec((256, 2048), BY_ROWS)],
        [shaped((1024, 2048), BF), shaped((1024, 2048), BF)],
        [pltpu.VMEM((4, 1024, 512), BF), pltpu.SemaphoreType.DMA((32,))],
        flops=2 * 1024 * 1024 * 2048,
        moved=14 << 20,
        exps=4 << 20,
    )


def contract(meta, activated, pieces):
    def kernel(m, x_ref, *rest):
        refs, (send_ref, own_ref, weight, sem) = rest[:4], rest[4:]
        i = pl.program_id(0)

        @pl.when(i == 0)
        def _():
            load_all(load_own_rows(m, refs, 0, 2, 128, weight, sem))

        for b in range(2):
            columns = pl.ds(b * 512, 512)
            result = dot(x_ref[...], weight[b])

            @pl.when(i < 2)
            def _():
                send_ref[:, columns] = result.astype(BF)

            @pl.when(i >= 2)
            def _():
                own_ref[:, columns] = result

    return kernel_call(
        kernel,
        meta,
        (activated, *pieces),
        [spec((256, 2048), lambda i, m: (turned(i), 0))] + [HBM] * 4,
        [spec((256, 1024), lambda i, m: (low_block(i), 0)), spec((256, 1024), lambda i, m: (high_block(i), 0))],
        [shaped((512, 1024), BF), shaped((512, 1024), F32)],
        [pltpu.VMEM((2, 2048, 512), BF), pltpu.SemaphoreType.DMA((16,))],
        flops=2 * 1024 * 1024 * 2048,
        moved=11 << 20,
    )


def row_sums(sum_ref, i, rows):
    @pl.when(i == 0)
    def _():
        sum_ref[...] = jnp.zeros_like(sum_ref)

    for n, value in enumerate(rows):
        sum_ref[n : n + 1, :] += jnp.sum(value, axis=0, keepdims=True)


def second_norm(meta, normal_one, own, received, cotangent, vectors):
    def kernel(m, normal_ref, own_ref, recv_ref, cot_ref, vec_ref, out_ref, resid_ref, low_ref, sum_ref):
        normed = normal_ref[...] * vec_ref[1:2, :] + vec_ref[2:3, :]
        downward = own_ref[...] + recv_ref[...].astype(F32) + vec_ref[3:4, :]
        normal_part, inverse = normal_parts(normed + downward)
        out_ref[...] = (normal_part * vec_ref[4:5, :] + vec_ref[5:6, :]).astype(BF)
        upstream = cot_ref[...].astype(F32)
        resid = normal_back(upstream, normal_part, inverse, vec_ref[4:5, :])
        resid_ref[...] = resid
        low = resid.astype(BF)
        low_ref[...] = low
        row_sums(sum_ref, pl.program_id(0), (upstream * normal_part, upstream, low.astype(F32)))

    block = spec((256, 1024), BY_ROWS)
    return kernel_call(
        kernel,
        meta,
        (normal_one, own, received, cotangent, vectors),
        [block, block, block, block, whole((8, 1024))],
        [block, block, block, whole((8, 1024))],
        [shaped((512, 1024), BF), shaped((512, 1024), F32), shaped((512, 1024), BF), shaped((8, 1024), F32)],
        grid=(2,),
        flops=512 * 1024 * 30,
        moved=10 << 20,
    )


def feed_back(meta, own, other, slope, down_pieces, up_pieces):
    def kernel(m, own_ref, other_ref, slope_ref, *rest):
        down_refs, up_refs = rest[:4], rest[4:8]
        du_ref, send_ref, mine_ref, sum_ref, down, up, down_sem, up_sem = rest[8:]
        i = pl.program_id(0)

        @pl.when(i == 0)
        def _():
            load_all(
                load_own_rows(m, down_refs, 0, 2, 128, down, down_sem)
                + load_split_rows(m, up_refs, 2, 4, up, up_sem)
            )
            sum_ref[...] = jnp.zeros_like(sum_ref)

        df = jnp.where(i < 2, other_ref[...].astype(F32), own_ref[...].astype(F32)).astype(BF)
        total = jnp.zeros((256, 1024), F32)
        for b in range(4):
            rows = pl.ds(b * 512, 512)
            act = dot(df[:, :512], down[0, rows, :], NT) + dot(df[:, 512:], down[1, rows, :], NT)
            du = (act * slope_ref[:, rows].astype(F32)).astype(BF)
            du_ref[:, rows] = du
            sum_ref[0:1, rows] += jnp.sum(du.astype(F32), axis=0, keepdims=True)
            total += dot(du, up[b], NT)

        @pl.when(i < 2)
        def _():
            send_ref[...] = total.astype(BF)

        @pl.when(i >= 2)
        def _():
            mine_ref[...] = total

    return kernel_call(
        kernel,
        meta,
        (own, other, slope, *down_pieces, *up_pieces),
        [
            spec((256, 1024), lambda i, m: (high_block(i), 0)),
            spec((256, 1024), lambda i, m: (low_block(i), 0)),
            spec((256, 2048), lambda i, m: (turned(i), 0)),
        ]
        + [HBM] * 8,
        [
            spec((256, 2048), lambda i, m: (turned(i), 0)),
            spec((256, 1024), lambda i, m: (low_block(i), 0)),
            spec((256, 1024), lambda i, m: (high_block(i), 0)),
            whole((8, 2048)),
        ],
        [shaped((1024, 2048), BF), shaped((512, 1024), BF), shaped((512, 1024), F32), shaped((8, 2048), F32)],
        [
            pltpu.VMEM((2, 2048, 512), BF),
            pltpu.VMEM((4, 1024, 512), BF),
            pltpu.SemaphoreType.DMA((16,)),
            pltpu.SemaphoreType.DMA((32,)),
        ],
        flops=4 * 1024 * 1024 * 2048,
        moved=22 << 20,
    )


def first_norm_back(meta, resid, own, received, normal_one, inverse_one, vectors):
    def kernel(m, resid_ref, own_ref, recv_ref, normal_ref, inverse_ref, vec_ref, out_ref, low_ref, sum_ref):
        upstream = resid_ref[...] + own_ref[...] + recv_ref[...].astype(F32)
        normal_part = normal_ref[...]
        resid_one = normal_back(upstream, normal_part, inverse_ref[:, 0:1], vec_ref[1:2, :])
        out_ref[...] = resid_one
        low = resid_one.astype(BF)
        low_ref[...] = low
        row_sums(sum_ref, pl.program_id(0), (upstream * normal_part, upstream, low.astype(F32)))

    block = spec((256, 1024), BY_ROWS)
    return kernel_call(
        kernel,
        meta,
        (resid, own, received, normal_one, inverse_one, vectors),
        [block, block, block, block, spec((256, 128), BY_ROWS), whole((8, 1024))],
        [block, block, whole((8, 1024))],
        [shaped((512, 1024), F32), shaped((512, 1024), BF), shaped((8, 1024), F32)],
        grid=(2,),
        flops=512 * 1024 * 20,
        moved=10 << 20,
    )


def output_back(meta, own, other, pieces):
    def kernel(m, own_ref, other_ref, *rest):
        refs, (out_ref, weight, sem) = rest[:4], rest[4:]
        i = pl.program_id(0)

        @pl.when(i == 0)
        def _():
            load_all(load_own_rows(m, refs, 0, 2, 32, weight, sem))

        da = jnp.where(i < 2, own_ref[...].astype(F32), other_ref[...].astype(F32)).astype(BF)
        out_ref[...] = (dot(da[:, :512], weight[0], NT) + dot(da[:, 512:], weight[1], NT)).astype(BF)

    return kernel_call(
        kernel,
        meta,
        (own, other, *pieces),
        [
            spec((256, 1024), lambda i, m: (low_block(i), 0)),
            spec((256, 1024), lambda i, m: (high_block(i), 0)),
        ]
        + [HBM] * 4,
        spec((256, 512), BY_ROWS),
        shaped((1024, 512), BF),
        [pltpu.VMEM((2, 512, 512), BF), pltpu.SemaphoreType.DMA((16,))],
        flops=2 * 1024 * 1024 * 512,
        moved=4 << 20,
    )


def rel_chip(s, m):
    return (m[0] ^ (s // 2)) * 2 + (m[1] ^ lax.rem(s, 2))


def piece_outputs(blocks, rows, columns=512):
    shape = (2, 2, blocks, rows, columns)
    return [HBM] * 4, [shaped(shape, BF)] * 4


def push(s, outs, copy_for):
    first_keep, first_send, second_keep, second_send = outs
    slots = (
        ((first_keep, 0), (second_keep, 0)),
        ((first_keep, 1), (second_send, 0)),
        ((first_send, 0), (second_keep, 1)),
        ((first_send, 1), (second_send, 1)),
    )
    for n, (first, second) in enumerate(slots):

        @pl.when(s == n)
        def _(n=n, first=first, second=second):
            for k in range(4):
                ref, at = (first, second)[k // 2]
                for copy in copy_for(n, k, ref.at[at, k % 2]):
                    copy.start()

    @pl.when(s == 3)
    def _():
        for n, (first, second) in enumerate(slots):
            for k in range(4):
                ref, at = (first, second)[k // 2]
                for copy in copy_for(n, k, ref.at[at, k % 2]):
                    copy.wait()


def weigh_down(meta, activated, own, other):
    def kernel(m, x_ref, own_ref, other_ref, *rest):
        outs, (stage, sem) = rest[:4], rest[4:]
        s = pl.program_id(0)
        x = x_ref[...]
        for b in range(2):
            columns = pl.ds(b * 512, 512)
            stage[s, b] = (dot(x[:512], own_ref[:, columns], TN) + dot(x[512:], other_ref[:, columns], TN)).astype(BF)

        def copy_for(n, k, target):
            row = pl.multiple_of((m[3] ^ z_relative(k // 2, k % 2)) * 128, 128)
            return [pltpu.make_async_copy(stage.at[n, :, pl.ds(row, 128), :], target, sem.at[n * 4 + k])]

        push(s, outs, copy_for)

    out_specs, out_shape = piece_outputs(2, 128)
    return kernel_call(
        kernel,
        meta,
        (activated, own, other),
        [spec((1024, 512), lambda s, m: (0, rel_chip(s, m))), whole((512, 1024)), whole((512, 1024))],
        out_specs,
        out_shape,
        [pltpu.VMEM((4, 2, 512, 512), BF), pltpu.SemaphoreType.DMA((16,))],
        flops=2 * 1024 * 1024 * 2048,
        moved=10 << 20,
    )


def weigh_up(meta, normed_own, normed_other, du):
    def kernel(m, own_ref, other_ref, du_ref, *rest):
        outs, (up, sem) = rest[:4], rest[4:]
        s = pl.program_id(0)
        for b in range(4):
            columns = pl.ds(b * 512, 512)
            up[s, b] = (dot(own_ref[...], du_ref[:512, columns], TN) + dot(other_ref[...], du_ref[512:, columns], TN)).astype(BF)

        def copy_for(n, k, target):
            z = m[3] ^ z_relative(k // 2, k % 2)
            copies = []
            for rel in range(2):
                row = pl.multiple_of((m[2] ^ rel) * 128 + z * 32, 32)
                copies.append(
                    pltpu.make_async_copy(
                        up.at[n, :, pl.ds(row, 32), :],
                        target.at[pl.ds(rel * 4, 4)],
                        sem.at[(n * 4 + k) * 2 + rel],
                    )
                )
            return copies

        push(s, outs, copy_for)

    out_specs, out_shape = piece_outputs(8, 32)
    return kernel_call(
        kernel,
        meta,
        (normed_own, normed_other, du),
        [
            spec((512, 256), lambda s, m: (0, rel_chip(s, m))),
            spec((512, 256), lambda s, m: (0, rel_chip(s, m))),
            whole((1024, 2048)),
        ],
        out_specs,
        out_shape,
        [pltpu.VMEM((4, 4, 256, 512), BF), pltpu.SemaphoreType.DMA((32,))],
        flops=2 * 1024 * 1024 * 2048,
        moved=15 << 20,
    )


def weigh_qkv(meta, hidden, dqkv, out_terms=()):
    def kernel(m, x_ref, d_ref, *rest):
        s = pl.program_id(0)
        if out_terms:
            mixed_ref, more_ref, own_ref, other_ref = rest[:4]
            rest = rest[4:]
        outs, stage, sem = rest[:4], rest[4], rest[5]
        for t in range(3):
            stage[s, t] = dot(x_ref[...], d_ref[t], TN).astype(BF)
        if out_terms:
            stage_out, sem_out = rest[6:]
            x = jnp.where(rel_chip(s, m) < 2, mixed_ref[...].astype(F32), more_ref[...].astype(F32)).astype(BF)
            for b in range(4):
                columns = pl.ds(b * 256, 256)
                stage_out[s, b] = (
                    dot(x[:512], own_ref[:, columns], TN) + dot(x[512:], other_ref[:, columns], TN)
                ).astype(BF)

        def copy_for(n, k, target):
            z = m[3] ^ z_relative(k // 2, k % 2)
            copies = []
            for rel in range(2):
                row = pl.multiple_of((m[2] ^ rel) * 128 + z * 32, 32)
                copies.append(
                    pltpu.make_async_copy(
                        stage.at[n, :, pl.ds(row, 32), :],
                        target.at[pl.ds(rel * 3, 3)],
                        sem.at[(n * 4 + k) * 2 + rel],
                    )
                )
            if out_terms:
                copies.append(
                    pltpu.make_async_copy(
                        stage_out.at[n, :, pl.ds(pl.multiple_of(z * 32, 32), 32), :],
                        target.at[pl.ds(6, 4)],
                        sem_out.at[n * 4 + k],
                    )
                )
            return copies

        push(s, outs, copy_for)

    out_specs, out_shape = piece_outputs(10 if out_terms else 6, 32, 256)
    in_specs = [spec((1024, 256), lambda s, m: (0, rel_chip(s, m))), whole((3, 1024, 256))]
    scratch = [pltpu.VMEM((4, 3, 256, 256), BF), pltpu.SemaphoreType.DMA((32,))]
    if out_terms:
        in_specs += [spec((1024, 128), lambda s, m: (0, rel_chip(s, m) % 2))] * 2 + [whole((512, 1024))] * 2
        scratch += [pltpu.VMEM((4, 4, 128, 256), BF), pltpu.SemaphoreType.DMA((16,))]
    return kernel_call(
        kernel,
        meta,
        (hidden, dqkv, *out_terms),
        in_specs,
        out_specs,
        out_shape,
        scratch,
        flops=2 * 1024 * 1024 * 1024,
        moved=8 << 20,
    )


def qkv_back(meta, dqkv, pieces):
    def kernel(m, d_ref, e_ref, *rest):
        refs, (send_ref, own_ref, weight, sem) = rest[:4], rest[4:]
        i = pl.program_id(0)

        @pl.when(i == 0)
        def _():
            load_all(load_qkv(m, refs, weight, sem))

        total = jnp.zeros((256, 1024), F32)
        for t in range(3):
            total += dot(d_ref[t], weight[t, :, :256], NT) + dot(e_ref[t], weight[t, :, 256:], NT)

        @pl.when(i < 2)
        def _():
            send_ref[...] = total.astype(BF)

        @pl.when(i >= 2)
        def _():
            own_ref[...] = total

    return kernel_call(
        kernel,
        meta,
        (*dqkv, *pieces),
        [spec((3, 256, 256), lambda i, m: (0, turned(i), 0))] * 2 + [HBM] * 4,
        [spec((256, 1024), lambda i, m: (low_block(i), 0)), spec((256, 1024), lambda i, m: (high_block(i), 0))],
        [shaped((512, 1024), BF), shaped((512, 1024), F32)],
        [pltpu.VMEM((3, 1024, 512), BF), pltpu.SemaphoreType.DMA((96,))],
        flops=2 * 1024 * 1024 * 1536,
        moved=9 << 20,
    )


def last_sum(meta, resid, own, received):
    def kernel(m, resid_ref, own_ref, recv_ref, out_ref, sum_ref):
        total = resid_ref[...] + own_ref[...] + recv_ref[...].astype(F32)
        out_ref[...] = total.astype(BF)
        row_sums(sum_ref, pl.program_id(0), (total,))

    block = spec((256, 1024), BY_ROWS)
    return kernel_call(
        kernel,
        meta,
        (resid, own, received),
        [block, block, block],
        [block, whole((8, 1024))],
        [shaped((512, 1024), BF), shaped((8, 1024), F32)],
        grid=(2,),
        flops=512 * 1024 * 4,
        moved=6 << 20,
    )


VECTOR_SIZES = (64, 32, 32, 32, 128, 32, 32, 32)


def split_vectors(packed):
    parts, start = [], 0
    for size in VECTOR_SIZES:
        parts.append(packed[:, start : start + size])
        start += size
    return parts


def chip_body(
    tokens,
    timestep,
    segment_ids,
    cotangent,
    time_weight,
    qkv_weight,
    qv_bias,
    out_weight,
    out_bias,
    norm_gain,
    norm_bias,
    up_weight,
    up_bias,
    down_weight,
    down_bias,
    final_gain,
    final_bias,
):
    dp, z = lax.axis_index("dp"), lax.axis_index("sp")
    y, x, c = dp // 4, (dp // 2) % 2, dp % 2
    meta = jnp.stack([y, x, c, z]).astype(jnp.int32)
    pick = lambda value, index, axis: lax.dynamic_index_in_dim(value, index, axis, keepdims=False)

    me = dp * 4 + z

    qkv_split = qkv_weight.reshape(32, 3, 4, 2, 128)
    up_split = up_weight.reshape(32, 4, 2, 512)
    qkv_half = lambda core: pick(qkv_split, core, 3).reshape(32, 3, 512).transpose(1, 0, 2).reshape(96, 512)
    up_half = lambda core: pick(up_split, core, 2).transpose(1, 0, 2)
    small = jnp.concatenate([qv_bias, out_bias, norm_gain, norm_bias, up_bias, down_bias, final_gain, final_bias])
    small = jnp.pad(small[None], ((0, 15), (0, 128)))
    received = send(jnp.concatenate([qkv_half(1 - c), small]), PAIR)
    small = jnp.concatenate([small[:1], received[96:97], small[2:]])
    qkv_shard = jnp.concatenate([qkv_half(c), received[:96], small])
    out_shard = out_weight.reshape(32, 2, 512).transpose(1, 0, 2)
    mid_shard = jnp.concatenate([out_shard, up_half(c), send(up_half(1 - c), PAIR)])
    down_shard = down_weight.reshape(128, 2, 512).transpose(1, 0, 2)
    qkv_line = gather_line(qkv_shard)

    stamps = after(timestep.astype(jnp.int32), received)[:, None]
    stamps = jnp.concatenate([stamps // 64, stamps % 64], axis=1).astype(BF)
    for pairs in (PAIR, ALONG_X, ALONG_Y):
        stamps = jnp.concatenate([stamps, send(stamps, pairs)])
    stamps = stamps.astype(F32)
    stamps = (stamps[:, 0] * 64.0 + stamps[:, 1]).reshape(4, 4)
    sums_order = jnp.arange(4, dtype=jnp.int32) ^ z
    from_pair = (sums_order // 2) ^ c
    stamps = jnp.take_along_axis(stamps, jnp.broadcast_to(from_pair * 2 + sums_order % 2, (4, 4)), axis=1).reshape(16, 1)
    column = me * 32 + jnp.arange(32, dtype=jnp.int32)
    frequency = jnp.exp(-math.log(10000.0) * (column % 512).astype(F32) / 512)
    phases = stamps * frequency[None, :]
    features = jnp.where(column[None, :] < 512, jnp.sin(phases), jnp.cos(phases)).astype(BF)
    features = after(features, qkv_line[0])
    embedded = jnp.dot(features, time_weight, preferred_element_type=F32)
    embedded = embedded + send(embedded, PAIR)
    for width, pairs in ((8, ALONG_Y), (4, ALONG_X), (2, ALONG_Z[2]), (1, ALONG_Z[1])):
        embedded = embedded[:width] + send(embedded[width:], pairs)

    mid_line = gather_line(after(mid_shard, qkv_line))
    qkv_pieces = gather_plane(*qkv_line)

    def take_rows(value):
        return jnp.stack([send(pick(value, (z + k) % 2, 0), ROW_OUT[k]) for k in range(2)])

    def give_rows(value):
        parts = [send(value[k * 256 : (k + 1) * 256], ROW_BACK[k]) for k in range(2)]
        swapped = (z % 2) == 1
        return jnp.stack([jnp.where(swapped, parts[1], parts[0]), jnp.where(swapped, parts[0], parts[1])])

    documents = jnp.concatenate([segment_ids // 32, segment_ids % 32], axis=1).astype(BF)
    documents = jnp.pad(documents[:, None, :], ((0, 0), (0, 15), (0, 512)))
    own_tokens = take_rows(after(jnp.concatenate([tokens, documents], axis=1), mid_line))
    other_tokens = send(own_tokens, PAIR)
    codes = jnp.concatenate([own_tokens[:, 256], other_tokens[:, 256]]).astype(F32)
    segments = (codes[:, :256] * 32.0 + codes[:, 256:512]).reshape(1024)
    seg_column, seg_row = segments[:, None], segments[None, :]

    mid_pieces = gather_plane(*mid_line)

    natural = jnp.arange(32, dtype=jnp.int32)
    order = (natural[:, None] ^ me) == natural[None, :]
    small = jnp.stack([piece[:, :, 192:194, :384] for piece in qkv_pieces])
    small = jnp.stack(
        [
            small[half * 2 + (x_rel if half else y_rel), y_rel if half else x_rel, j, rel]
            for y_rel in range(2)
            for x_rel in range(2)
            for rel in range(2)
            for j in range(2)
            for half in range(2)
        ]
    )
    small = jnp.dot(order.astype(BF), small, preferred_element_type=F32)
    full = [part.reshape(1, -1) for part in split_vectors(small)]
    qv_full, out_shift, first_gain, first_shift, up_full, down_shift, second_gain, second_shift = full
    blank = jnp.zeros((2, 1024), F32)
    vectors = jnp.concatenate([out_shift, first_gain, first_shift, down_shift, second_gain, second_shift, blank])
    qv_mine = pick(qv_full.reshape(2, 4, 2, 128), c, 2).reshape(2, 512)
    qkv_shift = jnp.stack([qv_mine[0], jnp.zeros((512,), F32), qv_mine[1]])
    up_shift = pick(up_full.reshape(4, 2, 512), c, 1).reshape(1, 2048)

    hidden, qkv = project_qkv(meta, own_tokens, other_tokens, embedded, qkv_shift, qkv_pieces)
    mixed_one, lse_one = attend(meta, 0, qkv, seg_column, seg_row)
    down_first = jnp.stack([after(down_shard, mixed_one), send(after(down_shard, qkv), ALONG_Z[2])])
    mixed_two, lse_two = attend(meta, 1, after(qkv, down_first), seg_column, seg_row)
    down_second = after(send(down_first, ALONG_Z[1]), mixed_two)
    mixed = mixed_one, after(mixed_two, down_second)
    away, mine = project_out(meta, mixed, mid_pieces)
    own_cotangent = take_rows(after(cotangent, down_second))
    down_pieces = gather_plane(down_first, down_second, mine)
    normal_one, inverse_one, normed = first_norm(meta, own_tokens, embedded, mine, send(away, PAIR), vectors)
    normed_other = send(normed, PAIR)
    activated, slope = expand(meta, normed, after(normed_other, down_pieces[0], down_pieces[2]), up_shift, mid_pieces)
    away, mine = contract(meta, after(activated, own_cotangent), down_pieces)
    own_cotangent = after(own_cotangent, mine).reshape(512, 1024)
    result, resid_two, df, sums_two = second_norm(meta, normal_one, mine, send(away, PAIR), own_cotangent, vectors)

    df_other = send(df, PAIR)
    down_terms = weigh_down(meta, activated, df, df_other)
    du, away, mine, up_sums = feed_back(meta, after(df, down_terms), df_other, slope, down_pieces, mid_pieces)
    received = send(away, PAIR)
    up_terms = weigh_up(meta, normed, normed_other, du)
    down_sums = add_one(*scatter_one(*down_terms), up_terms)
    resid_one, da, sums_one = first_norm_back(
        meta, after(resid_two, down_sums), mine, received, normal_one, inverse_one, vectors
    )
    da_other = send(da, PAIR)
    dout = output_back(meta, da, da_other, mid_pieces)
    down_sums = add_two(*scatter_two(*down_sums), dout)
    output = give_rows(after(result, dout))
    grad = after(dout, down_sums)
    dqkv_one, qv_sums_one = attend_back(meta, 0, qkv, mixed_one, grad, lse_one, seg_column, seg_row)
    output = after(output, dqkv_one)
    qkv_terms_one = weigh_qkv(meta, hidden, after(dqkv_one, output), (mixed_one, mixed_two, da, da_other))
    up_sums_one = add_one(*scatter_one(*after(up_terms, dout)), qkv_terms_one)
    down_sums = add_three(*scatter_three(*down_sums), qkv_terms_one)
    grad = after(dout, up_sums_one, down_sums)
    dqkv_two, qv_sums_two = attend_back(meta, 1, qkv, mixed_two, grad, lse_two, seg_column, seg_row)
    up_sums_two = add_two(*scatter_two(*up_sums_one), dqkv_two)
    down_share = scatter_four(*down_sums, dqkv_two)
    away, mine = qkv_back(meta, (dqkv_one, after(dqkv_two, up_sums_two, down_share)), qkv_pieces)
    received = send(away, PAIR)
    qkv_terms_two = weigh_qkv(meta, hidden, after(dqkv_two, mine))
    qkv_sums_one = add_one(*scatter_one(*qkv_terms_one), mine)
    input_low, embed_sums = last_sum(meta, resid_one, after(mine, qkv_terms_two), received)
    input_grad = give_rows(input_low)
    up_sums_three = add_three(*scatter_three(*up_sums_two), qkv_terms_two)
    qkv_sums_one = add_two(*scatter_two(*qkv_sums_one), input_low)
    qkv_sums_two = add_one(*scatter_one(*qkv_terms_two), input_low)
    qkv_sums_two = add_two(*scatter_two(*qkv_sums_two))
    qkv_sums_one = add_three(*scatter_three(*qkv_sums_one))
    up_share = scatter_four(*up_sums_three, input_low)
    qkv_sums_two = add_three(*scatter_three(*qkv_sums_two))
    qkv_share_one = scatter_four(*qkv_sums_one)
    qkv_share_two = scatter_four(*after(qkv_sums_two, input_grad))
    qkv_share = jnp.concatenate([qkv_share_one[:6], qkv_share_two], axis=2)
    qv_sums = jnp.concatenate([qv_sums_one[0:2], qv_sums_two[0:2]], axis=1)

    def both_halves(own, received):
        return jnp.where(c == 0, jnp.stack([own, received], axis=-2), jnp.stack([received, own], axis=-2))

    grad_down = down_share.transpose(1, 0, 2).reshape(128, 1024)
    grad_out = qkv_share_one[6:].transpose(1, 0, 2).reshape(32, 1024)
    grad_up = both_halves(up_share[:4], send(up_share[4:], PAIR))
    grad_up = grad_up.transpose(1, 0, 2, 3).reshape(32, 4096)
    split = lambda share: share.reshape(3, 32, 4, 128)
    grad_qkv = both_halves(split(qkv_share[:3]), split(send(qkv_share[3:], PAIR)))
    grad_qkv = grad_qkv.transpose(1, 0, 2, 3, 4).reshape(32, 3072)

    core_lane = (jnp.arange(2) == c).astype(F32)
    spread = lambda sums, width: (sums.reshape(-1, 1, width) * core_lane[None, :, None]).reshape(32, -1)
    grads = jnp.concatenate(
        [
            spread(qv_sums, 128),
            sums_one[2].reshape(32, 32),
            sums_one[0].reshape(32, 32),
            sums_one[1].reshape(32, 32),
            spread(up_sums[0:1], 512),
            sums_two[2].reshape(32, 32),
            sums_two[0].reshape(32, 32),
            sums_two[1].reshape(32, 32),
        ],
        axis=1,
    )
    total = jnp.dot(order.astype(F32), after(grads, embed_sums), precision=lax.Precision.HIGHEST)
    total = total.reshape(2, 2, 2, 4, 3, 128).transpose(2, 3, 1, 0, 4, 5).reshape(96, 128)
    sums = embed_sums[0:1].reshape(8, 128)
    received = send(jnp.concatenate([total[48:], sums]), PAIR)
    total, sums = total[:48] + received[:48], sums + received[48:]
    for width, pairs in ((24, ALONG_Z[2]), (12, ALONG_Z[1]), (6, ALONG_X), (3, ALONG_Y)):
        received = send(jnp.concatenate([total[width:], sums]), pairs)
        total, sums = total[:width] + received[:width], jnp.concatenate([sums, received[width:]])
    small_grads = [part.reshape(-1) for part in split_vectors(total.reshape(1, 384))]
    sums = sums.reshape(2, 2, 2, 2, 1024).transpose(0, 1, 3, 2, 4).reshape(16, 1024)
    grad_time = jnp.dot(features.astype(F32).T, sums, precision=lax.Precision.HIGHEST)

    return (
        output,
        input_grad,
        grad_time,
        grad_qkv,
        small_grads[0],
        grad_out,
        *small_grads[1:4],
        grad_up,
        small_grads[4],
        grad_down,
        *small_grads[5:],
    )


def solution(mesh):
    in_specs = (
        P("dp", "sp", None),
        P("dp"),
        P("dp", "sp"),
        P("dp", "sp", None),
        P(("dp", "sp"), None),
        P(("dp", "sp"), None),
        P(("dp", "sp")),
        P(("dp", "sp"), None),
        P(("dp", "sp")),
        P(("dp", "sp")),
        P(("dp", "sp")),
        P(("dp", "sp"), None),
        P(("dp", "sp")),
        P(("dp", "sp"), None),
        P(("dp", "sp")),
        P(("dp", "sp")),
        P(("dp", "sp")),
    )
    out_specs = (
        P("dp", "sp", None),
        P("dp", "sp", None),
        P(("dp", "sp"), None),
        P(("dp", "sp"), None),
        P(("dp", "sp")),
        P(("dp", "sp"), None),
        P(("dp", "sp")),
        P(("dp", "sp")),
        P(("dp", "sp")),
        P(("dp", "sp"), None),
        P(("dp", "sp")),
        P(("dp", "sp"), None),
        P(("dp", "sp")),
        P(("dp", "sp")),
        P(("dp", "sp")),
    )
    plan = chip_body if dict(mesh.shape) == {"dp": 8, "sp": 4} else body
    return jax.shard_map(plan, mesh=mesh, in_specs=in_specs, out_specs=out_specs, check_vma=False)
```

```python
import math

import jax
import jax.numpy as jnp
from jax import lax
from jax.experimental import pallas as pl
from jax.experimental.pallas import tpu as pltpu
from jax.sharding import PartitionSpec as P

HEADS = 16
HEAD_DIM = 64


EPSILON = 1e-05
INVERSE_ROOT_TWO = 1.0 / math.sqrt(2.0)
INVERSE_ROOT_TWO_PI = 1.0 / math.sqrt(2.0 * math.pi)


def time_features(stamps, model_width):
    halfway = model_width // 2
    frequency = jnp.exp(-math.log(10000.0) * jnp.arange(halfway, dtype=jnp.float32) / halfway)
    phases = stamps.astype(jnp.float32)[:, None] * frequency[None, :]
    return jnp.concatenate([jnp.sin(phases), jnp.cos(phases)], axis=1)


def layer_norm_parts(values, gain, offset):
    center = values - jnp.mean(values, axis=-1, keepdims=True)
    variance = jnp.mean(center * center, axis=-1, keepdims=True)
    inverse = lax.rsqrt(variance + EPSILON)
    normal_part = center * inverse
    return (normal_part * gain + offset, normal_part, inverse)


def layer_norm_back(upstream, normal_part, inverse, gain):
    scaled = upstream * gain
    return inverse * (
        scaled
        - jnp.mean(scaled, axis=-1, keepdims=True)
        - normal_part * jnp.mean(scaled * normal_part, axis=-1, keepdims=True)
    )


def gelu_slope(values):
    cumulative = 0.5 * (1.0 + lax.erf(values * INVERSE_ROOT_TWO))
    density = jnp.exp(-0.5 * values * values) * INVERSE_ROOT_TWO_PI
    return cumulative + values * density


def contract_rows(left, right):
    return lax.dot_general(
        left, right, (((0,), (0,)), ((), ())), preferred_element_type=jnp.float32
    )


def times_transposed(left, right):
    return lax.dot_general(
        left, right, (((1,), (1,)), ((), ())), preferred_element_type=jnp.float32
    )


def flatten_grads(grads):
    return tuple((grad.reshape(-1, 128) if grad.ndim == 2 else grad for grad in grads))


def restore_grads(shares, templates):
    return tuple((share.reshape(template.shape) for share, template in zip(shares, templates)))


def attention_forward(queries, keys_all, values_all, seg_full, query_block, scale):
    block_count = queries.shape[1] // query_block

    def one_block(index):
        start = index * query_block
        query_part = lax.dynamic_slice_in_dim(queries, start, query_block, 1)
        seg_part = lax.dynamic_slice_in_dim(seg_full, start, query_block, 1)
        scores = (
            jnp.einsum("rqhd,rkhd->rhqk", query_part, keys_all, preferred_element_type=jnp.float32)
            * scale
        )
        allowed = seg_part[:, None, :, None] == seg_full[:, None, None, :]
        scores = jnp.where(allowed, scores, -1e30)
        largest = jnp.max(scores, axis=-1, keepdims=True)
        exponent = jnp.exp(scores - largest)
        totals = jnp.sum(exponent, axis=-1, keepdims=True)
        probability = exponent / totals
        log_total = largest[..., 0] + jnp.log(totals[..., 0])
        mixed = jnp.einsum(
            "rhqk,rkhd->rqhd",
            probability.astype(jnp.bfloat16),
            values_all,
            preferred_element_type=jnp.float32,
        )
        return (mixed, log_total)

    mixed_blocks, log_totals = lax.map(one_block, jnp.arange(block_count, dtype=jnp.int32))
    mixed = jnp.moveaxis(mixed_blocks, 0, 1).reshape(queries.shape)
    return (mixed, log_totals)


def attention_backward(
    queries, keys_all, values_all, seg_full, grad_heads, log_totals, query_block, scale
):
    block_count = queries.shape[1] // query_block

    def one_block(carry, index):
        key_grad, value_grad = carry
        start = index * query_block
        query_part = lax.dynamic_slice_in_dim(queries, start, query_block, 1)
        seg_part = lax.dynamic_slice_in_dim(seg_full, start, query_block, 1)
        grad_part = lax.dynamic_slice_in_dim(grad_heads, start, query_block, 1)
        scores = (
            jnp.einsum("rqhd,rkhd->rhqk", query_part, keys_all, preferred_element_type=jnp.float32)
            * scale
        )
        allowed = seg_part[:, None, :, None] == seg_full[:, None, None, :]
        scores = jnp.where(allowed, scores, -1e30)
        probability = jnp.exp(scores - log_totals[index][..., None])
        dotted = jnp.einsum(
            "rqhd,rkhd->rhqk", grad_part, values_all, preferred_element_type=jnp.float32
        )
        center = jnp.sum(probability * dotted, axis=-1, keepdims=True)
        score_grad = (probability * (dotted - center)).astype(jnp.bfloat16)
        query_grad = (
            jnp.einsum("rhqk,rkhd->rqhd", score_grad, keys_all, preferred_element_type=jnp.float32)
            * scale
        )
        key_grad = (
            key_grad
            + jnp.einsum(
                "rhqk,rqhd->rkhd", score_grad, query_part, preferred_element_type=jnp.float32
            )
            * scale
        )
        value_grad = value_grad + jnp.einsum(
            "rhqk,rqhd->rkhd",
            probability.astype(jnp.bfloat16),
            grad_part,
            preferred_element_type=jnp.float32,
        )
        return ((key_grad, value_grad), query_grad)

    starting = (jnp.zeros(keys_all.shape, jnp.float32), jnp.zeros(values_all.shape, jnp.float32))
    (key_grad, value_grad), query_blocks = lax.scan(
        one_block, starting, jnp.arange(block_count, dtype=jnp.int32)
    )
    query_grad = jnp.moveaxis(query_blocks, 0, 1).reshape(queries.shape)
    return (query_grad, key_grad, value_grad)


def body(
    tokens,
    timestep,
    segment_ids,
    cotangent,
    time_weight,
    qkv_weight,
    qv_bias,
    out_weight,
    out_bias,
    norm_gain,
    norm_bias,
    up_weight,
    up_bias,
    down_weight,
    down_bias,
    final_gain,
    final_bias,
):
    shards = (
        time_weight,
        qkv_weight,
        qv_bias,
        out_weight,
        out_bias,
        norm_gain,
        norm_bias,
        up_weight,
        up_bias,
        down_weight,
        down_bias,
        final_gain,
        final_bias,
    )
    sp_count = lax.axis_size("sp")
    micro_count = max(2, sp_count // 2)
    rows_local, piece_len, model_width = tokens.shape
    rows_micro = rows_local // micro_count
    seq_len = piece_len * sp_count
    width_local = model_width // sp_count
    heads_local = HEADS // sp_count
    query_block = min(512, seq_len)
    scale = 1.0 / math.sqrt(HEAD_DIM)
    tok_count = rows_micro * piece_len
    owned = tuple((jnp.zeros(piece.shape, jnp.float32) for piece in shards))
    output_parts = []
    input_parts = []
    for micro in range(micro_count):
        first_row = micro * rows_micro
        block_tokens = tokens[first_row : first_row + rows_micro]
        block_cotangent = cotangent[first_row : first_row + rows_micro]
        block_segments = segment_ids[first_row : first_row + rows_micro]
        block_stamps = timestep[first_row : first_row + rows_micro]
        gathered = (
            lax.all_gather(shards[0], ("dp", "sp"), axis=0, tiled=True),
            lax.all_gather(shards[1], ("dp", "sp"), axis=0, tiled=True),
            lax.all_gather(shards[2], ("dp", "sp"), axis=0, tiled=True),
            lax.all_gather(shards[3], ("dp", "sp"), axis=0, tiled=True),
            lax.all_gather(shards[4], ("dp", "sp"), axis=0, tiled=True),
            lax.all_gather(shards[5], ("dp", "sp"), axis=0, tiled=True),
            lax.all_gather(shards[6], ("dp", "sp"), axis=0, tiled=True),
            lax.all_gather(shards[7], ("dp", "sp"), axis=0, tiled=True),
            lax.all_gather(shards[8], ("dp", "sp"), axis=0, tiled=True),
            lax.all_gather(shards[9], ("dp", "sp"), axis=0, tiled=True),
            lax.all_gather(shards[10], ("dp", "sp"), axis=0, tiled=True),
            lax.all_gather(shards[11], ("dp", "sp"), axis=0, tiled=True),
            lax.all_gather(shards[12], ("dp", "sp"), axis=0, tiled=True),
        )
        (
            time_full,
            qkv_full,
            qv_full,
            out_full,
            out_shift,
            first_gain,
            first_shift,
            up_full,
            up_shift,
            down_full,
            down_shift,
            second_gain,
            second_shift,
        ) = gathered
        features = time_features(block_stamps, model_width).astype(jnp.bfloat16)
        embedded = jnp.dot(features, time_full, preferred_element_type=jnp.float32)
        hidden = block_tokens.astype(jnp.float32) + embedded[:, None, :]
        hidden_flat = hidden.reshape(tok_count, model_width)
        hidden_low = hidden_flat.astype(jnp.bfloat16)
        qv_float = qv_full.astype(jnp.float32)
        qkv_shift = jnp.concatenate(
            [qv_float[:model_width], jnp.zeros((model_width,), jnp.float32), qv_float[model_width:]]
        )
        packed = jnp.dot(hidden_low, qkv_full, preferred_element_type=jnp.float32) + qkv_shift
        packed = packed.astype(jnp.bfloat16).reshape(rows_micro, piece_len, 3, model_width)
        seg_copies = jnp.broadcast_to(
            block_segments[:, :, None, None], (rows_micro, piece_len, 1, sp_count)
        )
        packed_heads, seg_heads = (
            lax.all_to_all(packed, "sp", split_axis=3, concat_axis=1, tiled=True),
            lax.all_to_all(seg_copies, "sp", split_axis=3, concat_axis=1, tiled=True),
        )
        seg_full = seg_heads[:, :, 0, 0]
        head_shape = (rows_micro, seq_len, heads_local, HEAD_DIM)
        queries = packed_heads[:, :, 0].reshape(head_shape)
        keys_all = packed_heads[:, :, 1].reshape(head_shape)
        values_all = packed_heads[:, :, 2].reshape(head_shape)
        mixed, log_totals = attention_forward(
            queries, keys_all, values_all, seg_full, query_block, scale
        )
        mixed_low = mixed.astype(jnp.bfloat16).reshape(rows_micro, seq_len, width_local)
        mixed_local = lax.all_to_all(mixed_low, "sp", split_axis=1, concat_axis=2, tiled=True)
        mixed_flat = mixed_local.reshape(tok_count, model_width)
        attended = jnp.dot(
            mixed_flat, out_full, preferred_element_type=jnp.float32
        ) + out_shift.astype(jnp.float32)
        first_gain_f = first_gain.astype(jnp.float32)
        normed, normal_one, inverse_one = layer_norm_parts(
            hidden_flat + attended, first_gain_f, first_shift.astype(jnp.float32)
        )
        normed_low = normed.astype(jnp.bfloat16)
        upward = jnp.dot(normed_low, up_full, preferred_element_type=jnp.float32) + up_shift.astype(
            jnp.float32
        )
        activated = jax.nn.gelu(upward, approximate=False).astype(jnp.bfloat16)
        downward = jnp.dot(
            activated, down_full, preferred_element_type=jnp.float32
        ) + down_shift.astype(jnp.float32)
        second_gain_f = second_gain.astype(jnp.float32)
        result, normal_two, inverse_two = layer_norm_parts(
            normed + downward, second_gain_f, second_shift.astype(jnp.float32)
        )
        output_parts.append(result.astype(jnp.bfloat16).reshape(rows_micro, piece_len, model_width))
        upstream = block_cotangent.reshape(tok_count, model_width).astype(jnp.float32)
        grad_second_gain = jnp.sum(upstream * normal_two, axis=0)
        grad_second_shift = jnp.sum(upstream, axis=0)
        resid_two = layer_norm_back(upstream, normal_two, inverse_two, second_gain_f)
        down_grad = resid_two.astype(jnp.bfloat16)
        grad_down_shift = jnp.sum(down_grad, axis=0, dtype=jnp.float32)
        grad_down_full = contract_rows(activated, down_grad)
        act_grad = times_transposed(down_grad, down_full)
        up_grad = (act_grad * gelu_slope(upward)).astype(jnp.bfloat16)
        grad_up_shift = jnp.sum(up_grad, axis=0, dtype=jnp.float32)
        grad_up_full = contract_rows(normed_low, up_grad)
        normed_grad = resid_two + times_transposed(up_grad, up_full)
        grad_first_gain = jnp.sum(normed_grad * normal_one, axis=0)
        grad_first_shift = jnp.sum(normed_grad, axis=0)
        resid_one = layer_norm_back(normed_grad, normal_one, inverse_one, first_gain_f)
        attended_grad = resid_one.astype(jnp.bfloat16)
        grad_out_shift = jnp.sum(attended_grad, axis=0, dtype=jnp.float32)
        grad_out_full = contract_rows(mixed_flat, attended_grad)
        mixed_grad = times_transposed(attended_grad, out_full).astype(jnp.bfloat16)
        mixed_grad = mixed_grad.reshape(rows_micro, piece_len, model_width)
        grad_heads = lax.all_to_all(
            mixed_grad, "sp", split_axis=2, concat_axis=1, tiled=True
        ).reshape(head_shape)
        query_grad, key_grad, value_grad = attention_backward(
            queries, keys_all, values_all, seg_full, grad_heads, log_totals, query_block, scale
        )
        packed_grad = jnp.stack([query_grad, key_grad, value_grad], axis=2)
        packed_grad = packed_grad.reshape(rows_micro, seq_len, 3, width_local).astype(jnp.bfloat16)
        packed_local = lax.all_to_all(packed_grad, "sp", split_axis=1, concat_axis=3, tiled=True)
        packed_flat = packed_local.reshape(tok_count, 3 * model_width)
        third_sums = jnp.sum(packed_flat, axis=0, dtype=jnp.float32)
        grad_qv_full = jnp.concatenate([third_sums[:model_width], third_sums[2 * model_width :]])
        grad_qkv_full = contract_rows(hidden_low, packed_flat)
        hidden_grad = resid_one + times_transposed(packed_flat, qkv_full)
        input_parts.append(
            hidden_grad.astype(jnp.bfloat16).reshape(rows_micro, piece_len, model_width)
        )
        embed_grad = jnp.sum(hidden_grad.reshape(rows_micro, piece_len, model_width), axis=1)
        grad_time_full = jnp.dot(
            features.astype(jnp.float32).T, embed_grad, precision=lax.Precision.HIGHEST
        )
        grads = (
            grad_time_full,
            grad_qkv_full,
            grad_qv_full,
            grad_out_full,
            grad_out_shift,
            grad_first_gain,
            grad_first_shift,
            grad_up_full,
            grad_up_shift,
            grad_down_full,
            grad_down_shift,
            grad_second_gain,
            grad_second_shift,
        )
        shares = lax.psum_scatter(
            flatten_grads(grads), ("dp", "sp"), scatter_dimension=0, tiled=True
        )
        owned = jax.tree.map(jnp.add, owned, restore_grads(shares, owned))
    output = jnp.concatenate(output_parts, axis=0)
    input_grad = jnp.concatenate(input_parts, axis=0)
    return (
        output,
        input_grad,
        owned[0],
        owned[1],
        owned[2],
        owned[3],
        owned[4],
        owned[5],
        owned[6],
        owned[7],
        owned[8],
        owned[9],
        owned[10],
        owned[11],
        owned[12],
    )


AXES = ("dp", "sp")
BF = jnp.bfloat16
F32 = jnp.float32
NT = (((1,), (1,)), ((), ()))
TN = (((0,), (0,)), ((), ()))
NN = (((1,), (0,)), ((), ()))
VMEM_LIMIT = 58 * 1024 * 1024
CHIP_SLOTS = (
    ((0, 0, 0), (0, 0, 1)),
    ((0, 1, 0), (0, 1, 1)),
    ((1, 0, 0), (1, 1, 0)),
    ((1, 0, 1), (1, 1, 1)),
)


def dot(left, right, dims=NN):
    return lax.dot_general(left, right, dims, preferred_element_type=F32)


def device_perm(target):
    pairs = []
    for y in range(2):
        for x in range(2):
            for c in range(2):
                for z in range(4):
                    ty, tx, tc, tz = target(y, x, c, z)
                    source = ((y * 2 + x) * 2 + c) * 4 + z
                    pairs.append((source, ((ty * 2 + tx) * 2 + tc) * 4 + tz))
    return pairs


PAIR = device_perm(lambda y, x, c, z: (y, x, 1 - c, z))
ALONG_X = device_perm(lambda y, x, c, z: (y, 1 - x, c, z))
ALONG_Y = device_perm(lambda y, x, c, z: (1 - y, x, c, z))
ALONG_Z = [device_perm(lambda y, x, c, z, k=k: (y, x, c, z ^ k)) for k in range(3)]
ROW_OUT = [device_perm(lambda y, x, c, z, k=k: (y, x, z // 2, c * 2 + (z + k) % 2)) for k in range(2)]
ROW_BACK = [[(t, s) for s, t in pairs] for pairs in ROW_OUT]


def send(value, pairs):
    return lax.ppermute(value, AXES, pairs)


def after(value, *earlier):
    return lax.optimization_barrier((value, earlier))[0]


def gather_line(shard):
    first = jnp.stack([shard, send(shard, ALONG_Z[2])])
    return first, send(first, ALONG_Z[1])


def gather_plane(first, second, *earlier):
    first_x, second_y = lax.optimization_barrier((send(first, ALONG_X), send(second, ALONG_Y)))
    first, second = jnp.stack([after(first, earlier), first_x]), jnp.stack([after(second, earlier), second_y])
    return [first, send(first, ALONG_Y), second, send(second, ALONG_X)]


def add_low(a, b):
    return (a.astype(F32) + b.astype(F32)).astype(BF)


def scatter_one(first_keep, first_send, second_keep, second_send):
    return first_keep, send(first_send, ALONG_Y), second_keep, send(second_send, ALONG_X)


def add_one(first_keep, from_y, second_keep, from_x, *earlier):
    first_keep, second_keep = after((first_keep, second_keep), earlier)
    to_x, to_y = add_low(first_keep[1], from_y[1]), add_low(second_keep[1], from_x[1])
    return add_low(first_keep[0], from_y[0]), to_x, add_low(second_keep[0], from_x[0]), to_y


def scatter_two(first, to_x, second, to_y):
    return first, send(to_x, ALONG_X), second, send(to_y, ALONG_Y)


def add_two(first, from_x, second, from_y, *earlier):
    first, second = after((first, second), earlier)
    return add_low(first, from_x), add_low(second, from_y)


def scatter_three(first, second):
    return first, send(second, ALONG_Z[1])


def add_three(first, received, *earlier):
    first = after(first, earlier)
    return add_low(first[0], received[0]), add_low(first[1], received[1])


def scatter_four(near, far, *earlier):
    return after(near, earlier).astype(F32) + send(far, ALONG_Z[2]).astype(F32)


def z_relative(half, j):
    return 2 * j + half


def place(meta, slot, at, j):
    half, y_rel, x_rel = CHIP_SLOTS[slot][at]
    chip = (meta[0] ^ y_rel) * 2 + (meta[1] ^ x_rel)
    return chip, meta[3] ^ z_relative(half, j)


def load_all(copies):
    for copy in copies:
        copy.start()
    for copy in copies:
        copy.wait()


def load_qkv(meta, refs, weight, sem):
    copies = []
    for slot, ref in enumerate(refs):
        for at in range(2):
            for j in range(2):
                chip, z = place(meta, slot, at, j)
                for other in range(2):
                    row = pl.multiple_of((chip * 2 + (meta[2] ^ other)) * 128 + z * 32, 32)
                    for t in range(3):
                        copies.append(
                            pltpu.make_async_copy(
                                ref.at[at, j, pl.ds((other * 3 + t) * 32, 32)],
                                weight.at[t, pl.ds(row, 32), :],
                                sem.at[len(copies)],
                            )
                        )
    return copies


def load_split_rows(meta, refs, base, blocks, weight, sem):
    copies = []
    for slot, ref in enumerate(refs):
        for at in range(2):
            for j in range(2):
                chip, z = place(meta, slot, at, j)
                for other in range(2):
                    row = pl.multiple_of((chip * 2 + (meta[2] ^ other)) * 128 + z * 32, 32)
                    copies.append(
                        pltpu.make_async_copy(
                            ref.at[at, j, pl.ds(base + other * blocks, blocks)],
                            weight.at[:, pl.ds(row, 32), :],
                            sem.at[len(copies)],
                        )
                    )
    return copies


def load_out(meta, refs, weight, sem):
    copies = []
    for slot, ref in enumerate(refs):
        for at in range(2):
            for j in range(2):
                chip, z = place(meta, slot, at, j)
                row = pl.multiple_of((chip * 4 + z) * 32, 32)
                for b in range(2):
                    copies.append(
                        pltpu.make_async_copy(
                            ref.at[at, j, pl.ds(192 + b * 32, 32)],
                            weight.at[b, pl.ds(row, 32), :],
                            sem.at[len(copies)],
                        )
                    )
    return copies


def load_own_rows(meta, refs, base, blocks, rows, weight, sem):
    copies = []
    for slot, ref in enumerate(refs):
        for at in range(2):
            for j in range(2):
                chip, z = place(meta, slot, at, j)
                row = pl.multiple_of((chip * 4 + z) * rows, 32)
                copies.append(
                    pltpu.make_async_copy(
                        ref.at[at, j, pl.ds(base, blocks)],
                        weight.at[:, pl.ds(row, rows), :],
                        sem.at[len(copies)],
                    )
                )
    return copies


def kernel_call(kernel, meta, operands, in_specs, out_specs, out_shape, scratch=(), grid=(4,), flops=0, moved=0, exps=0):
    return pl.pallas_call(
        kernel,
        grid_spec=pltpu.PrefetchScalarGridSpec(
            num_scalar_prefetch=1,
            grid=grid,
            in_specs=in_specs,
            out_specs=out_specs,
            scratch_shapes=list(scratch),
        ),
        out_shape=out_shape,
        compiler_params=pltpu.CompilerParams(vmem_limit_bytes=VMEM_LIMIT),
        cost_estimate=pl.CostEstimate(
            flops=int(flops * 1.5), bytes_accessed=int(moved * 1.5), transcendentals=int(exps * 1.5)
        ),
    )(meta, *operands)


HBM = pl.BlockSpec(memory_space=pl.ANY)


def spec(shape, index):
    return pl.BlockSpec(shape, index)


def whole(shape):
    return pl.BlockSpec(shape, lambda i, m: (0,) * len(shape))


def shaped(shape, kind):
    return jax.ShapeDtypeStruct(shape, kind)


def low_block(i):
    return jnp.minimum(i, 1)


def high_block(i):
    return jnp.maximum(i - 2, 0)


def turned(i):
    return lax.rem(i + 2, 4)


def project_qkv(meta, own, other, embedded, shift, pieces):
    def kernel(m, own_ref, other_ref, emb_ref, shift_ref, *rest):
        refs, (hidden_ref, out_ref, weight, sem) = rest[:4], rest[4:]
        i = pl.program_id(0)

        @pl.when(i == 0)
        def _():
            load_all(load_qkv(m, refs, weight, sem))

        tokens = jnp.where(i < 2, own_ref[0].astype(F32), other_ref[0].astype(F32))
        hidden = (tokens + emb_ref[...]).astype(BF)
        hidden_ref[...] = hidden
        for t in range(3):
            out_ref[t] = (dot(hidden, weight[t]) + shift_ref[t : t + 1, :]).astype(BF)

    return kernel_call(
        kernel,
        meta,
        (own, other, embedded, shift, *pieces),
        [
            spec((1, 256, 1024), lambda i, m: (low_block(i), 0, 0)),
            spec((1, 256, 1024), lambda i, m: (high_block(i), 0, 0)),
            whole((1, 1024)),
            whole((3, 512)),
        ]
        + [HBM] * 4,
        [spec((256, 1024), lambda i, m: (i, 0)), spec((3, 256, 512), lambda i, m: (0, i, 0))],
        [shaped((1024, 1024), BF), shaped((3, 1024, 512), BF)],
        [pltpu.VMEM((3, 1024, 512), BF), pltpu.SemaphoreType.DMA((96,))],
        flops=2 * 1024 * 1024 * 1536,
        moved=10 << 20,
    )


def head_lanes(h, kind):
    lane = lax.broadcasted_iota(jnp.int32, (1, 128), 1)
    return jnp.where(lane // HEAD_DIM == h, 1.0, 0.0).astype(kind)


def attend(meta, part, qkv, seg_column, seg_row):
    def kernel(m, q_ref, k_ref, v_ref, column_ref, row_ref, out_ref, lse_ref):
        queries, keys, values = q_ref[0] * jnp.asarray(0.125, BF), k_ref[0], v_ref[0]
        allowed = column_ref[...] == row_ref[...]
        mixed = jnp.zeros((128, 1024), F32)
        for h in range(2):
            lanes = head_lanes(h, BF)
            scores = jnp.where(allowed, dot(keys * lanes, queries, NT), -1e30)
            largest = jnp.max(scores, axis=0, keepdims=True)
            exponent = jnp.exp(scores - largest)
            total = jnp.sum(exponent, axis=0, keepdims=True)
            mixed += dot(values * lanes, exponent.astype(BF), TN) / total
            lse_ref[0, h : h + 1, :] = largest + jnp.log(total)
        out_ref[...] = jnp.transpose(mixed).astype(BF)

    base = part * 2
    third = lambda t: spec((1, 1024, 128), lambda i, m: (t, 0, base + i))
    return kernel_call(
        kernel,
        meta,
        (qkv, qkv, qkv, seg_column, seg_row),
        [third(0), third(1), third(2), whole((1024, 1)), whole((1, 1024))],
        [spec((1024, 128), lambda i, m: (0, i)), spec((1, 8, 1024), lambda i, m: (i, 0, 0))],
        [shaped((1024, 256), BF), shaped((2, 8, 1024), F32)],
        grid=(2,),
        flops=8 * 4 * 1024 * 1024 * 256,
        moved=5 << 20,
        exps=8 << 20,
    )


def attend_back(meta, part, qkv, out, grad, lse, seg_column, seg_row):
    def kernel(m, q_ref, k_ref, v_ref, out_ref, grad_ref, lse_ref, column_ref, row_ref, d_ref, sum_ref, prob, ds):
        queries, upstream = q_ref[0], grad_ref[...]
        product = out_ref[...].astype(F32) * upstream.astype(F32)
        row = lax.broadcasted_iota(jnp.int32, (8, 128), 0)
        lane = lax.broadcasted_iota(jnp.int32, (8, 128), 1)
        picked = jnp.where(lane // HEAD_DIM == row, 1.0, 0.0).astype(F32)
        center = lax.dot_general(picked, product, NT, precision=lax.Precision.HIGHEST, preferred_element_type=F32)
        dq, dk, dv = (jnp.zeros((1024, 128), F32) for _ in range(3))
        for h in range(2):
            lanes = head_lanes(h, BF)
            for block in range(4):
                rows = pl.ds(block * 256, 256)
                allowed = column_ref[rows, :] == row_ref[...]
                scores = dot(k_ref[0, rows, :] * lanes * jnp.asarray(0.125, BF), queries, NT)
                p = jnp.where(allowed, jnp.exp(scores - lse_ref[0, h : h + 1, :]), 0.0)
                dp = dot(v_ref[0, rows, :] * lanes, upstream, NT)
                prob[rows, :] = p.astype(BF)
                ds[rows, :] = (p * (dp - center[h : h + 1, :])).astype(BF)
            dv += dot(prob[...], upstream * lanes)
            dk += dot(ds[...], queries * lanes)
            dq += dot(ds[...], k_ref[0] * lanes, TN)
        dq, dk, dv = (dq * 0.125).astype(BF), (dk * 0.125).astype(BF), dv.astype(BF)
        d_ref[0], d_ref[1], d_ref[2] = dq, dk, dv
        sum_ref[0:1, :] = jnp.sum(dq.astype(F32), axis=0, keepdims=True)
        sum_ref[1:2, :] = jnp.sum(dv.astype(F32), axis=0, keepdims=True)

    base = part * 2
    third = lambda t: spec((1, 1024, 128), lambda i, m: (t, 0, base + i))
    heads = lambda first: spec((1024, 128), lambda i, m: (0, first + i))
    return kernel_call(
        kernel,
        meta,
        (qkv, qkv, qkv, out, grad, lse, seg_column, seg_row),
        [third(0), third(1), third(2), heads(0), heads(base), spec((1, 8, 1024), lambda i, m: (i, 0, 0)), whole((1024, 1)), whole((1, 1024))],
        [spec((3, 1024, 128), lambda i, m: (0, 0, i)), spec((8, 128), lambda i, m: (0, i))],
        [shaped((3, 1024, 256), BF), shaped((8, 256), F32)],
        [pltpu.VMEM((1024, 1024), BF), pltpu.VMEM((1024, 1024), BF)],
        grid=(2,),
        flops=8 * 10 * 1024 * 1024 * 256,
        moved=8 << 20,
        exps=8 << 20,
    )


def project_out(meta, mixed, pieces):
    def kernel(m, x_ref, w_ref, *rest):
        refs, (send_ref, own_ref, weight, sem) = rest[:4], rest[4:]
        i = pl.program_id(0)

        @pl.when(i == 0)
        def _():
            load_all(load_out(m, refs, weight, sem))

        for b in range(2):
            columns = pl.ds(b * 512, 512)
            result = dot(x_ref[...], weight[b, :256, :]) + dot(w_ref[...], weight[b, 256:, :])

            @pl.when(i < 2)
            def _():
                send_ref[:, columns] = result.astype(BF)

            @pl.when(i >= 2)
            def _():
                own_ref[:, columns] = result

    return kernel_call(
        kernel,
        meta,
        (*mixed, *pieces),
        [spec((256, 256), lambda i, m: (turned(i), 0))] * 2 + [HBM] * 4,
        [spec((256, 1024), lambda i, m: (low_block(i), 0)), spec((256, 1024), lambda i, m: (high_block(i), 0))],
        [shaped((512, 1024), BF), shaped((512, 1024), F32)],
        [pltpu.VMEM((2, 512, 512), BF), pltpu.SemaphoreType.DMA((32,))],
        flops=2 * 1024 * 1024 * 512,
        moved=6 << 20,
    )


def normal_parts(values):
    center = values - jnp.mean(values, axis=-1, keepdims=True)
    inverse = lax.rsqrt(jnp.mean(center * center, axis=-1, keepdims=True) + EPSILON)
    return center * inverse, inverse


def normal_back(upstream, normal_part, inverse, gain):
    scaled = upstream * gain
    return inverse * (
        scaled
        - jnp.mean(scaled, axis=-1, keepdims=True)
        - normal_part * jnp.mean(scaled * normal_part, axis=-1, keepdims=True)
    )


BY_ROWS = lambda i, m: (i, 0)


def first_norm(meta, tokens, embedded, own, received, vectors):
    def kernel(m, tok_ref, emb_ref, own_ref, recv_ref, vec_ref, normal_ref, inverse_ref, low_ref):
        hidden = tok_ref[0].astype(F32) + emb_ref[...]
        attended = own_ref[...] + recv_ref[...].astype(F32) + vec_ref[0:1, :]
        normal_part, inverse = normal_parts(hidden + attended)
        normal_ref[...] = normal_part
        inverse_ref[...] = jnp.broadcast_to(inverse, (256, 128))
        low_ref[...] = (normal_part * vec_ref[1:2, :] + vec_ref[2:3, :]).astype(BF)

    block = spec((256, 1024), BY_ROWS)
    return kernel_call(
        kernel,
        meta,
        (tokens, embedded, own, received, vectors),
        [spec((1, 256, 1024), lambda i, m: (i, 0, 0)), whole((1, 1024)), block, block, whole((8, 1024))],
        [block, spec((256, 128), BY_ROWS), block],
        [shaped((512, 1024), F32), shaped((512, 128), F32), shaped((512, 1024), BF)],
        grid=(2,),
        flops=512 * 1024 * 12,
        moved=8 << 20,
    )


def expand(meta, own, other, shift, pieces):
    def kernel(m, own_ref, other_ref, shift_ref, *rest):
        refs, (act_ref, slope_ref, weight, sem) = rest[:4], rest[4:]
        i = pl.program_id(0)

        @pl.when(i == 0)
        def _():
            load_all(load_split_rows(m, refs, 0, 4, weight, sem))

        x = jnp.where(i < 2, own_ref[...].astype(F32), other_ref[...].astype(F32)).astype(BF)
        for b in range(4):
            columns = pl.ds(b * 512, 512)
            u = dot(x, weight[b]) + shift_ref[:, columns]
            cumulative = 0.5 * (1.0 + lax.erf(u * INVERSE_ROOT_TWO))
            act_ref[:, columns] = (u * cumulative).astype(BF)
            density = jnp.exp(-0.5 * u * u) * INVERSE_ROOT_TWO_PI
            slope_ref[:, columns] = (cumulative + u * density).astype(BF)

    return kernel_call(
        kernel,
        meta,
        (own, other, shift, *pieces),
        [
            spec((256, 1024), lambda i, m: (low_block(i), 0)),
            spec((256, 1024), lambda i, m: (high_block(i), 0)),
            whole((1, 2048)),
        ]
        + [HBM] * 4,
        [spec((256, 2048), BY_ROWS), spec((256, 2048), BY_ROWS)],
        [shaped((1024, 2048), BF), shaped((1024, 2048), BF)],
        [pltpu.VMEM((4, 1024, 512), BF), pltpu.SemaphoreType.DMA((32,))],
        flops=2 * 1024 * 1024 * 2048,
        moved=14 << 20,
        exps=4 << 20,
    )


def contract(meta, activated, pieces):
    def kernel(m, x_ref, *rest):
        refs, (send_ref, own_ref, weight, sem) = rest[:4], rest[4:]
        i = pl.program_id(0)

        @pl.when(i == 0)
        def _():
            load_all(load_own_rows(m, refs, 0, 2, 128, weight, sem))

        for b in range(2):
            columns = pl.ds(b * 512, 512)
            result = dot(x_ref[...], weight[b])

            @pl.when(i < 2)
            def _():
                send_ref[:, columns] = result.astype(BF)

            @pl.when(i >= 2)
            def _():
                own_ref[:, columns] = result

    return kernel_call(
        kernel,
        meta,
        (activated, *pieces),
        [spec((256, 2048), lambda i, m: (turned(i), 0))] + [HBM] * 4,
        [spec((256, 1024), lambda i, m: (low_block(i), 0)), spec((256, 1024), lambda i, m: (high_block(i), 0))],
        [shaped((512, 1024), BF), shaped((512, 1024), F32)],
        [pltpu.VMEM((2, 2048, 512), BF), pltpu.SemaphoreType.DMA((16,))],
        flops=2 * 1024 * 1024 * 2048,
        moved=11 << 20,
    )


def row_sums(sum_ref, i, rows):
    @pl.when(i == 0)
    def _():
        sum_ref[...] = jnp.zeros_like(sum_ref)

    for n, value in enumerate(rows):
        sum_ref[n : n + 1, :] += jnp.sum(value, axis=0, keepdims=True)


def second_norm(meta, normal_one, own, received, cotangent, vectors):
    def kernel(m, normal_ref, own_ref, recv_ref, cot_ref, vec_ref, out_ref, resid_ref, low_ref, sum_ref):
        normed = normal_ref[...] * vec_ref[1:2, :] + vec_ref[2:3, :]
        downward = own_ref[...] + recv_ref[...].astype(F32) + vec_ref[3:4, :]
        normal_part, inverse = normal_parts(normed + downward)
        out_ref[...] = (normal_part * vec_ref[4:5, :] + vec_ref[5:6, :]).astype(BF)
        upstream = cot_ref[...].astype(F32)
        resid = normal_back(upstream, normal_part, inverse, vec_ref[4:5, :])
        resid_ref[...] = resid
        low = resid.astype(BF)
        low_ref[...] = low
        row_sums(sum_ref, pl.program_id(0), (upstream * normal_part, upstream, low.astype(F32)))

    block = spec((256, 1024), BY_ROWS)
    return kernel_call(
        kernel,
        meta,
        (normal_one, own, received, cotangent, vectors),
        [block, block, block, block, whole((8, 1024))],
        [block, block, block, whole((8, 1024))],
        [shaped((512, 1024), BF), shaped((512, 1024), F32), shaped((512, 1024), BF), shaped((8, 1024), F32)],
        grid=(2,),
        flops=512 * 1024 * 30,
        moved=10 << 20,
    )


def feed_back(meta, own, other, slope, down_pieces, up_pieces):
    def kernel(m, own_ref, other_ref, slope_ref, *rest):
        down_refs, up_refs = rest[:4], rest[4:8]
        du_ref, send_ref, mine_ref, sum_ref, down, up, down_sem, up_sem = rest[8:]
        i = pl.program_id(0)

        @pl.when(i == 0)
        def _():
            load_all(
                load_own_rows(m, down_refs, 0, 2, 128, down, down_sem)
                + load_split_rows(m, up_refs, 0, 4, up, up_sem)
            )
            sum_ref[...] = jnp.zeros_like(sum_ref)

        df = jnp.where(i < 2, other_ref[...].astype(F32), own_ref[...].astype(F32)).astype(BF)
        total = jnp.zeros((256, 1024), F32)
        for b in range(4):
            rows = pl.ds(b * 512, 512)
            act = dot(df[:, :512], down[0, rows, :], NT) + dot(df[:, 512:], down[1, rows, :], NT)
            du = (act * slope_ref[:, rows].astype(F32)).astype(BF)
            du_ref[:, rows] = du
            sum_ref[0:1, rows] += jnp.sum(du.astype(F32), axis=0, keepdims=True)
            total += dot(du, up[b], NT)

        @pl.when(i < 2)
        def _():
            send_ref[...] = total.astype(BF)

        @pl.when(i >= 2)
        def _():
            mine_ref[...] = total

    return kernel_call(
        kernel,
        meta,
        (own, other, slope, *down_pieces, *up_pieces),
        [
            spec((256, 1024), lambda i, m: (high_block(i), 0)),
            spec((256, 1024), lambda i, m: (low_block(i), 0)),
            spec((256, 2048), lambda i, m: (turned(i), 0)),
        ]
        + [HBM] * 8,
        [
            spec((256, 2048), lambda i, m: (turned(i), 0)),
            spec((256, 1024), lambda i, m: (low_block(i), 0)),
            spec((256, 1024), lambda i, m: (high_block(i), 0)),
            whole((8, 2048)),
        ],
        [shaped((1024, 2048), BF), shaped((512, 1024), BF), shaped((512, 1024), F32), shaped((8, 2048), F32)],
        [
            pltpu.VMEM((2, 2048, 512), BF),
            pltpu.VMEM((4, 1024, 512), BF),
            pltpu.SemaphoreType.DMA((16,)),
            pltpu.SemaphoreType.DMA((32,)),
        ],
        flops=4 * 1024 * 1024 * 2048,
        moved=22 << 20,
    )


def first_norm_back(meta, resid, own, received, normal_one, inverse_one, vectors):
    def kernel(m, resid_ref, own_ref, recv_ref, normal_ref, inverse_ref, vec_ref, out_ref, low_ref, sum_ref):
        upstream = resid_ref[...] + own_ref[...] + recv_ref[...].astype(F32)
        normal_part = normal_ref[...]
        resid_one = normal_back(upstream, normal_part, inverse_ref[:, 0:1], vec_ref[1:2, :])
        out_ref[...] = resid_one
        low = resid_one.astype(BF)
        low_ref[...] = low
        row_sums(sum_ref, pl.program_id(0), (upstream * normal_part, upstream, low.astype(F32)))

    block = spec((256, 1024), BY_ROWS)
    return kernel_call(
        kernel,
        meta,
        (resid, own, received, normal_one, inverse_one, vectors),
        [block, block, block, block, spec((256, 128), BY_ROWS), whole((8, 1024))],
        [block, block, whole((8, 1024))],
        [shaped((512, 1024), F32), shaped((512, 1024), BF), shaped((8, 1024), F32)],
        grid=(2,),
        flops=512 * 1024 * 20,
        moved=10 << 20,
    )


def output_back(meta, own, other, pieces):
    def kernel(m, own_ref, other_ref, *rest):
        refs, (out_ref, weight, sem) = rest[:4], rest[4:]
        i = pl.program_id(0)

        @pl.when(i == 0)
        def _():
            load_all(load_out(m, refs, weight, sem))

        da = jnp.where(i < 2, own_ref[...].astype(F32), other_ref[...].astype(F32)).astype(BF)
        out_ref[...] = (dot(da[:, :512], weight[0], NT) + dot(da[:, 512:], weight[1], NT)).astype(BF)

    return kernel_call(
        kernel,
        meta,
        (own, other, *pieces),
        [
            spec((256, 1024), lambda i, m: (low_block(i), 0)),
            spec((256, 1024), lambda i, m: (high_block(i), 0)),
        ]
        + [HBM] * 4,
        spec((256, 512), BY_ROWS),
        shaped((1024, 512), BF),
        [pltpu.VMEM((2, 512, 512), BF), pltpu.SemaphoreType.DMA((32,))],
        flops=2 * 1024 * 1024 * 512,
        moved=4 << 20,
    )


def rel_chip(s, m):
    return (m[0] ^ (s // 2)) * 2 + (m[1] ^ lax.rem(s, 2))


def piece_outputs(blocks, rows, columns=512):
    shape = (2, 2, blocks, rows, columns)
    return [HBM] * 4, [shaped(shape, BF)] * 4


def push(s, outs, copy_for):
    first_keep, first_send, second_keep, second_send = outs
    slots = (
        ((first_keep, 0), (second_keep, 0)),
        ((first_keep, 1), (second_send, 0)),
        ((first_send, 0), (second_keep, 1)),
        ((first_send, 1), (second_send, 1)),
    )
    for n, (first, second) in enumerate(slots):

        @pl.when(s == n)
        def _(n=n, first=first, second=second):
            for k in range(4):
                ref, at = (first, second)[k // 2]
                for copy in copy_for(n, k, ref.at[at, k % 2]):
                    copy.start()

    @pl.when(s == 3)
    def _():
        for n, (first, second) in enumerate(slots):
            for k in range(4):
                ref, at = (first, second)[k // 2]
                for copy in copy_for(n, k, ref.at[at, k % 2]):
                    copy.wait()


def weigh_down(meta, activated, own, other):
    def kernel(m, x_ref, own_ref, other_ref, *rest):
        outs, (stage, sem) = rest[:4], rest[4:]
        s = pl.program_id(0)
        x = x_ref[...]
        for b in range(2):
            columns = pl.ds(b * 512, 512)
            stage[s, b] = (dot(x[:512], own_ref[:, columns], TN) + dot(x[512:], other_ref[:, columns], TN)).astype(BF)

        def copy_for(n, k, target):
            row = pl.multiple_of((m[3] ^ z_relative(k // 2, k % 2)) * 128, 128)
            return [pltpu.make_async_copy(stage.at[n, :, pl.ds(row, 128), :], target, sem.at[n * 4 + k])]

        push(s, outs, copy_for)

    out_specs, out_shape = piece_outputs(2, 128)
    return kernel_call(
        kernel,
        meta,
        (activated, own, other),
        [spec((1024, 512), lambda s, m: (0, rel_chip(s, m))), whole((512, 1024)), whole((512, 1024))],
        out_specs,
        out_shape,
        [pltpu.VMEM((4, 2, 512, 512), BF), pltpu.SemaphoreType.DMA((16,))],
        flops=2 * 1024 * 1024 * 2048,
        moved=10 << 20,
    )


def weigh_up(meta, normed_own, normed_other, du):
    def kernel(m, own_ref, other_ref, du_ref, *rest):
        outs, (up, sem) = rest[:4], rest[4:]
        s = pl.program_id(0)
        for b in range(4):
            columns = pl.ds(b * 512, 512)
            up[s, b] = (dot(own_ref[...], du_ref[:512, columns], TN) + dot(other_ref[...], du_ref[512:, columns], TN)).astype(BF)

        def copy_for(n, k, target):
            z = m[3] ^ z_relative(k // 2, k % 2)
            copies = []
            for rel in range(2):
                row = pl.multiple_of((m[2] ^ rel) * 128 + z * 32, 32)
                copies.append(
                    pltpu.make_async_copy(
                        up.at[n, :, pl.ds(row, 32), :],
                        target.at[pl.ds(rel * 4, 4)],
                        sem.at[(n * 4 + k) * 2 + rel],
                    )
                )
            return copies

        push(s, outs, copy_for)

    out_specs, out_shape = piece_outputs(8, 32)
    return kernel_call(
        kernel,
        meta,
        (normed_own, normed_other, du),
        [
            spec((512, 256), lambda s, m: (0, rel_chip(s, m))),
            spec((512, 256), lambda s, m: (0, rel_chip(s, m))),
            whole((1024, 2048)),
        ],
        out_specs,
        out_shape,
        [pltpu.VMEM((4, 4, 256, 512), BF), pltpu.SemaphoreType.DMA((32,))],
        flops=2 * 1024 * 1024 * 2048,
        moved=15 << 20,
    )


def weigh_qkv(meta, hidden, dqkv, out_terms=()):
    def kernel(m, x_ref, d_ref, *rest):
        s = pl.program_id(0)
        if out_terms:
            mixed_ref, more_ref, own_ref, other_ref = rest[:4]
            rest = rest[4:]
        outs, stage, sem = rest[:4], rest[4], rest[5]
        for t in range(3):
            stage[s, t] = dot(x_ref[...], d_ref[t], TN).astype(BF)
        if out_terms:
            stage_out, sem_out = rest[6:]
            x = jnp.where(rel_chip(s, m) < 2, mixed_ref[...].astype(F32), more_ref[...].astype(F32)).astype(BF)
            for b in range(4):
                columns = pl.ds(b * 256, 256)
                stage_out[s, b] = (
                    dot(x[:512], own_ref[:, columns], TN) + dot(x[512:], other_ref[:, columns], TN)
                ).astype(BF)

        def copy_for(n, k, target):
            z = m[3] ^ z_relative(k // 2, k % 2)
            copies = []
            for rel in range(2):
                row = pl.multiple_of((m[2] ^ rel) * 128 + z * 32, 32)
                copies.append(
                    pltpu.make_async_copy(
                        stage.at[n, :, pl.ds(row, 32), :],
                        target.at[pl.ds(rel * 3, 3)],
                        sem.at[(n * 4 + k) * 2 + rel],
                    )
                )
            if out_terms:
                copies.append(
                    pltpu.make_async_copy(
                        stage_out.at[n, :, pl.ds(pl.multiple_of(z * 32, 32), 32), :],
                        target.at[pl.ds(6, 4)],
                        sem_out.at[n * 4 + k],
                    )
                )
            return copies

        push(s, outs, copy_for)

    out_specs, out_shape = piece_outputs(10 if out_terms else 6, 32, 256)
    in_specs = [spec((1024, 256), lambda s, m: (0, rel_chip(s, m))), whole((3, 1024, 256))]
    scratch = [pltpu.VMEM((4, 3, 256, 256), BF), pltpu.SemaphoreType.DMA((32,))]
    if out_terms:
        in_specs += [spec((1024, 128), lambda s, m: (0, rel_chip(s, m) % 2))] * 2 + [whole((512, 1024))] * 2
        scratch += [pltpu.VMEM((4, 4, 128, 256), BF), pltpu.SemaphoreType.DMA((16,))]
    return kernel_call(
        kernel,
        meta,
        (hidden, dqkv, *out_terms),
        in_specs,
        out_specs,
        out_shape,
        scratch,
        flops=2 * 1024 * 1024 * 1024,
        moved=8 << 20,
    )


def qkv_back(meta, dqkv, pieces):
    def kernel(m, d_ref, e_ref, *rest):
        refs, (send_ref, own_ref, weight, sem) = rest[:4], rest[4:]
        i = pl.program_id(0)

        @pl.when(i == 0)
        def _():
            load_all(load_qkv(m, refs, weight, sem))

        total = jnp.zeros((256, 1024), F32)
        for t in range(3):
            total += dot(d_ref[t], weight[t, :, :256], NT) + dot(e_ref[t], weight[t, :, 256:], NT)

        @pl.when(i < 2)
        def _():
            send_ref[...] = total.astype(BF)

        @pl.when(i >= 2)
        def _():
            own_ref[...] = total

    return kernel_call(
        kernel,
        meta,
        (*dqkv, *pieces),
        [spec((3, 256, 256), lambda i, m: (0, turned(i), 0))] * 2 + [HBM] * 4,
        [spec((256, 1024), lambda i, m: (low_block(i), 0)), spec((256, 1024), lambda i, m: (high_block(i), 0))],
        [shaped((512, 1024), BF), shaped((512, 1024), F32)],
        [pltpu.VMEM((3, 1024, 512), BF), pltpu.SemaphoreType.DMA((96,))],
        flops=2 * 1024 * 1024 * 1536,
        moved=9 << 20,
    )


def last_sum(meta, resid, own, received):
    def kernel(m, resid_ref, own_ref, recv_ref, out_ref, sum_ref):
        total = resid_ref[...] + own_ref[...] + recv_ref[...].astype(F32)
        out_ref[...] = total.astype(BF)
        row_sums(sum_ref, pl.program_id(0), (total,))

    block = spec((256, 1024), BY_ROWS)
    return kernel_call(
        kernel,
        meta,
        (resid, own, received),
        [block, block, block],
        [block, whole((8, 1024))],
        [shaped((512, 1024), BF), shaped((8, 1024), F32)],
        grid=(2,),
        flops=512 * 1024 * 4,
        moved=6 << 20,
    )


VECTOR_SIZES = (64, 32, 32, 32, 128, 32, 32, 32)


def split_vectors(packed):
    parts, start = [], 0
    for size in VECTOR_SIZES:
        parts.append(packed[:, start : start + size])
        start += size
    return parts


def chip_body(
    tokens,
    timestep,
    segment_ids,
    cotangent,
    time_weight,
    qkv_weight,
    qv_bias,
    out_weight,
    out_bias,
    norm_gain,
    norm_bias,
    up_weight,
    up_bias,
    down_weight,
    down_bias,
    final_gain,
    final_bias,
):
    dp, z = lax.axis_index("dp"), lax.axis_index("sp")
    y, x, c = dp // 4, (dp // 2) % 2, dp % 2
    meta = jnp.stack([y, x, c, z]).astype(jnp.int32)
    pick = lambda value, index, axis: lax.dynamic_index_in_dim(value, index, axis, keepdims=False)

    me = dp * 4 + z

    qkv_split = qkv_weight.reshape(32, 3, 4, 2, 128)
    up_split = up_weight.reshape(32, 4, 2, 512)
    qkv_half = lambda core: pick(qkv_split, core, 3).reshape(32, 3, 512).transpose(1, 0, 2).reshape(96, 512)
    up_half = lambda core: pick(up_split, core, 2).transpose(1, 0, 2)
    small = jnp.concatenate([qv_bias, out_bias, norm_gain, norm_bias, up_bias, down_bias, final_gain, final_bias])
    small = jnp.pad(small[None], ((0, 15), (0, 128)))
    received = send(jnp.concatenate([qkv_half(1 - c), small]), PAIR)
    small = jnp.concatenate([small[:1], received[96:97], small[2:]])
    out_shard = out_weight.reshape(32, 2, 512).transpose(1, 0, 2).reshape(64, 512)
    qkv_shard = jnp.concatenate([qkv_half(c), received[:96], out_shard, small])
    up_shard = jnp.concatenate([up_half(c), send(up_half(1 - c), PAIR)])
    down_shard = down_weight.reshape(128, 2, 512).transpose(1, 0, 2)
    qkv_line = gather_line(qkv_shard)

    stamps = after(timestep.astype(jnp.int32), received)[:, None]
    stamps = jnp.concatenate([stamps // 64, stamps % 64], axis=1).astype(BF)
    for pairs in (PAIR, ALONG_X, ALONG_Y):
        stamps = jnp.concatenate([stamps, send(stamps, pairs)])
    stamps = stamps.astype(F32)
    stamps = (stamps[:, 0] * 64.0 + stamps[:, 1]).reshape(4, 4)
    sums_order = jnp.arange(4, dtype=jnp.int32) ^ z
    from_pair = (sums_order // 2) ^ c
    stamps = jnp.take_along_axis(stamps, jnp.broadcast_to(from_pair * 2 + sums_order % 2, (4, 4)), axis=1).reshape(16, 1)
    column = me * 32 + jnp.arange(32, dtype=jnp.int32)
    frequency = jnp.exp(-math.log(10000.0) * (column % 512).astype(F32) / 512)
    phases = stamps * frequency[None, :]
    features = jnp.where(column[None, :] < 512, jnp.sin(phases), jnp.cos(phases)).astype(BF)
    features = after(features, qkv_line[0])
    embedded = jnp.dot(features, time_weight, preferred_element_type=F32)
    embedded = embedded + send(embedded, PAIR)
    for width, pairs in ((8, ALONG_Y), (4, ALONG_X), (2, ALONG_Z[2]), (1, ALONG_Z[1])):
        embedded = embedded[:width] + send(embedded[width:], pairs)

    qkv_pieces = gather_plane(*qkv_line)

    def take_rows(value, *earlier):
        return jnp.stack(after([send(pick(value, (z + k) % 2, 0), ROW_OUT[k]) for k in range(2)], earlier))

    def give_rows(value):
        parts = [send(value[k * 256 : (k + 1) * 256], ROW_BACK[k]) for k in range(2)]
        swapped = (z % 2) == 1
        return jnp.stack([jnp.where(swapped, parts[1], parts[0]), jnp.where(swapped, parts[0], parts[1])])

    documents = jnp.concatenate([segment_ids // 32, segment_ids % 32], axis=1).astype(BF)
    documents = jnp.pad(documents[:, None, :], ((0, 0), (0, 15), (0, 512)))
    own_tokens = take_rows(after(jnp.concatenate([tokens, documents], axis=1), qkv_line))
    other_tokens = send(own_tokens, PAIR)
    codes = jnp.concatenate([own_tokens[:, 256], other_tokens[:, 256]]).astype(F32)
    segments = (codes[:, :256] * 32.0 + codes[:, 256:512]).reshape(1024)
    seg_column, seg_row = segments[:, None], segments[None, :]

    up_far = send(after(up_shard, own_tokens), ALONG_Z[2])

    natural = jnp.arange(32, dtype=jnp.int32)
    order = (natural[:, None] ^ me) == natural[None, :]
    small = jnp.stack([piece[:, :, 256:258, :384] for piece in qkv_pieces])
    small = jnp.stack(
        [
            small[half * 2 + (x_rel if half else y_rel), y_rel if half else x_rel, j, rel]
            for y_rel in range(2)
            for x_rel in range(2)
            for rel in range(2)
            for j in range(2)
            for half in range(2)
        ]
    )
    small = jnp.dot(order.astype(BF), small, preferred_element_type=F32)
    full = [part.reshape(1, -1) for part in split_vectors(small)]
    qv_full, out_shift, first_gain, first_shift, up_full, down_shift, second_gain, second_shift = full
    blank = jnp.zeros((2, 1024), F32)
    vectors = jnp.concatenate([out_shift, first_gain, first_shift, down_shift, second_gain, second_shift, blank])
    qv_mine = pick(qv_full.reshape(2, 4, 2, 128), c, 2).reshape(2, 512)
    qkv_shift = jnp.stack([qv_mine[0], jnp.zeros((512,), F32), qv_mine[1]])
    up_shift = pick(up_full.reshape(4, 2, 512), c, 1).reshape(1, 2048)

    hidden, qkv = project_qkv(meta, own_tokens, other_tokens, embedded, qkv_shift, qkv_pieces)
    up_first = jnp.stack([after(up_shard, qkv), up_far])
    mixed_one, lse_one = attend(meta, 0, after(qkv, up_first), seg_column, seg_row)
    up_second = after(send(up_first, ALONG_Z[1]), mixed_one)
    mixed_two, lse_two = attend(meta, 1, after(qkv, up_second), seg_column, seg_row)
    up_pieces = gather_plane(up_first, up_second, mixed_two)
    down_first = jnp.stack([after(down_shard, mixed_two), send(after(down_shard, up_second), ALONG_Z[2])])
    mixed = mixed_one, after(mixed_two, down_first, up_pieces[0], up_pieces[2])
    away, mine = project_out(meta, mixed, qkv_pieces)
    down_second = after(send(down_first, ALONG_Z[1]), mine)
    normal_one, inverse_one, normed = first_norm(
        meta, own_tokens, embedded, after(mine, down_second, up_pieces), send(away, PAIR), vectors
    )
    normed_other = send(normed, PAIR)
    down_pieces = gather_plane(down_first, down_second, normed)
    normed_other = after(normed_other, down_pieces[0], down_pieces[2])
    activated, slope = expand(meta, normed, normed_other, up_shift, up_pieces)
    own_cotangent = take_rows(after(cotangent, normed), activated).reshape(512, 1024)
    away, mine = contract(meta, after(activated, own_cotangent), down_pieces)
    result, resid_two, df, sums_two = second_norm(meta, normal_one, mine, send(away, PAIR), own_cotangent, vectors)

    df_other = send(df, PAIR)
    down_terms = weigh_down(meta, activated, df, df_other)
    du, away, mine, up_sums = feed_back(meta, after(df, down_terms), df_other, slope, down_pieces, up_pieces)
    received = send(away, PAIR)
    up_terms = weigh_up(meta, normed, normed_other, du)
    down_sums = add_one(*scatter_one(*down_terms), up_terms)
    resid_one, da, sums_one = first_norm_back(
        meta, after(resid_two, down_sums), mine, received, normal_one, inverse_one, vectors
    )
    da_other = send(da, PAIR)
    dout = output_back(meta, da, da_other, qkv_pieces)
    down_sums = add_two(*scatter_two(*down_sums), dout)
    output = give_rows(after(result, dout))
    grad = after(dout, down_sums)
    dqkv_one, qv_sums_one = attend_back(meta, 0, qkv, mixed_one, grad, lse_one, seg_column, seg_row)
    output = after(output, dqkv_one)
    qkv_terms_one = weigh_qkv(meta, hidden, after(dqkv_one, output), (mixed_one, mixed_two, da, da_other))
    up_sums_one = add_one(*scatter_one(*after(up_terms, dout)), qkv_terms_one)
    down_sums = add_three(*scatter_three(*down_sums), qkv_terms_one)
    grad = after(dout, up_sums_one, down_sums)
    dqkv_two, qv_sums_two = attend_back(meta, 1, qkv, mixed_two, grad, lse_two, seg_column, seg_row)
    up_sums_two = add_two(*scatter_two(*up_sums_one), dqkv_two)
    down_share = scatter_four(*down_sums, dqkv_two)
    away, mine = qkv_back(meta, (dqkv_one, after(dqkv_two, up_sums_two, down_share)), qkv_pieces)
    received = send(away, PAIR)
    qkv_terms_two = weigh_qkv(meta, hidden, after(dqkv_two, mine))
    qkv_sums_one = add_one(*scatter_one(*qkv_terms_one), mine)
    input_low, embed_sums = last_sum(meta, resid_one, after(mine, qkv_terms_two), received)
    input_grad = give_rows(input_low)
    up_sums_three = add_three(*scatter_three(*up_sums_two), qkv_terms_two)
    qkv_sums_one = add_two(*scatter_two(*qkv_sums_one), input_low)
    qkv_sums_two = add_one(*scatter_one(*qkv_terms_two), input_low)
    qkv_sums_two = add_two(*scatter_two(*qkv_sums_two))
    qkv_sums_one = add_three(*scatter_three(*qkv_sums_one))
    up_share = scatter_four(*up_sums_three, input_low)
    qkv_sums_two = add_three(*scatter_three(*qkv_sums_two))
    qkv_share_one = scatter_four(*after(qkv_sums_one, input_grad))
    qkv_share_two = scatter_four(*after(qkv_sums_two, input_grad))
    qkv_share = jnp.concatenate([qkv_share_one[:6], qkv_share_two], axis=2)
    qv_sums = jnp.concatenate([qv_sums_one[0:2], qv_sums_two[0:2]], axis=1)

    def both_halves(own, received):
        return jnp.where(c == 0, jnp.stack([own, received], axis=-2), jnp.stack([received, own], axis=-2))

    grad_down = down_share.transpose(1, 0, 2).reshape(128, 1024)
    grad_out = qkv_share_one[6:].transpose(1, 0, 2).reshape(32, 1024)
    grad_up = both_halves(up_share[:4], send(up_share[4:], PAIR))
    grad_up = grad_up.transpose(1, 0, 2, 3).reshape(32, 4096)
    split = lambda share: share.reshape(3, 32, 4, 128)
    grad_qkv = both_halves(split(qkv_share[:3]), split(send(qkv_share[3:], PAIR)))
    grad_qkv = grad_qkv.transpose(1, 0, 2, 3, 4).reshape(32, 3072)

    qv_sums, up_sums, sums_one, sums_two = after((qv_sums, up_sums, sums_one, sums_two), input_low)
    core_lane = (jnp.arange(2) == c).astype(F32)
    spread = lambda sums, width: (sums.reshape(-1, 1, width) * core_lane[None, :, None]).reshape(32, -1)
    grads = jnp.concatenate(
        [
            spread(qv_sums, 128),
            sums_one[2].reshape(32, 32),
            sums_one[0].reshape(32, 32),
            sums_one[1].reshape(32, 32),
            spread(up_sums[0:1], 512),
            sums_two[2].reshape(32, 32),
            sums_two[0].reshape(32, 32),
            sums_two[1].reshape(32, 32),
        ],
        axis=1,
    )
    total = jnp.dot(order.astype(F32), grads, precision=lax.Precision.HIGHEST)
    total = total.reshape(4, 2, 4, 3, 128).transpose(1, 0, 2, 3, 4).reshape(96, 128)
    sums = embed_sums[0:1].reshape(8, 128)
    received = send(jnp.concatenate([total[48:], sums]), PAIR)
    total, sums = total[:48] + received[:48], sums + received[48:]
    for width, pairs in ((24, ALONG_Y), (12, ALONG_X), (6, ALONG_Z[2]), (3, ALONG_Z[1])):
        message = jnp.concatenate([total[width:], sums])
        received = send(after(message, input_grad) if width == 6 else message, pairs)
        total, sums = total[:width] + received[:width], jnp.concatenate([sums, received[width:]])
    small_grads = [part.reshape(-1) for part in split_vectors(total.reshape(1, 384))]
    sums = sums.reshape(2, 2, 2, 2, 1024).transpose(3, 2, 1, 0, 4).reshape(16, 1024)
    grad_time = jnp.dot(features.astype(F32).T, sums, precision=lax.Precision.HIGHEST)

    return (
        output,
        input_grad,
        grad_time,
        grad_qkv,
        small_grads[0],
        grad_out,
        *small_grads[1:4],
        grad_up,
        small_grads[4],
        grad_down,
        *small_grads[5:],
    )


def solution(mesh):
    in_specs = (
        P("dp", "sp", None),
        P("dp"),
        P("dp", "sp"),
        P("dp", "sp", None),
        P(("dp", "sp"), None),
        P(("dp", "sp"), None),
        P(("dp", "sp")),
        P(("dp", "sp"), None),
        P(("dp", "sp")),
        P(("dp", "sp")),
        P(("dp", "sp")),
        P(("dp", "sp"), None),
        P(("dp", "sp")),
        P(("dp", "sp"), None),
        P(("dp", "sp")),
        P(("dp", "sp")),
        P(("dp", "sp")),
    )
    out_specs = (
        P("dp", "sp", None),
        P("dp", "sp", None),
        P(("dp", "sp"), None),
        P(("dp", "sp"), None),
        P(("dp", "sp")),
        P(("dp", "sp"), None),
        P(("dp", "sp")),
        P(("dp", "sp")),
        P(("dp", "sp")),
        P(("dp", "sp"), None),
        P(("dp", "sp")),
        P(("dp", "sp"), None),
        P(("dp", "sp")),
        P(("dp", "sp")),
        P(("dp", "sp")),
    )
    plan = chip_body if dict(mesh.shape) == {"dp": 8, "sp": 4} else body
    return jax.shard_map(plan, mesh=mesh, in_specs=in_specs, out_specs=out_specs, check_vma=False)
```

```python
import math

import jax
import jax.numpy as jnp
from jax import lax
from jax.experimental import pallas as pl
from jax.experimental.pallas import tpu as pltpu
from jax.sharding import PartitionSpec as P

HEADS = 16
HEAD_DIM = 64


EPSILON = 1e-05
INVERSE_ROOT_TWO = 1.0 / math.sqrt(2.0)
INVERSE_ROOT_TWO_PI = 1.0 / math.sqrt(2.0 * math.pi)


def time_features(stamps, model_width):
    halfway = model_width // 2
    frequency = jnp.exp(-math.log(10000.0) * jnp.arange(halfway, dtype=jnp.float32) / halfway)
    phases = stamps.astype(jnp.float32)[:, None] * frequency[None, :]
    return jnp.concatenate([jnp.sin(phases), jnp.cos(phases)], axis=1)


def layer_norm_parts(values, gain, offset):
    center = values - jnp.mean(values, axis=-1, keepdims=True)
    variance = jnp.mean(center * center, axis=-1, keepdims=True)
    inverse = lax.rsqrt(variance + EPSILON)
    normal_part = center * inverse
    return (normal_part * gain + offset, normal_part, inverse)


def layer_norm_back(upstream, normal_part, inverse, gain):
    scaled = upstream * gain
    return inverse * (
        scaled
        - jnp.mean(scaled, axis=-1, keepdims=True)
        - normal_part * jnp.mean(scaled * normal_part, axis=-1, keepdims=True)
    )


def gelu_slope(values):
    cumulative = 0.5 * (1.0 + lax.erf(values * INVERSE_ROOT_TWO))
    density = jnp.exp(-0.5 * values * values) * INVERSE_ROOT_TWO_PI
    return cumulative + values * density


def contract_rows(left, right):
    return lax.dot_general(
        left, right, (((0,), (0,)), ((), ())), preferred_element_type=jnp.float32
    )


def times_transposed(left, right):
    return lax.dot_general(
        left, right, (((1,), (1,)), ((), ())), preferred_element_type=jnp.float32
    )


def flatten_grads(grads):
    return tuple((grad.reshape(-1, 128) if grad.ndim == 2 else grad for grad in grads))


def restore_grads(shares, templates):
    return tuple((share.reshape(template.shape) for share, template in zip(shares, templates)))


def attention_forward(queries, keys_all, values_all, seg_full, query_block, scale):
    block_count = queries.shape[1] // query_block

    def one_block(index):
        start = index * query_block
        query_part = lax.dynamic_slice_in_dim(queries, start, query_block, 1)
        seg_part = lax.dynamic_slice_in_dim(seg_full, start, query_block, 1)
        scores = (
            jnp.einsum("rqhd,rkhd->rhqk", query_part, keys_all, preferred_element_type=jnp.float32)
            * scale
        )
        allowed = seg_part[:, None, :, None] == seg_full[:, None, None, :]
        scores = jnp.where(allowed, scores, -1e30)
        largest = jnp.max(scores, axis=-1, keepdims=True)
        exponent = jnp.exp(scores - largest)
        totals = jnp.sum(exponent, axis=-1, keepdims=True)
        probability = exponent / totals
        log_total = largest[..., 0] + jnp.log(totals[..., 0])
        mixed = jnp.einsum(
            "rhqk,rkhd->rqhd",
            probability.astype(jnp.bfloat16),
            values_all,
            preferred_element_type=jnp.float32,
        )
        return (mixed, log_total)

    mixed_blocks, log_totals = lax.map(one_block, jnp.arange(block_count, dtype=jnp.int32))
    mixed = jnp.moveaxis(mixed_blocks, 0, 1).reshape(queries.shape)
    return (mixed, log_totals)


def attention_backward(
    queries, keys_all, values_all, seg_full, grad_heads, log_totals, query_block, scale
):
    block_count = queries.shape[1] // query_block

    def one_block(carry, index):
        key_grad, value_grad = carry
        start = index * query_block
        query_part = lax.dynamic_slice_in_dim(queries, start, query_block, 1)
        seg_part = lax.dynamic_slice_in_dim(seg_full, start, query_block, 1)
        grad_part = lax.dynamic_slice_in_dim(grad_heads, start, query_block, 1)
        scores = (
            jnp.einsum("rqhd,rkhd->rhqk", query_part, keys_all, preferred_element_type=jnp.float32)
            * scale
        )
        allowed = seg_part[:, None, :, None] == seg_full[:, None, None, :]
        scores = jnp.where(allowed, scores, -1e30)
        probability = jnp.exp(scores - log_totals[index][..., None])
        dotted = jnp.einsum(
            "rqhd,rkhd->rhqk", grad_part, values_all, preferred_element_type=jnp.float32
        )
        center = jnp.sum(probability * dotted, axis=-1, keepdims=True)
        score_grad = (probability * (dotted - center)).astype(jnp.bfloat16)
        query_grad = (
            jnp.einsum("rhqk,rkhd->rqhd", score_grad, keys_all, preferred_element_type=jnp.float32)
            * scale
        )
        key_grad = (
            key_grad
            + jnp.einsum(
                "rhqk,rqhd->rkhd", score_grad, query_part, preferred_element_type=jnp.float32
            )
            * scale
        )
        value_grad = value_grad + jnp.einsum(
            "rhqk,rqhd->rkhd",
            probability.astype(jnp.bfloat16),
            grad_part,
            preferred_element_type=jnp.float32,
        )
        return ((key_grad, value_grad), query_grad)

    starting = (jnp.zeros(keys_all.shape, jnp.float32), jnp.zeros(values_all.shape, jnp.float32))
    (key_grad, value_grad), query_blocks = lax.scan(
        one_block, starting, jnp.arange(block_count, dtype=jnp.int32)
    )
    query_grad = jnp.moveaxis(query_blocks, 0, 1).reshape(queries.shape)
    return (query_grad, key_grad, value_grad)


def body(
    tokens,
    timestep,
    segment_ids,
    cotangent,
    time_weight,
    qkv_weight,
    qv_bias,
    out_weight,
    out_bias,
    norm_gain,
    norm_bias,
    up_weight,
    up_bias,
    down_weight,
    down_bias,
    final_gain,
    final_bias,
):
    shards = (
        time_weight,
        qkv_weight,
        qv_bias,
        out_weight,
        out_bias,
        norm_gain,
        norm_bias,
        up_weight,
        up_bias,
        down_weight,
        down_bias,
        final_gain,
        final_bias,
    )
    sp_count = lax.axis_size("sp")
    micro_count = max(2, sp_count // 2)
    rows_local, piece_len, model_width = tokens.shape
    rows_micro = rows_local // micro_count
    seq_len = piece_len * sp_count
    width_local = model_width // sp_count
    heads_local = HEADS // sp_count
    query_block = min(512, seq_len)
    scale = 1.0 / math.sqrt(HEAD_DIM)
    tok_count = rows_micro * piece_len
    owned = tuple((jnp.zeros(piece.shape, jnp.float32) for piece in shards))
    output_parts = []
    input_parts = []
    for micro in range(micro_count):
        first_row = micro * rows_micro
        block_tokens = tokens[first_row : first_row + rows_micro]
        block_cotangent = cotangent[first_row : first_row + rows_micro]
        block_segments = segment_ids[first_row : first_row + rows_micro]
        block_stamps = timestep[first_row : first_row + rows_micro]
        gathered = (
            lax.all_gather(shards[0], ("dp", "sp"), axis=0, tiled=True),
            lax.all_gather(shards[1], ("dp", "sp"), axis=0, tiled=True),
            lax.all_gather(shards[2], ("dp", "sp"), axis=0, tiled=True),
            lax.all_gather(shards[3], ("dp", "sp"), axis=0, tiled=True),
            lax.all_gather(shards[4], ("dp", "sp"), axis=0, tiled=True),
            lax.all_gather(shards[5], ("dp", "sp"), axis=0, tiled=True),
            lax.all_gather(shards[6], ("dp", "sp"), axis=0, tiled=True),
            lax.all_gather(shards[7], ("dp", "sp"), axis=0, tiled=True),
            lax.all_gather(shards[8], ("dp", "sp"), axis=0, tiled=True),
            lax.all_gather(shards[9], ("dp", "sp"), axis=0, tiled=True),
            lax.all_gather(shards[10], ("dp", "sp"), axis=0, tiled=True),
            lax.all_gather(shards[11], ("dp", "sp"), axis=0, tiled=True),
            lax.all_gather(shards[12], ("dp", "sp"), axis=0, tiled=True),
        )
        (
            time_full,
            qkv_full,
            qv_full,
            out_full,
            out_shift,
            first_gain,
            first_shift,
            up_full,
            up_shift,
            down_full,
            down_shift,
            second_gain,
            second_shift,
        ) = gathered
        features = time_features(block_stamps, model_width).astype(jnp.bfloat16)
        embedded = jnp.dot(features, time_full, preferred_element_type=jnp.float32)
        hidden = block_tokens.astype(jnp.float32) + embedded[:, None, :]
        hidden_flat = hidden.reshape(tok_count, model_width)
        hidden_low = hidden_flat.astype(jnp.bfloat16)
        qv_float = qv_full.astype(jnp.float32)
        qkv_shift = jnp.concatenate(
            [qv_float[:model_width], jnp.zeros((model_width,), jnp.float32), qv_float[model_width:]]
        )
        packed = jnp.dot(hidden_low, qkv_full, preferred_element_type=jnp.float32) + qkv_shift
        packed = packed.astype(jnp.bfloat16).reshape(rows_micro, piece_len, 3, model_width)
        seg_copies = jnp.broadcast_to(
            block_segments[:, :, None, None], (rows_micro, piece_len, 1, sp_count)
        )
        packed_heads, seg_heads = (
            lax.all_to_all(packed, "sp", split_axis=3, concat_axis=1, tiled=True),
            lax.all_to_all(seg_copies, "sp", split_axis=3, concat_axis=1, tiled=True),
        )
        seg_full = seg_heads[:, :, 0, 0]
        head_shape = (rows_micro, seq_len, heads_local, HEAD_DIM)
        queries = packed_heads[:, :, 0].reshape(head_shape)
        keys_all = packed_heads[:, :, 1].reshape(head_shape)
        values_all = packed_heads[:, :, 2].reshape(head_shape)
        mixed, log_totals = attention_forward(
            queries, keys_all, values_all, seg_full, query_block, scale
        )
        mixed_low = mixed.astype(jnp.bfloat16).reshape(rows_micro, seq_len, width_local)
        mixed_local = lax.all_to_all(mixed_low, "sp", split_axis=1, concat_axis=2, tiled=True)
        mixed_flat = mixed_local.reshape(tok_count, model_width)
        attended = jnp.dot(
            mixed_flat, out_full, preferred_element_type=jnp.float32
        ) + out_shift.astype(jnp.float32)
        first_gain_f = first_gain.astype(jnp.float32)
        normed, normal_one, inverse_one = layer_norm_parts(
            hidden_flat + attended, first_gain_f, first_shift.astype(jnp.float32)
        )
        normed_low = normed.astype(jnp.bfloat16)
        upward = jnp.dot(normed_low, up_full, preferred_element_type=jnp.float32) + up_shift.astype(
            jnp.float32
        )
        activated = jax.nn.gelu(upward, approximate=False).astype(jnp.bfloat16)
        downward = jnp.dot(
            activated, down_full, preferred_element_type=jnp.float32
        ) + down_shift.astype(jnp.float32)
        second_gain_f = second_gain.astype(jnp.float32)
        result, normal_two, inverse_two = layer_norm_parts(
            normed + downward, second_gain_f, second_shift.astype(jnp.float32)
        )
        output_parts.append(result.astype(jnp.bfloat16).reshape(rows_micro, piece_len, model_width))
        upstream = block_cotangent.reshape(tok_count, model_width).astype(jnp.float32)
        grad_second_gain = jnp.sum(upstream * normal_two, axis=0)
        grad_second_shift = jnp.sum(upstream, axis=0)
        resid_two = layer_norm_back(upstream, normal_two, inverse_two, second_gain_f)
        down_grad = resid_two.astype(jnp.bfloat16)
        grad_down_shift = jnp.sum(down_grad, axis=0, dtype=jnp.float32)
        grad_down_full = contract_rows(activated, down_grad)
        act_grad = times_transposed(down_grad, down_full)
        up_grad = (act_grad * gelu_slope(upward)).astype(jnp.bfloat16)
        grad_up_shift = jnp.sum(up_grad, axis=0, dtype=jnp.float32)
        grad_up_full = contract_rows(normed_low, up_grad)
        normed_grad = resid_two + times_transposed(up_grad, up_full)
        grad_first_gain = jnp.sum(normed_grad * normal_one, axis=0)
        grad_first_shift = jnp.sum(normed_grad, axis=0)
        resid_one = layer_norm_back(normed_grad, normal_one, inverse_one, first_gain_f)
        attended_grad = resid_one.astype(jnp.bfloat16)
        grad_out_shift = jnp.sum(attended_grad, axis=0, dtype=jnp.float32)
        grad_out_full = contract_rows(mixed_flat, attended_grad)
        mixed_grad = times_transposed(attended_grad, out_full).astype(jnp.bfloat16)
        mixed_grad = mixed_grad.reshape(rows_micro, piece_len, model_width)
        grad_heads = lax.all_to_all(
            mixed_grad, "sp", split_axis=2, concat_axis=1, tiled=True
        ).reshape(head_shape)
        query_grad, key_grad, value_grad = attention_backward(
            queries, keys_all, values_all, seg_full, grad_heads, log_totals, query_block, scale
        )
        packed_grad = jnp.stack([query_grad, key_grad, value_grad], axis=2)
        packed_grad = packed_grad.reshape(rows_micro, seq_len, 3, width_local).astype(jnp.bfloat16)
        packed_local = lax.all_to_all(packed_grad, "sp", split_axis=1, concat_axis=3, tiled=True)
        packed_flat = packed_local.reshape(tok_count, 3 * model_width)
        third_sums = jnp.sum(packed_flat, axis=0, dtype=jnp.float32)
        grad_qv_full = jnp.concatenate([third_sums[:model_width], third_sums[2 * model_width :]])
        grad_qkv_full = contract_rows(hidden_low, packed_flat)
        hidden_grad = resid_one + times_transposed(packed_flat, qkv_full)
        input_parts.append(
            hidden_grad.astype(jnp.bfloat16).reshape(rows_micro, piece_len, model_width)
        )
        embed_grad = jnp.sum(hidden_grad.reshape(rows_micro, piece_len, model_width), axis=1)
        grad_time_full = jnp.dot(
            features.astype(jnp.float32).T, embed_grad, precision=lax.Precision.HIGHEST
        )
        grads = (
            grad_time_full,
            grad_qkv_full,
            grad_qv_full,
            grad_out_full,
            grad_out_shift,
            grad_first_gain,
            grad_first_shift,
            grad_up_full,
            grad_up_shift,
            grad_down_full,
            grad_down_shift,
            grad_second_gain,
            grad_second_shift,
        )
        shares = lax.psum_scatter(
            flatten_grads(grads), ("dp", "sp"), scatter_dimension=0, tiled=True
        )
        owned = jax.tree.map(jnp.add, owned, restore_grads(shares, owned))
    output = jnp.concatenate(output_parts, axis=0)
    input_grad = jnp.concatenate(input_parts, axis=0)
    return (
        output,
        input_grad,
        owned[0],
        owned[1],
        owned[2],
        owned[3],
        owned[4],
        owned[5],
        owned[6],
        owned[7],
        owned[8],
        owned[9],
        owned[10],
        owned[11],
        owned[12],
    )


AXES = ("dp", "sp")
BF = jnp.bfloat16
F32 = jnp.float32
NT = (((1,), (1,)), ((), ()))
TN = (((0,), (0,)), ((), ()))
NN = (((1,), (0,)), ((), ()))
VMEM_LIMIT = 58 * 1024 * 1024
CHIP_SLOTS = (
    ((0, 0, 0), (0, 0, 1)),
    ((0, 1, 0), (0, 1, 1)),
    ((1, 0, 0), (1, 1, 0)),
    ((1, 0, 1), (1, 1, 1)),
)


def dot(left, right, dims=NN):
    return lax.dot_general(left, right, dims, preferred_element_type=F32)


def device_perm(target):
    pairs = []
    for y in range(2):
        for x in range(2):
            for c in range(2):
                for z in range(4):
                    ty, tx, tc, tz = target(y, x, c, z)
                    source = ((y * 2 + x) * 2 + c) * 4 + z
                    pairs.append((source, ((ty * 2 + tx) * 2 + tc) * 4 + tz))
    return pairs


PAIR = device_perm(lambda y, x, c, z: (y, x, 1 - c, z))
ALONG_X = device_perm(lambda y, x, c, z: (y, 1 - x, c, z))
ALONG_Y = device_perm(lambda y, x, c, z: (1 - y, x, c, z))
ALONG_Z = [device_perm(lambda y, x, c, z, k=k: (y, x, c, z ^ k)) for k in range(3)]
ROW_OUT = [device_perm(lambda y, x, c, z, k=k: (y, x, z // 2, c * 2 + (z + k) % 2)) for k in range(2)]
ROW_BACK = [[(t, s) for s, t in pairs] for pairs in ROW_OUT]


def send(value, pairs):
    return lax.ppermute(value, AXES, pairs)


def after(value, *earlier):
    return lax.optimization_barrier((value, earlier))[0]


def gather_line(shard):
    first = jnp.stack([shard, send(shard, ALONG_Z[2])])
    return first, send(first, ALONG_Z[1])


def gather_plane(first, second, *earlier):
    first_x, second_y = lax.optimization_barrier((send(first, ALONG_X), send(second, ALONG_Y)))
    first, second = jnp.stack([after(first, earlier), first_x]), jnp.stack([after(second, earlier), second_y])
    return [first, send(first, ALONG_Y), second, send(second, ALONG_X)]


def add_low(a, b):
    return (a.astype(F32) + b.astype(F32)).astype(BF)


def scatter_one(first_keep, first_send, second_keep, second_send):
    return first_keep, send(first_send, ALONG_Y), second_keep, send(second_send, ALONG_X)


def add_one(first_keep, from_y, second_keep, from_x, *earlier):
    first_keep, second_keep = after((first_keep, second_keep), earlier)
    to_x, to_y = add_low(first_keep[1], from_y[1]), add_low(second_keep[1], from_x[1])
    return add_low(first_keep[0], from_y[0]), to_x, add_low(second_keep[0], from_x[0]), to_y


def scatter_two(first, to_x, second, to_y):
    return first, send(to_x, ALONG_X), second, send(to_y, ALONG_Y)


def add_two(first, from_x, second, from_y, *earlier):
    first, second = after((first, second), earlier)
    return add_low(first, from_x), add_low(second, from_y)


def scatter_three(first, second):
    return first, send(second, ALONG_Z[1])


def add_three(first, received, *earlier):
    first = after(first, earlier)
    return add_low(first[0], received[0]), add_low(first[1], received[1])


def scatter_four(near, far, *earlier):
    return after(near, earlier).astype(F32) + send(far, ALONG_Z[2]).astype(F32)


def z_relative(half, j):
    return 2 * j + half


def place(meta, slot, at, j):
    half, y_rel, x_rel = CHIP_SLOTS[slot][at]
    chip = (meta[0] ^ y_rel) * 2 + (meta[1] ^ x_rel)
    return chip, meta[3] ^ z_relative(half, j)


def load_all(copies):
    for copy in copies:
        copy.start()
    for copy in copies:
        copy.wait()


def load_qkv(meta, refs, weight, sem):
    copies = []
    for slot, ref in enumerate(refs):
        for at in range(2):
            for j in range(2):
                chip, z = place(meta, slot, at, j)
                for other in range(2):
                    row = pl.multiple_of((chip * 2 + (meta[2] ^ other)) * 128 + z * 32, 32)
                    for t in range(3):
                        copies.append(
                            pltpu.make_async_copy(
                                ref.at[at, j, pl.ds((other * 3 + t) * 32, 32)],
                                weight.at[t, pl.ds(row, 32), :],
                                sem.at[len(copies)],
                            )
                        )
    return copies


def load_split_rows(meta, refs, base, blocks, weight, sem):
    copies = []
    for slot, ref in enumerate(refs):
        for at in range(2):
            for j in range(2):
                chip, z = place(meta, slot, at, j)
                for other in range(2):
                    row = pl.multiple_of((chip * 2 + (meta[2] ^ other)) * 128 + z * 32, 32)
                    copies.append(
                        pltpu.make_async_copy(
                            ref.at[at, j, pl.ds(base + other * blocks, blocks)],
                            weight.at[:, pl.ds(row, 32), :],
                            sem.at[len(copies)],
                        )
                    )
    return copies


def load_out(meta, refs, weight, sem):
    copies = []
    for slot, ref in enumerate(refs):
        for at in range(2):
            for j in range(2):
                chip, z = place(meta, slot, at, j)
                row = pl.multiple_of((chip * 4 + z) * 32, 32)
                for b in range(2):
                    copies.append(
                        pltpu.make_async_copy(
                            ref.at[at, j, pl.ds(192 + b * 32, 32)],
                            weight.at[b, pl.ds(row, 32), :],
                            sem.at[len(copies)],
                        )
                    )
    return copies


def load_own_rows(meta, refs, base, blocks, rows, weight, sem):
    copies = []
    for slot, ref in enumerate(refs):
        for at in range(2):
            for j in range(2):
                chip, z = place(meta, slot, at, j)
                row = pl.multiple_of((chip * 4 + z) * rows, 32)
                copies.append(
                    pltpu.make_async_copy(
                        ref.at[at, j, pl.ds(base, blocks)],
                        weight.at[:, pl.ds(row, rows), :],
                        sem.at[len(copies)],
                    )
                )
    return copies


def kernel_call(kernel, meta, operands, in_specs, out_specs, out_shape, scratch=(), grid=(4,), flops=0, moved=0, exps=0):
    return pl.pallas_call(
        kernel,
        grid_spec=pltpu.PrefetchScalarGridSpec(
            num_scalar_prefetch=1,
            grid=grid,
            in_specs=in_specs,
            out_specs=out_specs,
            scratch_shapes=list(scratch),
        ),
        out_shape=out_shape,
        compiler_params=pltpu.CompilerParams(vmem_limit_bytes=VMEM_LIMIT),
        cost_estimate=pl.CostEstimate(
            flops=int(flops * 1.5), bytes_accessed=int(moved * 1.5), transcendentals=int(exps * 1.5)
        ),
    )(meta, *operands)


HBM = pl.BlockSpec(memory_space=pl.ANY)


def spec(shape, index):
    return pl.BlockSpec(shape, index)


def whole(shape):
    return pl.BlockSpec(shape, lambda i, m: (0,) * len(shape))


def shaped(shape, kind):
    return jax.ShapeDtypeStruct(shape, kind)


def low_block(i):
    return jnp.minimum(i, 1)


def high_block(i):
    return jnp.maximum(i - 2, 0)


def turned(i):
    return lax.rem(i + 2, 4)


def project_qkv(meta, own, other, embedded, shift, pieces):
    def kernel(m, own_ref, other_ref, emb_ref, shift_ref, *rest):
        refs, (hidden_ref, out_ref, weight, sem) = rest[:4], rest[4:]
        i = pl.program_id(0)

        @pl.when(i == 0)
        def _():
            load_all(load_qkv(m, refs, weight, sem))

        tokens = jnp.where(i < 2, own_ref[0].astype(F32), other_ref[0].astype(F32))
        hidden = (tokens + emb_ref[...]).astype(BF)
        hidden_ref[...] = hidden
        for t in range(3):
            out_ref[t] = (dot(hidden, weight[t]) + shift_ref[t : t + 1, :]).astype(BF)

    return kernel_call(
        kernel,
        meta,
        (own, other, embedded, shift, *pieces),
        [
            spec((1, 256, 1024), lambda i, m: (low_block(i), 0, 0)),
            spec((1, 256, 1024), lambda i, m: (high_block(i), 0, 0)),
            whole((1, 1024)),
            whole((3, 512)),
        ]
        + [HBM] * 4,
        [spec((256, 1024), lambda i, m: (i, 0)), spec((3, 256, 512), lambda i, m: (0, i, 0))],
        [shaped((1024, 1024), BF), shaped((3, 1024, 512), BF)],
        [pltpu.VMEM((3, 1024, 512), BF), pltpu.SemaphoreType.DMA((96,))],
        flops=2 * 1024 * 1024 * 1536,
        moved=10 << 20,
    )


def head_lanes(h, kind):
    lane = lax.broadcasted_iota(jnp.int32, (1, 128), 1)
    return jnp.where(lane // HEAD_DIM == h, 1.0, 0.0).astype(kind)


def attend(meta, part, qkv, seg_column, seg_row):
    def kernel(m, q_ref, k_ref, v_ref, column_ref, row_ref, out_ref, lse_ref):
        queries, keys, values = q_ref[0] * jnp.asarray(0.125, BF), k_ref[0], v_ref[0]
        allowed = column_ref[...] == row_ref[...]
        mixed = jnp.zeros((128, 1024), F32)
        for h in range(2):
            lanes = head_lanes(h, BF)
            scores = jnp.where(allowed, dot(keys * lanes, queries, NT), -1e30)
            largest = jnp.max(scores, axis=0, keepdims=True)
            exponent = jnp.exp(scores - largest)
            total = jnp.sum(exponent, axis=0, keepdims=True)
            mixed += dot(values * lanes, exponent.astype(BF), TN) / total
            lse_ref[0, h : h + 1, :] = largest + jnp.log(total)
        out_ref[...] = jnp.transpose(mixed).astype(BF)

    base = part * 2
    third = lambda t: spec((1, 1024, 128), lambda i, m: (t, 0, base + i))
    return kernel_call(
        kernel,
        meta,
        (qkv, qkv, qkv, seg_column, seg_row),
        [third(0), third(1), third(2), whole((1024, 1)), whole((1, 1024))],
        [spec((1024, 128), lambda i, m: (0, i)), spec((1, 8, 1024), lambda i, m: (i, 0, 0))],
        [shaped((1024, 256), BF), shaped((2, 8, 1024), F32)],
        grid=(2,),
        flops=8 * 4 * 1024 * 1024 * 256,
        moved=5 << 20,
        exps=8 << 20,
    )


def attend_back(i, q_ref, k_ref, v_ref, out_ref, lse_ref, column_ref, row_ref, d_ref, sum_ref, dout, prob, ds):
    columns = pl.ds(pl.multiple_of(i * 128, 128), 128)
    queries, upstream = q_ref[0], dout[:, columns]
    product = out_ref[...].astype(F32) * upstream.astype(F32)
    row = lax.broadcasted_iota(jnp.int32, (8, 128), 0)
    lane = lax.broadcasted_iota(jnp.int32, (8, 128), 1)
    picked = jnp.where(lane // HEAD_DIM == row, 1.0, 0.0).astype(F32)
    center = lax.dot_general(picked, product, NT, precision=lax.Precision.HIGHEST, preferred_element_type=F32)
    dq, dk, dv = (jnp.zeros((1024, 128), F32) for _ in range(3))
    for h in range(2):
        lanes = head_lanes(h, BF)
        for block in range(4):
            rows = pl.ds(block * 256, 256)
            allowed = column_ref[rows, :] == row_ref[...]
            scores = dot(k_ref[0, rows, :] * lanes * jnp.asarray(0.125, BF), queries, NT)
            p = jnp.where(allowed, jnp.exp(scores - lse_ref[0, h : h + 1, :]), 0.0)
            dp = dot(v_ref[0, rows, :] * lanes, upstream, NT)
            prob[rows, :] = p.astype(BF)
            ds[rows, :] = (p * (dp - center[h : h + 1, :])).astype(BF)
        dv += dot(prob[...], upstream * lanes)
        dk += dot(ds[...], queries * lanes)
        dq += dot(ds[...], k_ref[0] * lanes, TN)
    dq, dk, dv = (dq * 0.125).astype(BF), (dk * 0.125).astype(BF), dv.astype(BF)
    d_ref[0, :, columns], d_ref[1, :, columns], d_ref[2, :, columns] = dq, dk, dv
    sum_ref[0:1, columns] = jnp.sum(dq.astype(F32), axis=0, keepdims=True)
    sum_ref[1:2, columns] = jnp.sum(dv.astype(F32), axis=0, keepdims=True)


def heads_out(part, own_ref, other_ref, weight, dout):
    rows = pl.ds(part * 256, 256)
    for half, ref in enumerate((own_ref, other_ref)):
        da = ref[...]
        result = dot(da[:, :512], weight[0, rows, :], NT) + dot(da[:, 512:], weight[1, rows, :], NT)
        dout[pl.ds(half * 512, 512), :] = result.astype(BF)


def attend_specs(part):
    pair = lambda i: jnp.minimum(i, 1)
    third = lambda t: spec((1, 1024, 128), lambda i, m: (t, 0, part * 2 + pair(i)))
    return [
        third(0),
        third(1),
        third(2),
        spec((1024, 128), lambda i, m: (0, pair(i))),
        spec((1, 8, 1024), lambda i, m: (pair(i), 0, 0)),
        whole((1024, 1)),
        whole((1, 1024)),
        whole((512, 1024)),
        whole((512, 1024)),
    ]


ATTEND_SCRATCH = (
    pltpu.VMEM((2, 512, 512), BF),
    pltpu.VMEM((1024, 256), BF),
    pltpu.VMEM((1024, 1024), BF),
    pltpu.VMEM((1024, 1024), BF),
    pltpu.SemaphoreType.DMA((32,)),
)


def attend_back_part(meta, part, qkv, mixed, lse, seg_column, seg_row, da_own, da_other, pieces):
    def kernel(m, q_ref, k_ref, v_ref, out_ref, lse_ref, column_ref, row_ref, own_ref, other_ref, *rest):
        refs, (d_ref, sum_ref), (weight, dout, prob, ds, sem) = rest[:4], rest[4:6], rest[6:]
        i = pl.program_id(0)

        @pl.when(i == 0)
        def _():
            load_all(load_out(m, refs, weight, sem))
            heads_out(part, own_ref, other_ref, weight, dout)

        attend_back(i, q_ref, k_ref, v_ref, out_ref, lse_ref, column_ref, row_ref, d_ref, sum_ref, dout, prob, ds)

    return kernel_call(
        kernel,
        meta,
        (qkv, qkv, qkv, mixed, lse, seg_column, seg_row, da_own, da_other, *pieces),
        attend_specs(part) + [HBM] * 4,
        [whole((3, 1024, 256)), whole((8, 256))],
        [shaped((3, 1024, 256), BF), shaped((8, 256), F32)],
        ATTEND_SCRATCH,
        grid=(2,),
        flops=11 * 10**9,
        moved=10 << 20,
        exps=4 << 20,
    )


def project_out(meta, mixed, pieces):
    def kernel(m, x_ref, w_ref, *rest):
        refs, (send_ref, own_ref, weight, sem) = rest[:4], rest[4:]
        i = pl.program_id(0)

        @pl.when(i == 0)
        def _():
            load_all(load_out(m, refs, weight, sem))

        for b in range(2):
            columns = pl.ds(b * 512, 512)
            result = dot(x_ref[...], weight[b, :256, :]) + dot(w_ref[...], weight[b, 256:, :])

            @pl.when(i < 2)
            def _():
                send_ref[:, columns] = result.astype(BF)

            @pl.when(i >= 2)
            def _():
                own_ref[:, columns] = result

    return kernel_call(
        kernel,
        meta,
        (*mixed, *pieces),
        [spec((256, 256), lambda i, m: (turned(i), 0))] * 2 + [HBM] * 4,
        [spec((256, 1024), lambda i, m: (low_block(i), 0)), spec((256, 1024), lambda i, m: (high_block(i), 0))],
        [shaped((512, 1024), BF), shaped((512, 1024), F32)],
        [pltpu.VMEM((2, 512, 512), BF), pltpu.SemaphoreType.DMA((32,))],
        flops=2 * 1024 * 1024 * 512,
        moved=6 << 20,
    )


def normal_parts(values):
    center = values - jnp.mean(values, axis=-1, keepdims=True)
    inverse = lax.rsqrt(jnp.mean(center * center, axis=-1, keepdims=True) + EPSILON)
    return center * inverse, inverse


def normal_back(upstream, normal_part, inverse, gain):
    scaled = upstream * gain
    return inverse * (
        scaled
        - jnp.mean(scaled, axis=-1, keepdims=True)
        - normal_part * jnp.mean(scaled * normal_part, axis=-1, keepdims=True)
    )


BY_ROWS = lambda i, m: (i, 0)


def first_norm(meta, tokens, embedded, own, received, vectors):
    def kernel(m, tok_ref, emb_ref, own_ref, recv_ref, vec_ref, normal_ref, inverse_ref, low_ref):
        hidden = tok_ref[0].astype(F32) + emb_ref[...]
        attended = own_ref[...] + recv_ref[...].astype(F32) + vec_ref[0:1, :]
        normal_part, inverse = normal_parts(hidden + attended)
        normal_ref[...] = normal_part
        inverse_ref[...] = jnp.broadcast_to(inverse, (256, 128))
        low_ref[...] = (normal_part * vec_ref[1:2, :] + vec_ref[2:3, :]).astype(BF)

    block = spec((256, 1024), BY_ROWS)
    return kernel_call(
        kernel,
        meta,
        (tokens, embedded, own, received, vectors),
        [spec((1, 256, 1024), lambda i, m: (i, 0, 0)), whole((1, 1024)), block, block, whole((8, 1024))],
        [block, spec((256, 128), BY_ROWS), block],
        [shaped((512, 1024), F32), shaped((512, 128), F32), shaped((512, 1024), BF)],
        grid=(2,),
        flops=512 * 1024 * 12,
        moved=8 << 20,
    )


def expand(meta, own, other, shift, pieces):
    def kernel(m, own_ref, other_ref, shift_ref, *rest):
        refs, (act_ref, slope_ref, weight, sem) = rest[:4], rest[4:]
        i = pl.program_id(0)

        @pl.when(i == 0)
        def _():
            load_all(load_split_rows(m, refs, 0, 4, weight, sem))

        x = jnp.where(i < 2, own_ref[...].astype(F32), other_ref[...].astype(F32)).astype(BF)
        for b in range(4):
            columns = pl.ds(b * 512, 512)
            u = dot(x, weight[b]) + shift_ref[:, columns]
            cumulative = 0.5 * (1.0 + lax.erf(u * INVERSE_ROOT_TWO))
            act_ref[:, columns] = (u * cumulative).astype(BF)
            density = jnp.exp(-0.5 * u * u) * INVERSE_ROOT_TWO_PI
            slope_ref[:, columns] = (cumulative + u * density).astype(BF)

    return kernel_call(
        kernel,
        meta,
        (own, other, shift, *pieces),
        [
            spec((256, 1024), lambda i, m: (low_block(i), 0)),
            spec((256, 1024), lambda i, m: (high_block(i), 0)),
            whole((1, 2048)),
        ]
        + [HBM] * 4,
        [spec((256, 2048), BY_ROWS), spec((256, 2048), BY_ROWS)],
        [shaped((1024, 2048), BF), shaped((1024, 2048), BF)],
        [pltpu.VMEM((4, 1024, 512), BF), pltpu.SemaphoreType.DMA((32,))],
        flops=2 * 1024 * 1024 * 2048,
        moved=14 << 20,
        exps=4 << 20,
    )


def contract(meta, activated, pieces):
    def kernel(m, x_ref, *rest):
        refs, (send_ref, own_ref, weight, sem) = rest[:4], rest[4:]
        i = pl.program_id(0)

        @pl.when(i == 0)
        def _():
            load_all(load_own_rows(m, refs, 0, 2, 128, weight, sem))

        for b in range(2):
            columns = pl.ds(b * 512, 512)
            result = dot(x_ref[...], weight[b])

            @pl.when(i < 2)
            def _():
                send_ref[:, columns] = result.astype(BF)

            @pl.when(i >= 2)
            def _():
                own_ref[:, columns] = result

    return kernel_call(
        kernel,
        meta,
        (activated, *pieces),
        [spec((256, 2048), lambda i, m: (turned(i), 0))] + [HBM] * 4,
        [spec((256, 1024), lambda i, m: (low_block(i), 0)), spec((256, 1024), lambda i, m: (high_block(i), 0))],
        [shaped((512, 1024), BF), shaped((512, 1024), F32)],
        [pltpu.VMEM((2, 2048, 512), BF), pltpu.SemaphoreType.DMA((16,))],
        flops=2 * 1024 * 1024 * 2048,
        moved=11 << 20,
    )


def row_sums(sum_ref, i, rows):
    @pl.when(i == 0)
    def _():
        sum_ref[...] = jnp.zeros_like(sum_ref)

    for n, value in enumerate(rows):
        sum_ref[n : n + 1, :] += jnp.sum(value, axis=0, keepdims=True)


def second_norm(meta, normal_one, own, received, cotangent, vectors):
    def kernel(m, normal_ref, own_ref, recv_ref, cot_ref, vec_ref, out_ref, resid_ref, low_ref, sum_ref):
        normed = normal_ref[...] * vec_ref[1:2, :] + vec_ref[2:3, :]
        downward = own_ref[...] + recv_ref[...].astype(F32) + vec_ref[3:4, :]
        normal_part, inverse = normal_parts(normed + downward)
        out_ref[...] = (normal_part * vec_ref[4:5, :] + vec_ref[5:6, :]).astype(BF)
        upstream = cot_ref[...].astype(F32)
        resid = normal_back(upstream, normal_part, inverse, vec_ref[4:5, :])
        resid_ref[...] = resid
        low = resid.astype(BF)
        low_ref[...] = low
        row_sums(sum_ref, pl.program_id(0), (upstream * normal_part, upstream, low.astype(F32)))

    block = spec((256, 1024), BY_ROWS)
    return kernel_call(
        kernel,
        meta,
        (normal_one, own, received, cotangent, vectors),
        [block, block, block, block, whole((8, 1024))],
        [block, block, block, whole((8, 1024))],
        [shaped((512, 1024), BF), shaped((512, 1024), F32), shaped((512, 1024), BF), shaped((8, 1024), F32)],
        grid=(2,),
        flops=512 * 1024 * 30,
        moved=10 << 20,
    )


def feed_back(meta, own, other, slope, down_pieces, up_pieces):
    def kernel(m, own_ref, other_ref, slope_ref, *rest):
        down_refs, up_refs = rest[:4], rest[4:8]
        du_ref, send_ref, mine_ref, sum_ref, down, up, down_sem, up_sem = rest[8:]
        i = pl.program_id(0)

        @pl.when(i == 0)
        def _():
            load_all(
                load_own_rows(m, down_refs, 0, 2, 128, down, down_sem)
                + load_split_rows(m, up_refs, 0, 4, up, up_sem)
            )
            sum_ref[...] = jnp.zeros_like(sum_ref)

        df = jnp.where(i < 2, other_ref[...].astype(F32), own_ref[...].astype(F32)).astype(BF)
        total = jnp.zeros((256, 1024), F32)
        for b in range(4):
            rows = pl.ds(b * 512, 512)
            act = dot(df[:, :512], down[0, rows, :], NT) + dot(df[:, 512:], down[1, rows, :], NT)
            du = (act * slope_ref[:, rows].astype(F32)).astype(BF)
            du_ref[:, rows] = du
            sum_ref[0:1, rows] += jnp.sum(du.astype(F32), axis=0, keepdims=True)
            total += dot(du, up[b], NT)

        @pl.when(i < 2)
        def _():
            send_ref[...] = total.astype(BF)

        @pl.when(i >= 2)
        def _():
            mine_ref[...] = total

    return kernel_call(
        kernel,
        meta,
        (own, other, slope, *down_pieces, *up_pieces),
        [
            spec((256, 1024), lambda i, m: (high_block(i), 0)),
            spec((256, 1024), lambda i, m: (low_block(i), 0)),
            spec((256, 2048), lambda i, m: (turned(i), 0)),
        ]
        + [HBM] * 8,
        [
            spec((256, 2048), lambda i, m: (turned(i), 0)),
            spec((256, 1024), lambda i, m: (low_block(i), 0)),
            spec((256, 1024), lambda i, m: (high_block(i), 0)),
            whole((8, 2048)),
        ],
        [shaped((1024, 2048), BF), shaped((512, 1024), BF), shaped((512, 1024), F32), shaped((8, 2048), F32)],
        [
            pltpu.VMEM((2, 2048, 512), BF),
            pltpu.VMEM((4, 1024, 512), BF),
            pltpu.SemaphoreType.DMA((16,)),
            pltpu.SemaphoreType.DMA((32,)),
        ],
        flops=4 * 1024 * 1024 * 2048,
        moved=22 << 20,
    )


def first_norm_back(meta, resid, own, received, normal_one, inverse_one, vectors):
    def kernel(m, resid_ref, own_ref, recv_ref, normal_ref, inverse_ref, vec_ref, out_ref, low_ref, sum_ref):
        upstream = resid_ref[...] + own_ref[...] + recv_ref[...].astype(F32)
        normal_part = normal_ref[...]
        resid_one = normal_back(upstream, normal_part, inverse_ref[:, 0:1], vec_ref[1:2, :])
        out_ref[...] = resid_one
        low = resid_one.astype(BF)
        low_ref[...] = low
        row_sums(sum_ref, pl.program_id(0), (upstream * normal_part, upstream, low.astype(F32)))

    block = spec((256, 1024), BY_ROWS)
    return kernel_call(
        kernel,
        meta,
        (resid, own, received, normal_one, inverse_one, vectors),
        [block, block, block, block, spec((256, 128), BY_ROWS), whole((8, 1024))],
        [block, block, whole((8, 1024))],
        [shaped((512, 1024), F32), shaped((512, 1024), BF), shaped((8, 1024), F32)],
        grid=(2,),
        flops=512 * 1024 * 20,
        moved=10 << 20,
    )


def rel_chip(s, m):
    return (m[0] ^ (s // 2)) * 2 + (m[1] ^ lax.rem(s, 2))


def piece_outputs(blocks, rows, columns=512):
    shape = (2, 2, blocks, rows, columns)
    return [HBM] * 4, [shaped(shape, BF)] * 4


def push(s, outs, copy_for):
    first_keep, first_send, second_keep, second_send = outs
    slots = (
        ((first_keep, 0), (second_keep, 0)),
        ((first_keep, 1), (second_send, 0)),
        ((first_send, 0), (second_keep, 1)),
        ((first_send, 1), (second_send, 1)),
    )
    for n, (first, second) in enumerate(slots):

        @pl.when(s == n)
        def _(n=n, first=first, second=second):
            for k in range(4):
                ref, at = (first, second)[k // 2]
                for copy in copy_for(n, k, ref.at[at, k % 2]):
                    copy.start()

    @pl.when(s == 3)
    def _():
        for n, (first, second) in enumerate(slots):
            for k in range(4):
                ref, at = (first, second)[k // 2]
                for copy in copy_for(n, k, ref.at[at, k % 2]):
                    copy.wait()


def weigh_down(meta, activated, own, other):
    def kernel(m, x_ref, own_ref, other_ref, *rest):
        outs, (stage, sem) = rest[:4], rest[4:]
        s = pl.program_id(0)
        x = x_ref[...]
        for b in range(2):
            columns = pl.ds(b * 512, 512)
            stage[s, b] = (dot(x[:512], own_ref[:, columns], TN) + dot(x[512:], other_ref[:, columns], TN)).astype(BF)

        def copy_for(n, k, target):
            row = pl.multiple_of((m[3] ^ z_relative(k // 2, k % 2)) * 128, 128)
            return [pltpu.make_async_copy(stage.at[n, :, pl.ds(row, 128), :], target, sem.at[n * 4 + k])]

        push(s, outs, copy_for)

    out_specs, out_shape = piece_outputs(2, 128)
    return kernel_call(
        kernel,
        meta,
        (activated, own, other),
        [spec((1024, 512), lambda s, m: (0, rel_chip(s, m))), whole((512, 1024)), whole((512, 1024))],
        out_specs,
        out_shape,
        [pltpu.VMEM((4, 2, 512, 512), BF), pltpu.SemaphoreType.DMA((16,))],
        flops=2 * 1024 * 1024 * 2048,
        moved=10 << 20,
    )


def weigh_up(meta, normed_own, normed_other, du):
    def kernel(m, own_ref, other_ref, du_ref, *rest):
        outs, (up, sem) = rest[:4], rest[4:]
        s = pl.program_id(0)
        for b in range(4):
            columns = pl.ds(b * 512, 512)
            up[s, b] = (dot(own_ref[...], du_ref[:512, columns], TN) + dot(other_ref[...], du_ref[512:, columns], TN)).astype(BF)

        def copy_for(n, k, target):
            z = m[3] ^ z_relative(k // 2, k % 2)
            copies = []
            for rel in range(2):
                row = pl.multiple_of((m[2] ^ rel) * 128 + z * 32, 32)
                copies.append(
                    pltpu.make_async_copy(
                        up.at[n, :, pl.ds(row, 32), :],
                        target.at[pl.ds(rel * 4, 4)],
                        sem.at[(n * 4 + k) * 2 + rel],
                    )
                )
            return copies

        push(s, outs, copy_for)

    out_specs, out_shape = piece_outputs(8, 32)
    return kernel_call(
        kernel,
        meta,
        (normed_own, normed_other, du),
        [
            spec((512, 256), lambda s, m: (0, rel_chip(s, m))),
            spec((512, 256), lambda s, m: (0, rel_chip(s, m))),
            whole((1024, 2048)),
        ],
        out_specs,
        out_shape,
        [pltpu.VMEM((4, 4, 256, 512), BF), pltpu.SemaphoreType.DMA((32,))],
        flops=2 * 1024 * 1024 * 2048,
        moved=15 << 20,
    )


def weigh_qkv(meta, hidden, dqkv, out_terms=()):
    def kernel(m, x_ref, d_ref, *rest):
        s = pl.program_id(0)
        if out_terms:
            mixed_ref, more_ref, own_ref, other_ref = rest[:4]
            rest = rest[4:]
        outs, stage, sem = rest[:4], rest[4], rest[5]
        for t in range(3):
            stage[s, t] = dot(x_ref[...], d_ref[t], TN).astype(BF)
        if out_terms:
            stage_out, sem_out = rest[6:]
            x = jnp.where(rel_chip(s, m) < 2, mixed_ref[...].astype(F32), more_ref[...].astype(F32)).astype(BF)
            for b in range(4):
                columns = pl.ds(b * 256, 256)
                stage_out[s, b] = (
                    dot(x[:512], own_ref[:, columns], TN) + dot(x[512:], other_ref[:, columns], TN)
                ).astype(BF)

        def copy_for(n, k, target):
            z = m[3] ^ z_relative(k // 2, k % 2)
            copies = []
            for rel in range(2):
                row = pl.multiple_of((m[2] ^ rel) * 128 + z * 32, 32)
                copies.append(
                    pltpu.make_async_copy(
                        stage.at[n, :, pl.ds(row, 32), :],
                        target.at[pl.ds(rel * 3, 3)],
                        sem.at[(n * 4 + k) * 2 + rel],
                    )
                )
            if out_terms:
                copies.append(
                    pltpu.make_async_copy(
                        stage_out.at[n, :, pl.ds(pl.multiple_of(z * 32, 32), 32), :],
                        target.at[pl.ds(6, 4)],
                        sem_out.at[n * 4 + k],
                    )
                )
            return copies

        push(s, outs, copy_for)

    out_specs, out_shape = piece_outputs(10 if out_terms else 6, 32, 256)
    in_specs = [spec((1024, 256), lambda s, m: (0, rel_chip(s, m))), whole((3, 1024, 256))]
    scratch = [pltpu.VMEM((4, 3, 256, 256), BF), pltpu.SemaphoreType.DMA((32,))]
    if out_terms:
        in_specs += [spec((1024, 128), lambda s, m: (0, rel_chip(s, m) % 2))] * 2 + [whole((512, 1024))] * 2
        scratch += [pltpu.VMEM((4, 4, 128, 256), BF), pltpu.SemaphoreType.DMA((16,))]
    return kernel_call(
        kernel,
        meta,
        (hidden, dqkv, *out_terms),
        in_specs,
        out_specs,
        out_shape,
        scratch,
        flops=2 * 1024 * 1024 * 1024,
        moved=8 << 20,
    )


def qkv_back(meta, dqkv, pieces):
    def kernel(m, d_ref, e_ref, *rest):
        refs, (send_ref, own_ref, weight, sem) = rest[:4], rest[4:]
        i = pl.program_id(0)

        @pl.when(i == 0)
        def _():
            load_all(load_qkv(m, refs, weight, sem))

        total = jnp.zeros((256, 1024), F32)
        for t in range(3):
            total += dot(d_ref[t], weight[t, :, :256], NT) + dot(e_ref[t], weight[t, :, 256:], NT)

        @pl.when(i < 2)
        def _():
            send_ref[...] = total.astype(BF)

        @pl.when(i >= 2)
        def _():
            own_ref[...] = total

    return kernel_call(
        kernel,
        meta,
        (*dqkv, *pieces),
        [spec((3, 256, 256), lambda i, m: (0, turned(i), 0))] * 2 + [HBM] * 4,
        [spec((256, 1024), lambda i, m: (low_block(i), 0)), spec((256, 1024), lambda i, m: (high_block(i), 0))],
        [shaped((512, 1024), BF), shaped((512, 1024), F32)],
        [pltpu.VMEM((3, 1024, 512), BF), pltpu.SemaphoreType.DMA((96,))],
        flops=2 * 1024 * 1024 * 1536,
        moved=9 << 20,
    )


def last_sum(meta, resid, own, received):
    def kernel(m, resid_ref, own_ref, recv_ref, out_ref, sum_ref):
        total = resid_ref[...] + own_ref[...] + recv_ref[...].astype(F32)
        out_ref[...] = total.astype(BF)
        row_sums(sum_ref, pl.program_id(0), (total,))

    block = spec((256, 1024), BY_ROWS)
    return kernel_call(
        kernel,
        meta,
        (resid, own, received),
        [block, block, block],
        [block, whole((8, 1024))],
        [shaped((512, 1024), BF), shaped((8, 1024), F32)],
        grid=(2,),
        flops=512 * 1024 * 4,
        moved=6 << 20,
    )


VECTOR_SIZES = (64, 32, 32, 32, 128, 32, 32, 32)


def split_vectors(packed):
    parts, start = [], 0
    for size in VECTOR_SIZES:
        parts.append(packed[:, start : start + size])
        start += size
    return parts


def chip_body(
    tokens,
    timestep,
    segment_ids,
    cotangent,
    time_weight,
    qkv_weight,
    qv_bias,
    out_weight,
    out_bias,
    norm_gain,
    norm_bias,
    up_weight,
    up_bias,
    down_weight,
    down_bias,
    final_gain,
    final_bias,
):
    dp, z = lax.axis_index("dp"), lax.axis_index("sp")
    y, x, c = dp // 4, (dp // 2) % 2, dp % 2
    meta = jnp.stack([y, x, c, z]).astype(jnp.int32)
    pick = lambda value, index, axis: lax.dynamic_index_in_dim(value, index, axis, keepdims=False)

    me = dp * 4 + z

    qkv_split = qkv_weight.reshape(32, 3, 4, 2, 128)
    up_split = up_weight.reshape(32, 4, 2, 512)
    qkv_half = lambda core: pick(qkv_split, core, 3).reshape(32, 3, 512).transpose(1, 0, 2).reshape(96, 512)
    up_half = lambda core: pick(up_split, core, 2).transpose(1, 0, 2)
    small = jnp.concatenate([qv_bias, out_bias, norm_gain, norm_bias, up_bias, down_bias, final_gain, final_bias])
    small = jnp.pad(small[None], ((0, 15), (0, 128)))
    received = send(jnp.concatenate([qkv_half(1 - c), small]), PAIR)
    small = jnp.concatenate([small[:1], received[96:97], small[2:]])
    out_shard = out_weight.reshape(32, 2, 512).transpose(1, 0, 2).reshape(64, 512)
    qkv_shard = jnp.concatenate([qkv_half(c), received[:96], out_shard, small])
    up_shard = jnp.concatenate([up_half(c), send(up_half(1 - c), PAIR)])
    down_shard = down_weight.reshape(128, 2, 512).transpose(1, 0, 2)
    qkv_line = gather_line(qkv_shard)

    stamps = after(timestep.astype(jnp.int32), received)[:, None]
    stamps = jnp.concatenate([stamps // 64, stamps % 64], axis=1).astype(BF)
    for pairs in (PAIR, ALONG_X, ALONG_Y):
        stamps = jnp.concatenate([stamps, send(stamps, pairs)])
    stamps = stamps.astype(F32)
    stamps = (stamps[:, 0] * 64.0 + stamps[:, 1]).reshape(4, 4)
    sums_order = jnp.arange(4, dtype=jnp.int32) ^ z
    from_pair = (sums_order // 2) ^ c
    stamps = jnp.take_along_axis(stamps, jnp.broadcast_to(from_pair * 2 + sums_order % 2, (4, 4)), axis=1).reshape(16, 1)
    column = me * 32 + jnp.arange(32, dtype=jnp.int32)
    frequency = jnp.exp(-math.log(10000.0) * (column % 512).astype(F32) / 512)
    phases = stamps * frequency[None, :]
    features = jnp.where(column[None, :] < 512, jnp.sin(phases), jnp.cos(phases)).astype(BF)
    features = after(features, qkv_line[0])
    embedded = jnp.dot(features, time_weight, preferred_element_type=F32)
    embedded = embedded + send(embedded, PAIR)
    for width, pairs in ((8, ALONG_Y), (4, ALONG_X), (2, ALONG_Z[2]), (1, ALONG_Z[1])):
        embedded = embedded[:width] + send(embedded[width:], pairs)

    qkv_pieces = gather_plane(*qkv_line)

    def take_rows(value, *earlier):
        return jnp.stack(after([send(pick(value, (z + k) % 2, 0), ROW_OUT[k]) for k in range(2)], earlier))

    def give_rows(value, *earlier):
        parts = after([send(value[k * 256 : (k + 1) * 256], ROW_BACK[k]) for k in range(2)], earlier)
        swapped = (z % 2) == 1
        return jnp.stack([jnp.where(swapped, parts[1], parts[0]), jnp.where(swapped, parts[0], parts[1])])

    documents = jnp.concatenate([segment_ids // 32, segment_ids % 32], axis=1).astype(BF)
    documents = jnp.pad(documents[:, None, :], ((0, 0), (0, 15), (0, 512)))
    own_tokens = take_rows(after(jnp.concatenate([tokens, documents], axis=1), qkv_line))
    other_tokens = send(own_tokens, PAIR)
    codes = jnp.concatenate([own_tokens[:, 256], other_tokens[:, 256]]).astype(F32)
    segments = (codes[:, :256] * 32.0 + codes[:, 256:512]).reshape(1024)
    seg_column, seg_row = segments[:, None], segments[None, :]

    up_far = send(after(up_shard, own_tokens), ALONG_Z[2])

    natural = jnp.arange(32, dtype=jnp.int32)
    order = (natural[:, None] ^ me) == natural[None, :]
    small = jnp.stack([piece[:, :, 256:258, :384] for piece in qkv_pieces])
    small = jnp.stack(
        [
            small[half * 2 + (x_rel if half else y_rel), y_rel if half else x_rel, j, rel]
            for y_rel in range(2)
            for x_rel in range(2)
            for rel in range(2)
            for j in range(2)
            for half in range(2)
        ]
    )
    small = jnp.dot(order.astype(BF), small, preferred_element_type=F32)
    full = [part.reshape(1, -1) for part in split_vectors(small)]
    qv_full, out_shift, first_gain, first_shift, up_full, down_shift, second_gain, second_shift = full
    blank = jnp.zeros((2, 1024), F32)
    vectors = jnp.concatenate([out_shift, first_gain, first_shift, down_shift, second_gain, second_shift, blank])
    qv_mine = pick(qv_full.reshape(2, 4, 2, 128), c, 2).reshape(2, 512)
    qkv_shift = jnp.stack([qv_mine[0], jnp.zeros((512,), F32), qv_mine[1]])
    up_shift = pick(up_full.reshape(4, 2, 512), c, 1).reshape(1, 2048)

    hidden, qkv = project_qkv(meta, own_tokens, other_tokens, embedded, qkv_shift, qkv_pieces)
    up_first = jnp.stack([after(up_shard, qkv), up_far])
    mixed_one, lse_one = attend(meta, 0, after(qkv, up_first), seg_column, seg_row)
    up_second = after(send(up_first, ALONG_Z[1]), mixed_one)
    mixed_two, lse_two = attend(meta, 1, after(qkv, up_second), seg_column, seg_row)
    up_pieces = gather_plane(up_first, up_second, mixed_two)
    down_first = jnp.stack([after(down_shard, mixed_two), send(after(down_shard, up_second), ALONG_Z[2])])
    mixed = mixed_one, after(mixed_two, down_first, up_pieces[0], up_pieces[2])
    away, mine = project_out(meta, mixed, qkv_pieces)
    down_second = after(send(down_first, ALONG_Z[1]), mine)
    normal_one, inverse_one, normed = first_norm(
        meta, own_tokens, embedded, after(mine, down_second, up_pieces), send(away, PAIR), vectors
    )
    normed_other = send(normed, PAIR)
    down_pieces = gather_plane(down_first, down_second, normed)
    normed_other = after(normed_other, down_pieces[0], down_pieces[2])
    activated, slope = expand(meta, normed, normed_other, up_shift, up_pieces)
    own_cotangent = take_rows(after(cotangent, normed), activated).reshape(512, 1024)
    away, mine = contract(meta, after(activated, own_cotangent), down_pieces)
    result, resid_two, df, sums_two = second_norm(meta, normal_one, mine, send(away, PAIR), own_cotangent, vectors)

    df_other = send(df, PAIR)
    down_terms = weigh_down(meta, activated, df, df_other)
    du, away, mine, bias_sums = feed_back(meta, after(df, down_terms), df_other, slope, down_pieces, up_pieces)
    received = send(away, PAIR)
    up_terms = weigh_up(meta, normed, normed_other, du)
    output = give_rows(after(result, down_terms), up_terms)
    down_sums = add_one(*scatter_one(*down_terms), up_terms)
    resid_one, da, sums_one = first_norm_back(
        meta, after(resid_two, down_sums, output), mine, received, normal_one, inverse_one, vectors
    )
    da_other = send(da, PAIR)
    down_sums = scatter_two(*down_sums)
    up_sums = scatter_one(*after(up_terms, da))
    heads = lambda part, mixed, lse, own: attend_back_part(
        meta, part, qkv, mixed, lse, seg_column, seg_row, own, da_other, qkv_pieces
    )
    dqkv_one, qv_sums_one = heads(0, mixed_one, lse_one, da)
    down_sums = add_two(*down_sums, dqkv_one)
    dqkv_one = after(dqkv_one, down_sums)
    qkv_terms_one = weigh_qkv(meta, hidden, dqkv_one, (mixed_one, mixed_two, da, da_other))
    up_sums = add_one(*up_sums, qkv_terms_one)
    dqkv_two, qv_sums_two = heads(1, mixed_two, lse_two, after(da, qkv_terms_one, up_sums))
    down_sums = add_three(*scatter_three(*down_sums), dqkv_two)
    up_sums = add_two(*scatter_two(*up_sums), dqkv_two)
    qkv_sums_one = add_one(*scatter_one(*qkv_terms_one), dqkv_two)
    dqkv_two = after(dqkv_two, up_sums, qkv_sums_one, down_sums)
    away, mine = qkv_back(meta, (dqkv_one, dqkv_two), qkv_pieces)
    received = send(away, PAIR)
    qkv_sums_one = add_two(*scatter_two(*qkv_sums_one), mine)
    up_sums = add_three(*scatter_three(*up_sums), mine)
    down_share = scatter_four(*down_sums, mine)
    qkv_terms_two = weigh_qkv(meta, hidden, after(dqkv_two, mine, qkv_sums_one))
    qkv_sums_one = add_three(*scatter_three(*qkv_sums_one), qkv_terms_two)
    input_low, embed_sums = last_sum(meta, resid_one, after(mine, qkv_terms_two), received)
    input_grad = give_rows(input_low)
    up_share = scatter_four(*up_sums, input_low)
    qkv_sums_two = add_two(*scatter_two(*add_one(*scatter_one(*qkv_terms_two), input_low)))
    qkv_sums_two = add_three(*scatter_three(*qkv_sums_two))
    qkv_share_one = scatter_four(*qkv_sums_one, input_low)
    qkv_share_two = scatter_four(*after(qkv_sums_two, input_grad))
    qkv_share = jnp.concatenate([qkv_share_one[:6], qkv_share_two], axis=2)
    qv_sums = jnp.concatenate([qv_sums_one[0:2], qv_sums_two[0:2]], axis=1)

    def both_halves(own, received):
        return jnp.where(c == 0, jnp.stack([own, received], axis=-2), jnp.stack([received, own], axis=-2))

    grad_down = down_share.transpose(1, 0, 2).reshape(128, 1024)
    grad_out = qkv_share_one[6:].transpose(1, 0, 2).reshape(32, 1024)
    grad_up = both_halves(up_share[:4], send(up_share[4:], PAIR))
    grad_up = grad_up.transpose(1, 0, 2, 3).reshape(32, 4096)
    split = lambda share: share.reshape(3, 32, 4, 128)
    grad_qkv = both_halves(split(qkv_share[:3]), split(send(qkv_share[3:], PAIR)))
    grad_qkv = grad_qkv.transpose(1, 0, 2, 3, 4).reshape(32, 3072)

    qv_sums, bias_sums, sums_one, sums_two = after((qv_sums, bias_sums, sums_one, sums_two), input_low)
    core_lane = (jnp.arange(2) == c).astype(F32)
    spread = lambda sums, width: (sums.reshape(-1, 1, width) * core_lane[None, :, None]).reshape(32, -1)
    grads = jnp.concatenate(
        [
            spread(qv_sums, 128),
            sums_one[2].reshape(32, 32),
            sums_one[0].reshape(32, 32),
            sums_one[1].reshape(32, 32),
            spread(bias_sums[0:1], 512),
            sums_two[2].reshape(32, 32),
            sums_two[0].reshape(32, 32),
            sums_two[1].reshape(32, 32),
        ],
        axis=1,
    )
    total = jnp.dot(order.astype(F32), grads, precision=lax.Precision.HIGHEST)
    total = total.reshape(4, 2, 4, 3, 128).transpose(1, 0, 2, 3, 4).reshape(96, 128)
    sums = embed_sums[0:1].reshape(8, 128)
    received = send(jnp.concatenate([total[48:], sums]), PAIR)
    total, sums = total[:48] + received[:48], sums + received[48:]
    for width, pairs in ((24, ALONG_Y), (12, ALONG_X), (6, ALONG_Z[2]), (3, ALONG_Z[1])):
        message = jnp.concatenate([total[width:], sums])
        received = send(after(message, input_grad) if width == 6 else message, pairs)
        total, sums = total[:width] + received[:width], jnp.concatenate([sums, received[width:]])
    small_grads = [part.reshape(-1) for part in split_vectors(total.reshape(1, 384))]
    sums = sums.reshape(2, 2, 2, 2, 1024).transpose(3, 2, 1, 0, 4).reshape(16, 1024)
    grad_time = jnp.dot(features.astype(F32).T, sums, precision=lax.Precision.HIGHEST)

    return (
        output,
        input_grad,
        grad_time,
        grad_qkv,
        small_grads[0],
        grad_out,
        *small_grads[1:4],
        grad_up,
        small_grads[4],
        grad_down,
        *small_grads[5:],
    )


def solution(mesh):
    in_specs = (
        P("dp", "sp", None),
        P("dp"),
        P("dp", "sp"),
        P("dp", "sp", None),
        P(("dp", "sp"), None),
        P(("dp", "sp"), None),
        P(("dp", "sp")),
        P(("dp", "sp"), None),
        P(("dp", "sp")),
        P(("dp", "sp")),
        P(("dp", "sp")),
        P(("dp", "sp"), None),
        P(("dp", "sp")),
        P(("dp", "sp"), None),
        P(("dp", "sp")),
        P(("dp", "sp")),
        P(("dp", "sp")),
    )
    out_specs = (
        P("dp", "sp", None),
        P("dp", "sp", None),
        P(("dp", "sp"), None),
        P(("dp", "sp"), None),
        P(("dp", "sp")),
        P(("dp", "sp"), None),
        P(("dp", "sp")),
        P(("dp", "sp")),
        P(("dp", "sp")),
        P(("dp", "sp"), None),
        P(("dp", "sp")),
        P(("dp", "sp"), None),
        P(("dp", "sp")),
        P(("dp", "sp")),
        P(("dp", "sp")),
    )
    plan = chip_body if dict(mesh.shape) == {"dp": 8, "sp": 4} else body
    return jax.shard_map(plan, mesh=mesh, in_specs=in_specs, out_specs=out_specs, check_vma=False)
```

```python
import math

import jax
import jax.numpy as jnp
from jax import lax
from jax.experimental import pallas as pl
from jax.experimental.pallas import tpu as pltpu
from jax.sharding import PartitionSpec as P

HEADS = 16
HEAD_DIM = 64


EPSILON = 1e-05
INVERSE_ROOT_TWO = 1.0 / math.sqrt(2.0)
INVERSE_ROOT_TWO_PI = 1.0 / math.sqrt(2.0 * math.pi)


def time_features(stamps, model_width):
    halfway = model_width // 2
    frequency = jnp.exp(-math.log(10000.0) * jnp.arange(halfway, dtype=jnp.float32) / halfway)
    phases = stamps.astype(jnp.float32)[:, None] * frequency[None, :]
    return jnp.concatenate([jnp.sin(phases), jnp.cos(phases)], axis=1)


def layer_norm_parts(values, gain, offset):
    center = values - jnp.mean(values, axis=-1, keepdims=True)
    variance = jnp.mean(center * center, axis=-1, keepdims=True)
    inverse = lax.rsqrt(variance + EPSILON)
    normal_part = center * inverse
    return (normal_part * gain + offset, normal_part, inverse)


def layer_norm_back(upstream, normal_part, inverse, gain):
    scaled = upstream * gain
    return inverse * (
        scaled
        - jnp.mean(scaled, axis=-1, keepdims=True)
        - normal_part * jnp.mean(scaled * normal_part, axis=-1, keepdims=True)
    )


def gelu_slope(values):
    cumulative = 0.5 * (1.0 + lax.erf(values * INVERSE_ROOT_TWO))
    density = jnp.exp(-0.5 * values * values) * INVERSE_ROOT_TWO_PI
    return cumulative + values * density


def contract_rows(left, right):
    return lax.dot_general(
        left, right, (((0,), (0,)), ((), ())), preferred_element_type=jnp.float32
    )


def times_transposed(left, right):
    return lax.dot_general(
        left, right, (((1,), (1,)), ((), ())), preferred_element_type=jnp.float32
    )


def flatten_grads(grads):
    return tuple((grad.reshape(-1, 128) if grad.ndim == 2 else grad for grad in grads))


def restore_grads(shares, templates):
    return tuple((share.reshape(template.shape) for share, template in zip(shares, templates)))


def attention_forward(queries, keys_all, values_all, seg_full, query_block, scale):
    block_count = queries.shape[1] // query_block

    def one_block(index):
        start = index * query_block
        query_part = lax.dynamic_slice_in_dim(queries, start, query_block, 1)
        seg_part = lax.dynamic_slice_in_dim(seg_full, start, query_block, 1)
        scores = (
            jnp.einsum("rqhd,rkhd->rhqk", query_part, keys_all, preferred_element_type=jnp.float32)
            * scale
        )
        allowed = seg_part[:, None, :, None] == seg_full[:, None, None, :]
        scores = jnp.where(allowed, scores, -1e30)
        largest = jnp.max(scores, axis=-1, keepdims=True)
        exponent = jnp.exp(scores - largest)
        totals = jnp.sum(exponent, axis=-1, keepdims=True)
        probability = exponent / totals
        log_total = largest[..., 0] + jnp.log(totals[..., 0])
        mixed = jnp.einsum(
            "rhqk,rkhd->rqhd",
            probability.astype(jnp.bfloat16),
            values_all,
            preferred_element_type=jnp.float32,
        )
        return (mixed, log_total)

    mixed_blocks, log_totals = lax.map(one_block, jnp.arange(block_count, dtype=jnp.int32))
    mixed = jnp.moveaxis(mixed_blocks, 0, 1).reshape(queries.shape)
    return (mixed, log_totals)


def attention_backward(
    queries, keys_all, values_all, seg_full, grad_heads, log_totals, query_block, scale
):
    block_count = queries.shape[1] // query_block

    def one_block(carry, index):
        key_grad, value_grad = carry
        start = index * query_block
        query_part = lax.dynamic_slice_in_dim(queries, start, query_block, 1)
        seg_part = lax.dynamic_slice_in_dim(seg_full, start, query_block, 1)
        grad_part = lax.dynamic_slice_in_dim(grad_heads, start, query_block, 1)
        scores = (
            jnp.einsum("rqhd,rkhd->rhqk", query_part, keys_all, preferred_element_type=jnp.float32)
            * scale
        )
        allowed = seg_part[:, None, :, None] == seg_full[:, None, None, :]
        scores = jnp.where(allowed, scores, -1e30)
        probability = jnp.exp(scores - log_totals[index][..., None])
        dotted = jnp.einsum(
            "rqhd,rkhd->rhqk", grad_part, values_all, preferred_element_type=jnp.float32
        )
        center = jnp.sum(probability * dotted, axis=-1, keepdims=True)
        score_grad = (probability * (dotted - center)).astype(jnp.bfloat16)
        query_grad = (
            jnp.einsum("rhqk,rkhd->rqhd", score_grad, keys_all, preferred_element_type=jnp.float32)
            * scale
        )
        key_grad = (
            key_grad
            + jnp.einsum(
                "rhqk,rqhd->rkhd", score_grad, query_part, preferred_element_type=jnp.float32
            )
            * scale
        )
        value_grad = value_grad + jnp.einsum(
            "rhqk,rqhd->rkhd",
            probability.astype(jnp.bfloat16),
            grad_part,
            preferred_element_type=jnp.float32,
        )
        return ((key_grad, value_grad), query_grad)

    starting = (jnp.zeros(keys_all.shape, jnp.float32), jnp.zeros(values_all.shape, jnp.float32))
    (key_grad, value_grad), query_blocks = lax.scan(
        one_block, starting, jnp.arange(block_count, dtype=jnp.int32)
    )
    query_grad = jnp.moveaxis(query_blocks, 0, 1).reshape(queries.shape)
    return (query_grad, key_grad, value_grad)


def body(
    tokens,
    timestep,
    segment_ids,
    cotangent,
    time_weight,
    qkv_weight,
    qv_bias,
    out_weight,
    out_bias,
    norm_gain,
    norm_bias,
    up_weight,
    up_bias,
    down_weight,
    down_bias,
    final_gain,
    final_bias,
):
    shards = (
        time_weight,
        qkv_weight,
        qv_bias,
        out_weight,
        out_bias,
        norm_gain,
        norm_bias,
        up_weight,
        up_bias,
        down_weight,
        down_bias,
        final_gain,
        final_bias,
    )
    sp_count = lax.axis_size("sp")
    micro_count = max(2, sp_count // 2)
    rows_local, piece_len, model_width = tokens.shape
    rows_micro = rows_local // micro_count
    seq_len = piece_len * sp_count
    width_local = model_width // sp_count
    heads_local = HEADS // sp_count
    query_block = min(512, seq_len)
    scale = 1.0 / math.sqrt(HEAD_DIM)
    tok_count = rows_micro * piece_len
    owned = tuple((jnp.zeros(piece.shape, jnp.float32) for piece in shards))
    output_parts = []
    input_parts = []
    for micro in range(micro_count):
        first_row = micro * rows_micro
        block_tokens = tokens[first_row : first_row + rows_micro]
        block_cotangent = cotangent[first_row : first_row + rows_micro]
        block_segments = segment_ids[first_row : first_row + rows_micro]
        block_stamps = timestep[first_row : first_row + rows_micro]
        gathered = (
            lax.all_gather(shards[0], ("dp", "sp"), axis=0, tiled=True),
            lax.all_gather(shards[1], ("dp", "sp"), axis=0, tiled=True),
            lax.all_gather(shards[2], ("dp", "sp"), axis=0, tiled=True),
            lax.all_gather(shards[3], ("dp", "sp"), axis=0, tiled=True),
            lax.all_gather(shards[4], ("dp", "sp"), axis=0, tiled=True),
            lax.all_gather(shards[5], ("dp", "sp"), axis=0, tiled=True),
            lax.all_gather(shards[6], ("dp", "sp"), axis=0, tiled=True),
            lax.all_gather(shards[7], ("dp", "sp"), axis=0, tiled=True),
            lax.all_gather(shards[8], ("dp", "sp"), axis=0, tiled=True),
            lax.all_gather(shards[9], ("dp", "sp"), axis=0, tiled=True),
            lax.all_gather(shards[10], ("dp", "sp"), axis=0, tiled=True),
            lax.all_gather(shards[11], ("dp", "sp"), axis=0, tiled=True),
            lax.all_gather(shards[12], ("dp", "sp"), axis=0, tiled=True),
        )
        (
            time_full,
            qkv_full,
            qv_full,
            out_full,
            out_shift,
            first_gain,
            first_shift,
            up_full,
            up_shift,
            down_full,
            down_shift,
            second_gain,
            second_shift,
        ) = gathered
        features = time_features(block_stamps, model_width).astype(jnp.bfloat16)
        embedded = jnp.dot(features, time_full, preferred_element_type=jnp.float32)
        hidden = block_tokens.astype(jnp.float32) + embedded[:, None, :]
        hidden_flat = hidden.reshape(tok_count, model_width)
        hidden_low = hidden_flat.astype(jnp.bfloat16)
        qv_float = qv_full.astype(jnp.float32)
        qkv_shift = jnp.concatenate(
            [qv_float[:model_width], jnp.zeros((model_width,), jnp.float32), qv_float[model_width:]]
        )
        packed = jnp.dot(hidden_low, qkv_full, preferred_element_type=jnp.float32) + qkv_shift
        packed = packed.astype(jnp.bfloat16).reshape(rows_micro, piece_len, 3, model_width)
        seg_copies = jnp.broadcast_to(
            block_segments[:, :, None, None], (rows_micro, piece_len, 1, sp_count)
        )
        packed_heads, seg_heads = (
            lax.all_to_all(packed, "sp", split_axis=3, concat_axis=1, tiled=True),
            lax.all_to_all(seg_copies, "sp", split_axis=3, concat_axis=1, tiled=True),
        )
        seg_full = seg_heads[:, :, 0, 0]
        head_shape = (rows_micro, seq_len, heads_local, HEAD_DIM)
        queries = packed_heads[:, :, 0].reshape(head_shape)
        keys_all = packed_heads[:, :, 1].reshape(head_shape)
        values_all = packed_heads[:, :, 2].reshape(head_shape)
        mixed, log_totals = attention_forward(
            queries, keys_all, values_all, seg_full, query_block, scale
        )
        mixed_low = mixed.astype(jnp.bfloat16).reshape(rows_micro, seq_len, width_local)
        mixed_local = lax.all_to_all(mixed_low, "sp", split_axis=1, concat_axis=2, tiled=True)
        mixed_flat = mixed_local.reshape(tok_count, model_width)
        attended = jnp.dot(
            mixed_flat, out_full, preferred_element_type=jnp.float32
        ) + out_shift.astype(jnp.float32)
        first_gain_f = first_gain.astype(jnp.float32)
        normed, normal_one, inverse_one = layer_norm_parts(
            hidden_flat + attended, first_gain_f, first_shift.astype(jnp.float32)
        )
        normed_low = normed.astype(jnp.bfloat16)
        upward = jnp.dot(normed_low, up_full, preferred_element_type=jnp.float32) + up_shift.astype(
            jnp.float32
        )
        activated = jax.nn.gelu(upward, approximate=False).astype(jnp.bfloat16)
        downward = jnp.dot(
            activated, down_full, preferred_element_type=jnp.float32
        ) + down_shift.astype(jnp.float32)
        second_gain_f = second_gain.astype(jnp.float32)
        result, normal_two, inverse_two = layer_norm_parts(
            normed + downward, second_gain_f, second_shift.astype(jnp.float32)
        )
        output_parts.append(result.astype(jnp.bfloat16).reshape(rows_micro, piece_len, model_width))
        upstream = block_cotangent.reshape(tok_count, model_width).astype(jnp.float32)
        grad_second_gain = jnp.sum(upstream * normal_two, axis=0)
        grad_second_shift = jnp.sum(upstream, axis=0)
        resid_two = layer_norm_back(upstream, normal_two, inverse_two, second_gain_f)
        down_grad = resid_two.astype(jnp.bfloat16)
        grad_down_shift = jnp.sum(down_grad, axis=0, dtype=jnp.float32)
        grad_down_full = contract_rows(activated, down_grad)
        act_grad = times_transposed(down_grad, down_full)
        up_grad = (act_grad * gelu_slope(upward)).astype(jnp.bfloat16)
        grad_up_shift = jnp.sum(up_grad, axis=0, dtype=jnp.float32)
        grad_up_full = contract_rows(normed_low, up_grad)
        normed_grad = resid_two + times_transposed(up_grad, up_full)
        grad_first_gain = jnp.sum(normed_grad * normal_one, axis=0)
        grad_first_shift = jnp.sum(normed_grad, axis=0)
        resid_one = layer_norm_back(normed_grad, normal_one, inverse_one, first_gain_f)
        attended_grad = resid_one.astype(jnp.bfloat16)
        grad_out_shift = jnp.sum(attended_grad, axis=0, dtype=jnp.float32)
        grad_out_full = contract_rows(mixed_flat, attended_grad)
        mixed_grad = times_transposed(attended_grad, out_full).astype(jnp.bfloat16)
        mixed_grad = mixed_grad.reshape(rows_micro, piece_len, model_width)
        grad_heads = lax.all_to_all(
            mixed_grad, "sp", split_axis=2, concat_axis=1, tiled=True
        ).reshape(head_shape)
        query_grad, key_grad, value_grad = attention_backward(
            queries, keys_all, values_all, seg_full, grad_heads, log_totals, query_block, scale
        )
        packed_grad = jnp.stack([query_grad, key_grad, value_grad], axis=2)
        packed_grad = packed_grad.reshape(rows_micro, seq_len, 3, width_local).astype(jnp.bfloat16)
        packed_local = lax.all_to_all(packed_grad, "sp", split_axis=1, concat_axis=3, tiled=True)
        packed_flat = packed_local.reshape(tok_count, 3 * model_width)
        third_sums = jnp.sum(packed_flat, axis=0, dtype=jnp.float32)
        grad_qv_full = jnp.concatenate([third_sums[:model_width], third_sums[2 * model_width :]])
        grad_qkv_full = contract_rows(hidden_low, packed_flat)
        hidden_grad = resid_one + times_transposed(packed_flat, qkv_full)
        input_parts.append(
            hidden_grad.astype(jnp.bfloat16).reshape(rows_micro, piece_len, model_width)
        )
        embed_grad = jnp.sum(hidden_grad.reshape(rows_micro, piece_len, model_width), axis=1)
        grad_time_full = jnp.dot(
            features.astype(jnp.float32).T, embed_grad, precision=lax.Precision.HIGHEST
        )
        grads = (
            grad_time_full,
            grad_qkv_full,
            grad_qv_full,
            grad_out_full,
            grad_out_shift,
            grad_first_gain,
            grad_first_shift,
            grad_up_full,
            grad_up_shift,
            grad_down_full,
            grad_down_shift,
            grad_second_gain,
            grad_second_shift,
        )
        shares = lax.psum_scatter(
            flatten_grads(grads), ("dp", "sp"), scatter_dimension=0, tiled=True
        )
        owned = jax.tree.map(jnp.add, owned, restore_grads(shares, owned))
    output = jnp.concatenate(output_parts, axis=0)
    input_grad = jnp.concatenate(input_parts, axis=0)
    return (
        output,
        input_grad,
        owned[0],
        owned[1],
        owned[2],
        owned[3],
        owned[4],
        owned[5],
        owned[6],
        owned[7],
        owned[8],
        owned[9],
        owned[10],
        owned[11],
        owned[12],
    )


AXES = ("dp", "sp")
BF = jnp.bfloat16
F32 = jnp.float32
NT = (((1,), (1,)), ((), ()))
TN = (((0,), (0,)), ((), ()))
NN = (((1,), (0,)), ((), ()))
VMEM_LIMIT = 58 * 1024 * 1024
CHIP_SLOTS = (
    ((0, 0, 0), (0, 0, 1)),
    ((0, 1, 0), (0, 1, 1)),
    ((1, 0, 0), (1, 1, 0)),
    ((1, 0, 1), (1, 1, 1)),
)


def dot(left, right, dims=NN):
    return lax.dot_general(left, right, dims, preferred_element_type=F32)


def device_perm(target):
    pairs = []
    for y in range(2):
        for x in range(2):
            for c in range(2):
                for z in range(4):
                    ty, tx, tc, tz = target(y, x, c, z)
                    source = ((y * 2 + x) * 2 + c) * 4 + z
                    pairs.append((source, ((ty * 2 + tx) * 2 + tc) * 4 + tz))
    return pairs


PAIR = device_perm(lambda y, x, c, z: (y, x, 1 - c, z))
ALONG_X = device_perm(lambda y, x, c, z: (y, 1 - x, c, z))
ALONG_Y = device_perm(lambda y, x, c, z: (1 - y, x, c, z))
ALONG_Z = [device_perm(lambda y, x, c, z, k=k: (y, x, c, z ^ k)) for k in range(3)]
ROW_OUT = [device_perm(lambda y, x, c, z, k=k: (y, x, z // 2, c * 2 + (z + k) % 2)) for k in range(2)]
ROW_BACK = [[(t, s) for s, t in pairs] for pairs in ROW_OUT]


def send(value, pairs):
    return lax.ppermute(value, AXES, pairs)


def after(value, *earlier):
    return lax.optimization_barrier((value, earlier))[0]


def gather_line(shard):
    first = jnp.stack([shard, send(shard, ALONG_Z[2])])
    return first, send(first, ALONG_Z[1])


def gather_plane(first, second, *earlier):
    first_x, second_y = lax.optimization_barrier((send(first, ALONG_X), send(second, ALONG_Y)))
    first, second = jnp.stack([after(first, earlier), first_x]), jnp.stack([after(second, earlier), second_y])
    return [first, send(first, ALONG_Y), second, send(second, ALONG_X)]


def gather_near(half):
    return send(half, ALONG_X), send(half, ALONG_Y)


def gather_far(first, first_near, second, second_near):
    first_far, second_far = send(first_near[0], ALONG_Y), send(second_near[1], ALONG_X)
    return [first, *first_near, first_far, second, second_near[1], second_near[0], second_far]


def add_low(a, b):
    return (a.astype(F32) + b.astype(F32)).astype(BF)


def scatter_one(first_keep, first_send, second_keep, second_send):
    return first_keep, send(first_send, ALONG_Y), second_keep, send(second_send, ALONG_X)


def add_one(first_keep, from_y, second_keep, from_x, *earlier):
    first_keep, second_keep = after((first_keep, second_keep), earlier)
    to_x, to_y = add_low(first_keep[1], from_y[1]), add_low(second_keep[1], from_x[1])
    return add_low(first_keep[0], from_y[0]), to_x, add_low(second_keep[0], from_x[0]), to_y


def scatter_two(first, to_x, second, to_y):
    return first, send(to_x, ALONG_X), second, send(to_y, ALONG_Y)


def add_two(first, from_x, second, from_y, *earlier):
    first, second = after((first, second), earlier)
    return add_low(first, from_x), add_low(second, from_y)


def scatter_three(first, second):
    return first, send(second, ALONG_Z[1])


def add_three(first, received, *earlier):
    first = after(first, earlier)
    return add_low(first[0], received[0]), add_low(first[1], received[1])


def scatter_four(near, far, *earlier):
    return after(near, earlier).astype(F32) + send(far, ALONG_Z[2]).astype(F32)


def z_relative(half, j):
    return 2 * j + half


def place(meta, slot, at, j):
    half, y_rel, x_rel = CHIP_SLOTS[slot][at]
    chip = (meta[0] ^ y_rel) * 2 + (meta[1] ^ x_rel)
    return chip, meta[3] ^ z_relative(half, j)


def load_all(copies):
    for copy in copies:
        copy.start()
    for copy in copies:
        copy.wait()


def load_qkv(meta, refs, weight, sem):
    copies = []
    for slot, ref in enumerate(refs):
        for at in range(2):
            for j in range(2):
                chip, z = place(meta, slot, at, j)
                for other in range(2):
                    row = pl.multiple_of((chip * 2 + (meta[2] ^ other)) * 128 + z * 32, 32)
                    for t in range(3):
                        copies.append(
                            pltpu.make_async_copy(
                                ref.at[at, j, pl.ds((other * 3 + t) * 32, 32)],
                                weight.at[t, pl.ds(row, 32), :],
                                sem.at[len(copies)],
                            )
                        )
    return copies


def load_split_rows(meta, refs, base, blocks, weight, sem):
    copies = []
    for n, ref in enumerate(refs):
        for j in range(2):
            chip, z = place(meta, n // 2, n % 2, j)
            for other in range(2):
                row = pl.multiple_of((chip * 2 + (meta[2] ^ other)) * 128 + z * 32, 32)
                copies.append(
                    pltpu.make_async_copy(
                        ref.at[j, pl.ds(base + other * blocks, blocks)],
                        weight.at[:, pl.ds(row, 32), :],
                        sem.at[len(copies)],
                    )
                )
    return copies


def load_out(meta, refs, weight, sem):
    copies = []
    for slot, ref in enumerate(refs):
        for at in range(2):
            for j in range(2):
                chip, z = place(meta, slot, at, j)
                row = pl.multiple_of((chip * 4 + z) * 32, 32)
                for b in range(2):
                    copies.append(
                        pltpu.make_async_copy(
                            ref.at[at, j, pl.ds(192 + b * 32, 32)],
                            weight.at[b, pl.ds(row, 32), :],
                            sem.at[len(copies)],
                        )
                    )
    return copies


def load_own_rows(meta, refs, base, blocks, rows, weight, sem):
    copies = []
    for slot, ref in enumerate(refs):
        for at in range(2):
            for j in range(2):
                chip, z = place(meta, slot, at, j)
                row = pl.multiple_of((chip * 4 + z) * rows, 32)
                copies.append(
                    pltpu.make_async_copy(
                        ref.at[at, j, pl.ds(base, blocks)],
                        weight.at[:, pl.ds(row, rows), :],
                        sem.at[len(copies)],
                    )
                )
    return copies


def kernel_call(kernel, meta, operands, in_specs, out_specs, out_shape, scratch=(), grid=(4,), flops=0, moved=0, exps=0):
    return pl.pallas_call(
        kernel,
        grid_spec=pltpu.PrefetchScalarGridSpec(
            num_scalar_prefetch=1,
            grid=grid,
            in_specs=in_specs,
            out_specs=out_specs,
            scratch_shapes=list(scratch),
        ),
        out_shape=out_shape,
        compiler_params=pltpu.CompilerParams(vmem_limit_bytes=VMEM_LIMIT),
        cost_estimate=pl.CostEstimate(
            flops=int(flops * 1.5), bytes_accessed=int(moved * 1.5), transcendentals=int(exps * 1.5)
        ),
    )(meta, *operands)


HBM = pl.BlockSpec(memory_space=pl.ANY)


def spec(shape, index):
    return pl.BlockSpec(shape, index)


def whole(shape):
    return pl.BlockSpec(shape, lambda i, m: (0,) * len(shape))


def shaped(shape, kind):
    return jax.ShapeDtypeStruct(shape, kind)


def low_block(i):
    return jnp.minimum(i, 1)


def high_block(i):
    return jnp.maximum(i - 2, 0)


def turned(i):
    return lax.rem(i + 2, 4)


def project_qkv(meta, own, other, embedded, shift, pieces):
    def kernel(m, own_ref, other_ref, emb_ref, shift_ref, *rest):
        refs, (hidden_ref, out_ref, weight, sem) = rest[:4], rest[4:]
        i = pl.program_id(0)

        @pl.when(i == 0)
        def _():
            load_all(load_qkv(m, refs, weight, sem))

        tokens = jnp.where(i < 2, own_ref[0].astype(F32), other_ref[0].astype(F32))
        hidden = (tokens + emb_ref[...]).astype(BF)
        hidden_ref[...] = hidden
        for t in range(3):
            out_ref[t] = (dot(hidden, weight[t]) + shift_ref[t : t + 1, :]).astype(BF)

    return kernel_call(
        kernel,
        meta,
        (own, other, embedded, shift, *pieces),
        [
            spec((1, 256, 1024), lambda i, m: (low_block(i), 0, 0)),
            spec((1, 256, 1024), lambda i, m: (high_block(i), 0, 0)),
            whole((1, 1024)),
            whole((3, 512)),
        ]
        + [HBM] * 4,
        [spec((256, 1024), lambda i, m: (i, 0)), spec((3, 256, 512), lambda i, m: (0, i, 0))],
        [shaped((1024, 1024), BF), shaped((3, 1024, 512), BF)],
        [pltpu.VMEM((3, 1024, 512), BF), pltpu.SemaphoreType.DMA((96,))],
        flops=2 * 1024 * 1024 * 1536,
        moved=10 << 20,
    )


def head_lanes(h, kind):
    lane = lax.broadcasted_iota(jnp.int32, (1, 128), 1)
    return jnp.where(lane // HEAD_DIM == h, 1.0, 0.0).astype(kind)


def attend(meta, part, qkv, seg_column, seg_row):
    def kernel(m, q_ref, k_ref, v_ref, column_ref, row_ref, out_ref, lse_ref):
        queries, keys, values = q_ref[0] * jnp.asarray(0.125, BF), k_ref[0], v_ref[0]
        allowed = column_ref[...] == row_ref[...]
        mixed = jnp.zeros((128, 1024), F32)
        for h in range(2):
            lanes = head_lanes(h, BF)
            scores = jnp.where(allowed, dot(keys * lanes, queries, NT), -1e30)
            largest = jnp.max(scores, axis=0, keepdims=True)
            exponent = jnp.exp(scores - largest)
            total = jnp.sum(exponent, axis=0, keepdims=True)
            mixed += dot(values * lanes, exponent.astype(BF), TN) / total
            lse_ref[0, h : h + 1, :] = largest + jnp.log(total)
        out_ref[...] = jnp.transpose(mixed).astype(BF)

    base = part * 2
    third = lambda t: spec((1, 1024, 128), lambda i, m: (t, 0, base + i))
    return kernel_call(
        kernel,
        meta,
        (qkv, qkv, qkv, seg_column, seg_row),
        [third(0), third(1), third(2), whole((1024, 1)), whole((1, 1024))],
        [spec((1024, 128), lambda i, m: (0, i)), spec((1, 8, 1024), lambda i, m: (i, 0, 0))],
        [shaped((1024, 256), BF), shaped((2, 8, 1024), F32)],
        grid=(2,),
        flops=8 * 4 * 1024 * 1024 * 256,
        moved=5 << 20,
        exps=8 << 20,
    )


def attend_back(i, q_ref, k_ref, v_ref, out_ref, lse_ref, column_ref, row_ref, d_ref, sum_ref, dout, prob, ds):
    columns = pl.ds(pl.multiple_of(i * 128, 128), 128)
    queries, upstream = q_ref[0], dout[:, columns]
    product = out_ref[...].astype(F32) * upstream.astype(F32)
    row = lax.broadcasted_iota(jnp.int32, (8, 128), 0)
    lane = lax.broadcasted_iota(jnp.int32, (8, 128), 1)
    picked = jnp.where(lane // HEAD_DIM == row, 1.0, 0.0).astype(F32)
    center = lax.dot_general(picked, product, NT, precision=lax.Precision.HIGHEST, preferred_element_type=F32)
    dq, dk, dv = (jnp.zeros((1024, 128), F32) for _ in range(3))
    for h in range(2):
        lanes = head_lanes(h, BF)
        for block in range(4):
            rows = pl.ds(block * 256, 256)
            allowed = column_ref[rows, :] == row_ref[...]
            scores = dot(k_ref[0, rows, :] * lanes * jnp.asarray(0.125, BF), queries, NT)
            p = jnp.where(allowed, jnp.exp(scores - lse_ref[0, h : h + 1, :]), 0.0)
            dp = dot(v_ref[0, rows, :] * lanes, upstream, NT)
            prob[rows, :] = p.astype(BF)
            ds[rows, :] = (p * (dp - center[h : h + 1, :])).astype(BF)
        dv += dot(prob[...], upstream * lanes)
        dk += dot(ds[...], queries * lanes)
        dq += dot(ds[...], k_ref[0] * lanes, TN)
    dq, dk, dv = (dq * 0.125).astype(BF), (dk * 0.125).astype(BF), dv.astype(BF)
    d_ref[0, :, columns], d_ref[1, :, columns], d_ref[2, :, columns] = dq, dk, dv
    sum_ref[0:1, columns] = jnp.sum(dq.astype(F32), axis=0, keepdims=True)
    sum_ref[1:2, columns] = jnp.sum(dv.astype(F32), axis=0, keepdims=True)


def heads_out(part, own_ref, other_ref, weight, dout):
    rows = pl.ds(part * 256, 256)
    for half, ref in enumerate((own_ref, other_ref)):
        da = ref[...]
        result = dot(da[:, :512], weight[0, rows, :], NT) + dot(da[:, 512:], weight[1, rows, :], NT)
        dout[pl.ds(half * 512, 512), :] = result.astype(BF)


def attend_specs(part):
    pair = lambda i: jnp.minimum(i, 1)
    third = lambda t: spec((1, 1024, 128), lambda i, m: (t, 0, part * 2 + pair(i)))
    return [
        third(0),
        third(1),
        third(2),
        spec((1024, 128), lambda i, m: (0, pair(i))),
        spec((1, 8, 1024), lambda i, m: (pair(i), 0, 0)),
        whole((1024, 1)),
        whole((1, 1024)),
        whole((512, 1024)),
        whole((512, 1024)),
    ]


ATTEND_SCRATCH = (
    pltpu.VMEM((2, 512, 512), BF),
    pltpu.VMEM((1024, 256), BF),
    pltpu.VMEM((1024, 1024), BF),
    pltpu.VMEM((1024, 1024), BF),
    pltpu.SemaphoreType.DMA((32,)),
)


def attend_back_part(meta, part, qkv, mixed, lse, seg_column, seg_row, da_own, da_other, pieces):
    def kernel(m, q_ref, k_ref, v_ref, out_ref, lse_ref, column_ref, row_ref, own_ref, other_ref, *rest):
        refs, (d_ref, sum_ref), (weight, dout, prob, ds, sem) = rest[:4], rest[4:6], rest[6:]
        i = pl.program_id(0)

        @pl.when(i == 0)
        def _():
            load_all(load_out(m, refs, weight, sem))
            heads_out(part, own_ref, other_ref, weight, dout)

        attend_back(i, q_ref, k_ref, v_ref, out_ref, lse_ref, column_ref, row_ref, d_ref, sum_ref, dout, prob, ds)

    return kernel_call(
        kernel,
        meta,
        (qkv, qkv, qkv, mixed, lse, seg_column, seg_row, da_own, da_other, *pieces),
        attend_specs(part) + [HBM] * 4,
        [whole((3, 1024, 256)), whole((8, 256))],
        [shaped((3, 1024, 256), BF), shaped((8, 256), F32)],
        ATTEND_SCRATCH,
        grid=(2,),
        flops=11 * 10**9,
        moved=10 << 20,
        exps=4 << 20,
    )


def project_out(meta, mixed, pieces):
    def kernel(m, x_ref, w_ref, *rest):
        refs, (send_ref, own_ref, weight, sem) = rest[:4], rest[4:]
        i = pl.program_id(0)

        @pl.when(i == 0)
        def _():
            load_all(load_out(m, refs, weight, sem))

        for b in range(2):
            columns = pl.ds(b * 512, 512)
            result = dot(x_ref[...], weight[b, :256, :]) + dot(w_ref[...], weight[b, 256:, :])

            @pl.when(i < 2)
            def _():
                send_ref[:, columns] = result.astype(BF)

            @pl.when(i >= 2)
            def _():
                own_ref[:, columns] = result

    return kernel_call(
        kernel,
        meta,
        (*mixed, *pieces),
        [spec((256, 256), lambda i, m: (turned(i), 0))] * 2 + [HBM] * 4,
        [spec((256, 1024), lambda i, m: (low_block(i), 0)), spec((256, 1024), lambda i, m: (high_block(i), 0))],
        [shaped((512, 1024), BF), shaped((512, 1024), F32)],
        [pltpu.VMEM((2, 512, 512), BF), pltpu.SemaphoreType.DMA((32,))],
        flops=2 * 1024 * 1024 * 512,
        moved=6 << 20,
    )


def normal_parts(values):
    center = values - jnp.mean(values, axis=-1, keepdims=True)
    inverse = lax.rsqrt(jnp.mean(center * center, axis=-1, keepdims=True) + EPSILON)
    return center * inverse, inverse


def normal_back(upstream, normal_part, inverse, gain):
    scaled = upstream * gain
    return inverse * (
        scaled
        - jnp.mean(scaled, axis=-1, keepdims=True)
        - normal_part * jnp.mean(scaled * normal_part, axis=-1, keepdims=True)
    )


BY_ROWS = lambda i, m: (i, 0)


def first_norm(meta, tokens, embedded, own, received, vectors):
    def kernel(m, tok_ref, emb_ref, own_ref, recv_ref, vec_ref, normal_ref, inverse_ref, low_ref):
        hidden = tok_ref[0].astype(F32) + emb_ref[...]
        attended = own_ref[...] + recv_ref[...].astype(F32) + vec_ref[0:1, :]
        normal_part, inverse = normal_parts(hidden + attended)
        normal_ref[...] = normal_part
        inverse_ref[...] = jnp.broadcast_to(inverse, (256, 128))
        low_ref[...] = (normal_part * vec_ref[1:2, :] + vec_ref[2:3, :]).astype(BF)

    block = spec((256, 1024), BY_ROWS)
    return kernel_call(
        kernel,
        meta,
        (tokens, embedded, own, received, vectors),
        [spec((1, 256, 1024), lambda i, m: (i, 0, 0)), whole((1, 1024)), block, block, whole((8, 1024))],
        [block, spec((256, 128), BY_ROWS), block],
        [shaped((512, 1024), F32), shaped((512, 128), F32), shaped((512, 1024), BF)],
        grid=(2,),
        flops=512 * 1024 * 12,
        moved=8 << 20,
    )


def expand(meta, own, other, shift, pieces):
    def kernel(m, own_ref, other_ref, shift_ref, *rest):
        refs, (act_ref, slope_ref, weight, sem) = rest[:8], rest[8:]
        i = pl.program_id(0)

        @pl.when(i == 0)
        def _():
            load_all(load_split_rows(m, refs, 0, 4, weight, sem))

        x = jnp.where(i < 2, own_ref[...].astype(F32), other_ref[...].astype(F32)).astype(BF)
        for b in range(4):
            columns = pl.ds(b * 512, 512)
            u = dot(x, weight[b]) + shift_ref[:, columns]
            cumulative = 0.5 * (1.0 + lax.erf(u * INVERSE_ROOT_TWO))
            act_ref[:, columns] = (u * cumulative).astype(BF)
            density = jnp.exp(-0.5 * u * u) * INVERSE_ROOT_TWO_PI
            slope_ref[:, columns] = (cumulative + u * density).astype(BF)

    return kernel_call(
        kernel,
        meta,
        (own, other, shift, *pieces),
        [
            spec((256, 1024), lambda i, m: (low_block(i), 0)),
            spec((256, 1024), lambda i, m: (high_block(i), 0)),
            whole((1, 2048)),
        ]
        + [HBM] * 8,
        [spec((256, 2048), BY_ROWS), spec((256, 2048), BY_ROWS)],
        [shaped((1024, 2048), BF), shaped((1024, 2048), BF)],
        [pltpu.VMEM((4, 1024, 512), BF), pltpu.SemaphoreType.DMA((32,))],
        flops=2 * 1024 * 1024 * 2048,
        moved=14 << 20,
        exps=4 << 20,
    )


def contract(meta, activated, pieces):
    def kernel(m, x_ref, *rest):
        refs, (send_ref, own_ref, weight, sem) = rest[:4], rest[4:]
        i = pl.program_id(0)

        @pl.when(i == 0)
        def _():
            load_all(load_own_rows(m, refs, 0, 2, 128, weight, sem))

        for b in range(2):
            columns = pl.ds(b * 512, 512)
            result = dot(x_ref[...], weight[b])

            @pl.when(i < 2)
            def _():
                send_ref[:, columns] = result.astype(BF)

            @pl.when(i >= 2)
            def _():
                own_ref[:, columns] = result

    return kernel_call(
        kernel,
        meta,
        (activated, *pieces),
        [spec((256, 2048), lambda i, m: (turned(i), 0))] + [HBM] * 4,
        [spec((256, 1024), lambda i, m: (low_block(i), 0)), spec((256, 1024), lambda i, m: (high_block(i), 0))],
        [shaped((512, 1024), BF), shaped((512, 1024), F32)],
        [pltpu.VMEM((2, 2048, 512), BF), pltpu.SemaphoreType.DMA((16,))],
        flops=2 * 1024 * 1024 * 2048,
        moved=11 << 20,
    )


def row_sums(sum_ref, i, rows):
    @pl.when(i == 0)
    def _():
        sum_ref[...] = jnp.zeros_like(sum_ref)

    for n, value in enumerate(rows):
        sum_ref[n : n + 1, :] += jnp.sum(value, axis=0, keepdims=True)


def second_norm(meta, normal_one, own, received, cotangent, vectors):
    def kernel(m, normal_ref, own_ref, recv_ref, cot_ref, vec_ref, out_ref, resid_ref, low_ref, sum_ref):
        normed = normal_ref[...] * vec_ref[1:2, :] + vec_ref[2:3, :]
        downward = own_ref[...] + recv_ref[...].astype(F32) + vec_ref[3:4, :]
        normal_part, inverse = normal_parts(normed + downward)
        out_ref[...] = (normal_part * vec_ref[4:5, :] + vec_ref[5:6, :]).astype(BF)
        upstream = cot_ref[...].astype(F32)
        resid = normal_back(upstream, normal_part, inverse, vec_ref[4:5, :])
        resid_ref[...] = resid
        low = resid.astype(BF)
        low_ref[...] = low
        row_sums(sum_ref, pl.program_id(0), (upstream * normal_part, upstream, low.astype(F32)))

    block = spec((256, 1024), BY_ROWS)
    return kernel_call(
        kernel,
        meta,
        (normal_one, own, received, cotangent, vectors),
        [block, block, block, block, whole((8, 1024))],
        [block, block, block, whole((8, 1024))],
        [shaped((512, 1024), BF), shaped((512, 1024), F32), shaped((512, 1024), BF), shaped((8, 1024), F32)],
        grid=(2,),
        flops=512 * 1024 * 30,
        moved=10 << 20,
    )


def feed_back(meta, own, other, slope, down_pieces, up_pieces):
    def kernel(m, own_ref, other_ref, slope_ref, *rest):
        down_refs, up_refs = rest[:4], rest[4:12]
        du_ref, send_ref, mine_ref, sum_ref, down, up, down_sem, up_sem = rest[12:]
        i = pl.program_id(0)

        @pl.when(i == 0)
        def _():
            load_all(
                load_own_rows(m, down_refs, 0, 2, 128, down, down_sem)
                + load_split_rows(m, up_refs, 0, 4, up, up_sem)
            )
            sum_ref[...] = jnp.zeros_like(sum_ref)

        df = jnp.where(i < 2, other_ref[...].astype(F32), own_ref[...].astype(F32)).astype(BF)
        total = jnp.zeros((256, 1024), F32)
        for b in range(4):
            rows = pl.ds(b * 512, 512)
            act = dot(df[:, :512], down[0, rows, :], NT) + dot(df[:, 512:], down[1, rows, :], NT)
            du = (act * slope_ref[:, rows].astype(F32)).astype(BF)
            du_ref[:, rows] = du
            sum_ref[0:1, rows] += jnp.sum(du.astype(F32), axis=0, keepdims=True)
            total += dot(du, up[b], NT)

        @pl.when(i < 2)
        def _():
            send_ref[...] = total.astype(BF)

        @pl.when(i >= 2)
        def _():
            mine_ref[...] = total

    return kernel_call(
        kernel,
        meta,
        (own, other, slope, *down_pieces, *up_pieces),
        [
            spec((256, 1024), lambda i, m: (high_block(i), 0)),
            spec((256, 1024), lambda i, m: (low_block(i), 0)),
            spec((256, 2048), lambda i, m: (turned(i), 0)),
        ]
        + [HBM] * 12,
        [
            spec((256, 2048), lambda i, m: (turned(i), 0)),
            spec((256, 1024), lambda i, m: (low_block(i), 0)),
            spec((256, 1024), lambda i, m: (high_block(i), 0)),
            whole((8, 2048)),
        ],
        [shaped((1024, 2048), BF), shaped((512, 1024), BF), shaped((512, 1024), F32), shaped((8, 2048), F32)],
        [
            pltpu.VMEM((2, 2048, 512), BF),
            pltpu.VMEM((4, 1024, 512), BF),
            pltpu.SemaphoreType.DMA((16,)),
            pltpu.SemaphoreType.DMA((32,)),
        ],
        flops=4 * 1024 * 1024 * 2048,
        moved=22 << 20,
    )


def first_norm_back(meta, resid, own, received, normal_one, inverse_one, vectors):
    def kernel(m, resid_ref, own_ref, recv_ref, normal_ref, inverse_ref, vec_ref, out_ref, low_ref, sum_ref):
        upstream = resid_ref[...] + own_ref[...] + recv_ref[...].astype(F32)
        normal_part = normal_ref[...]
        resid_one = normal_back(upstream, normal_part, inverse_ref[:, 0:1], vec_ref[1:2, :])
        out_ref[...] = resid_one
        low = resid_one.astype(BF)
        low_ref[...] = low
        row_sums(sum_ref, pl.program_id(0), (upstream * normal_part, upstream, low.astype(F32)))

    block = spec((256, 1024), BY_ROWS)
    return kernel_call(
        kernel,
        meta,
        (resid, own, received, normal_one, inverse_one, vectors),
        [block, block, block, block, spec((256, 128), BY_ROWS), whole((8, 1024))],
        [block, block, whole((8, 1024))],
        [shaped((512, 1024), F32), shaped((512, 1024), BF), shaped((8, 1024), F32)],
        grid=(2,),
        flops=512 * 1024 * 20,
        moved=10 << 20,
    )


def rel_chip(s, m):
    return (m[0] ^ (s // 2)) * 2 + (m[1] ^ lax.rem(s, 2))


def piece_outputs(blocks, rows, columns=512):
    shape = (2, 2, blocks, rows, columns)
    return [HBM] * 4, [shaped(shape, BF)] * 4


def push(s, outs, copy_for):
    first_keep, first_send, second_keep, second_send = outs
    slots = (
        ((first_keep, 0), (second_keep, 0)),
        ((first_keep, 1), (second_send, 0)),
        ((first_send, 0), (second_keep, 1)),
        ((first_send, 1), (second_send, 1)),
    )
    for n, (first, second) in enumerate(slots):

        @pl.when(s == n)
        def _(n=n, first=first, second=second):
            for k in range(4):
                ref, at = (first, second)[k // 2]
                for copy in copy_for(n, k, ref.at[at, k % 2]):
                    copy.start()

    @pl.when(s == 3)
    def _():
        for n, (first, second) in enumerate(slots):
            for k in range(4):
                ref, at = (first, second)[k // 2]
                for copy in copy_for(n, k, ref.at[at, k % 2]):
                    copy.wait()


def weigh_down(meta, activated, own, other):
    def kernel(m, x_ref, own_ref, other_ref, *rest):
        outs, (stage, sem) = rest[:4], rest[4:]
        s = pl.program_id(0)
        x = x_ref[...]
        for b in range(2):
            columns = pl.ds(b * 512, 512)
            stage[s, b] = (dot(x[:512], own_ref[:, columns], TN) + dot(x[512:], other_ref[:, columns], TN)).astype(BF)

        def copy_for(n, k, target):
            row = pl.multiple_of((m[3] ^ z_relative(k // 2, k % 2)) * 128, 128)
            return [pltpu.make_async_copy(stage.at[n, :, pl.ds(row, 128), :], target, sem.at[n * 4 + k])]

        push(s, outs, copy_for)

    out_specs, out_shape = piece_outputs(2, 128)
    return kernel_call(
        kernel,
        meta,
        (activated, own, other),
        [spec((1024, 512), lambda s, m: (0, rel_chip(s, m))), whole((512, 1024)), whole((512, 1024))],
        out_specs,
        out_shape,
        [pltpu.VMEM((4, 2, 512, 512), BF), pltpu.SemaphoreType.DMA((16,))],
        flops=2 * 1024 * 1024 * 2048,
        moved=10 << 20,
    )


def weigh_up(meta, normed_own, normed_other, du):
    def kernel(m, own_ref, other_ref, du_ref, *rest):
        outs, (up, sem) = rest[:4], rest[4:]
        s = pl.program_id(0)
        for b in range(4):
            columns = pl.ds(b * 512, 512)
            up[s, b] = (dot(own_ref[...], du_ref[:512, columns], TN) + dot(other_ref[...], du_ref[512:, columns], TN)).astype(BF)

        def copy_for(n, k, target):
            z = m[3] ^ z_relative(k // 2, k % 2)
            copies = []
            for rel in range(2):
                row = pl.multiple_of((m[2] ^ rel) * 128 + z * 32, 32)
                copies.append(
                    pltpu.make_async_copy(
                        up.at[n, :, pl.ds(row, 32), :],
                        target.at[pl.ds(rel * 4, 4)],
                        sem.at[(n * 4 + k) * 2 + rel],
                    )
                )
            return copies

        push(s, outs, copy_for)

    out_specs, out_shape = piece_outputs(8, 32)
    return kernel_call(
        kernel,
        meta,
        (normed_own, normed_other, du),
        [
            spec((512, 256), lambda s, m: (0, rel_chip(s, m))),
            spec((512, 256), lambda s, m: (0, rel_chip(s, m))),
            whole((1024, 2048)),
        ],
        out_specs,
        out_shape,
        [pltpu.VMEM((4, 4, 256, 512), BF), pltpu.SemaphoreType.DMA((32,))],
        flops=2 * 1024 * 1024 * 2048,
        moved=15 << 20,
    )


def weigh_qkv(meta, hidden, dqkv, out_terms=()):
    def kernel(m, x_ref, d_ref, *rest):
        s = pl.program_id(0)
        if out_terms:
            mixed_ref, more_ref, own_ref, other_ref = rest[:4]
            rest = rest[4:]
        outs, stage, sem = rest[:4], rest[4], rest[5]
        for t in range(3):
            stage[s, t] = dot(x_ref[...], d_ref[t], TN).astype(BF)
        if out_terms:
            stage_out, sem_out = rest[6:]
            x = jnp.where(rel_chip(s, m) < 2, mixed_ref[...].astype(F32), more_ref[...].astype(F32)).astype(BF)
            for b in range(4):
                columns = pl.ds(b * 256, 256)
                stage_out[s, b] = (
                    dot(x[:512], own_ref[:, columns], TN) + dot(x[512:], other_ref[:, columns], TN)
                ).astype(BF)

        def copy_for(n, k, target):
            z = m[3] ^ z_relative(k // 2, k % 2)
            copies = []
            for rel in range(2):
                row = pl.multiple_of((m[2] ^ rel) * 128 + z * 32, 32)
                copies.append(
                    pltpu.make_async_copy(
                        stage.at[n, :, pl.ds(row, 32), :],
                        target.at[pl.ds(rel * 3, 3)],
                        sem.at[(n * 4 + k) * 2 + rel],
                    )
                )
            if out_terms:
                copies.append(
                    pltpu.make_async_copy(
                        stage_out.at[n, :, pl.ds(pl.multiple_of(z * 32, 32), 32), :],
                        target.at[pl.ds(6, 4)],
                        sem_out.at[n * 4 + k],
                    )
                )
            return copies

        push(s, outs, copy_for)

    out_specs, out_shape = piece_outputs(10 if out_terms else 6, 32, 256)
    in_specs = [spec((1024, 256), lambda s, m: (0, rel_chip(s, m))), whole((3, 1024, 256))]
    scratch = [pltpu.VMEM((4, 3, 256, 256), BF), pltpu.SemaphoreType.DMA((32,))]
    if out_terms:
        in_specs += [spec((1024, 128), lambda s, m: (0, rel_chip(s, m) % 2))] * 2 + [whole((512, 1024))] * 2
        scratch += [pltpu.VMEM((4, 4, 128, 256), BF), pltpu.SemaphoreType.DMA((16,))]
    return kernel_call(
        kernel,
        meta,
        (hidden, dqkv, *out_terms),
        in_specs,
        out_specs,
        out_shape,
        scratch,
        flops=2 * 1024 * 1024 * 1024,
        moved=8 << 20,
    )


def qkv_back(meta, dqkv, pieces):
    def kernel(m, d_ref, e_ref, *rest):
        refs, (send_ref, own_ref, weight, sem) = rest[:4], rest[4:]
        i = pl.program_id(0)

        @pl.when(i == 0)
        def _():
            load_all(load_qkv(m, refs, weight, sem))

        total = jnp.zeros((256, 1024), F32)
        for t in range(3):
            total += dot(d_ref[t], weight[t, :, :256], NT) + dot(e_ref[t], weight[t, :, 256:], NT)

        @pl.when(i < 2)
        def _():
            send_ref[...] = total.astype(BF)

        @pl.when(i >= 2)
        def _():
            own_ref[...] = total

    return kernel_call(
        kernel,
        meta,
        (*dqkv, *pieces),
        [spec((3, 256, 256), lambda i, m: (0, turned(i), 0))] * 2 + [HBM] * 4,
        [spec((256, 1024), lambda i, m: (low_block(i), 0)), spec((256, 1024), lambda i, m: (high_block(i), 0))],
        [shaped((512, 1024), BF), shaped((512, 1024), F32)],
        [pltpu.VMEM((3, 1024, 512), BF), pltpu.SemaphoreType.DMA((96,))],
        flops=2 * 1024 * 1024 * 1536,
        moved=9 << 20,
    )


def last_sum(meta, resid, own, received):
    def kernel(m, resid_ref, own_ref, recv_ref, out_ref, sum_ref):
        total = resid_ref[...] + own_ref[...] + recv_ref[...].astype(F32)
        out_ref[...] = total.astype(BF)
        row_sums(sum_ref, pl.program_id(0), (total,))

    block = spec((256, 1024), BY_ROWS)
    return kernel_call(
        kernel,
        meta,
        (resid, own, received),
        [block, block, block],
        [block, whole((8, 1024))],
        [shaped((512, 1024), BF), shaped((8, 1024), F32)],
        grid=(2,),
        flops=512 * 1024 * 4,
        moved=6 << 20,
    )


VECTOR_SIZES = (64, 32, 32, 32, 128, 32, 32, 32)


def split_vectors(packed):
    parts, start = [], 0
    for size in VECTOR_SIZES:
        parts.append(packed[:, start : start + size])
        start += size
    return parts


def chip_body(
    tokens,
    timestep,
    segment_ids,
    cotangent,
    time_weight,
    qkv_weight,
    qv_bias,
    out_weight,
    out_bias,
    norm_gain,
    norm_bias,
    up_weight,
    up_bias,
    down_weight,
    down_bias,
    final_gain,
    final_bias,
):
    dp, z = lax.axis_index("dp"), lax.axis_index("sp")
    y, x, c = dp // 4, (dp // 2) % 2, dp % 2
    meta = jnp.stack([y, x, c, z]).astype(jnp.int32)
    pick = lambda value, index, axis: lax.dynamic_index_in_dim(value, index, axis, keepdims=False)

    me = dp * 4 + z

    qkv_split = qkv_weight.reshape(32, 3, 4, 2, 128)
    up_split = up_weight.reshape(32, 4, 2, 512)
    qkv_half = lambda core: pick(qkv_split, core, 3).reshape(32, 3, 512).transpose(1, 0, 2).reshape(96, 512)
    up_half = lambda core: pick(up_split, core, 2).transpose(1, 0, 2)
    small = jnp.concatenate([qv_bias, out_bias, norm_gain, norm_bias, up_bias, down_bias, final_gain, final_bias])
    small = jnp.pad(small[None], ((0, 15), (0, 128)))
    received = send(jnp.concatenate([qkv_half(1 - c), small]), PAIR)
    small = jnp.concatenate([small[:1], received[96:97], small[2:]])
    out_shard = out_weight.reshape(32, 2, 512).transpose(1, 0, 2).reshape(64, 512)
    qkv_shard = jnp.concatenate([qkv_half(c), received[:96], out_shard, small])
    up_shard = jnp.concatenate([up_half(c), send(up_half(1 - c), PAIR)])
    down_shard = down_weight.reshape(128, 2, 512).transpose(1, 0, 2)
    qkv_line = gather_line(qkv_shard)

    stamps = after(timestep.astype(jnp.int32), received)[:, None]
    stamps = jnp.concatenate([stamps // 64, stamps % 64], axis=1).astype(BF)
    for pairs in (PAIR, ALONG_X, ALONG_Y):
        stamps = jnp.concatenate([stamps, send(stamps, pairs)])
    stamps = stamps.astype(F32)
    stamps = (stamps[:, 0] * 64.0 + stamps[:, 1]).reshape(4, 4)
    sums_order = jnp.arange(4, dtype=jnp.int32) ^ z
    from_pair = (sums_order // 2) ^ c
    stamps = jnp.take_along_axis(stamps, jnp.broadcast_to(from_pair * 2 + sums_order % 2, (4, 4)), axis=1).reshape(16, 1)
    column = me * 32 + jnp.arange(32, dtype=jnp.int32)
    frequency = jnp.exp(-math.log(10000.0) * (column % 512).astype(F32) / 512)
    phases = stamps * frequency[None, :]
    features = jnp.where(column[None, :] < 512, jnp.sin(phases), jnp.cos(phases)).astype(BF)
    features = after(features, qkv_line[0])
    embedded = jnp.dot(features, time_weight, preferred_element_type=F32)
    embedded = embedded + send(embedded, PAIR)
    for width, pairs in ((8, ALONG_Y), (4, ALONG_X), (2, ALONG_Z[2]), (1, ALONG_Z[1])):
        embedded = embedded[:width] + send(embedded[width:], pairs)

    qkv_pieces = gather_plane(*qkv_line)

    def take_rows(value, *earlier):
        return jnp.stack(after([send(pick(value, (z + k) % 2, 0), ROW_OUT[k]) for k in range(2)], earlier))

    def give_rows(value, *earlier):
        parts = after([send(value[k * 256 : (k + 1) * 256], ROW_BACK[k]) for k in range(2)], earlier)
        swapped = (z % 2) == 1
        return jnp.stack([jnp.where(swapped, parts[1], parts[0]), jnp.where(swapped, parts[0], parts[1])])

    documents = jnp.concatenate([segment_ids // 32, segment_ids % 32], axis=1).astype(BF)
    documents = jnp.pad(documents[:, None, :], ((0, 0), (0, 15), (0, 512)))
    own_tokens = take_rows(after(jnp.concatenate([tokens, documents], axis=1), qkv_line))
    other_tokens = send(own_tokens, PAIR)
    codes = jnp.concatenate([own_tokens[:, 256], other_tokens[:, 256]]).astype(F32)
    segments = (codes[:, :256] * 32.0 + codes[:, 256:512]).reshape(1024)
    seg_column, seg_row = segments[:, None], segments[None, :]

    up_far = send(after(up_shard, own_tokens), ALONG_Z[2])

    natural = jnp.arange(32, dtype=jnp.int32)
    order = (natural[:, None] ^ me) == natural[None, :]
    small = jnp.stack([piece[:, :, 256:258, :384] for piece in qkv_pieces])
    small = jnp.stack(
        [
            small[half * 2 + (x_rel if half else y_rel), y_rel if half else x_rel, j, rel]
            for y_rel in range(2)
            for x_rel in range(2)
            for rel in range(2)
            for j in range(2)
            for half in range(2)
        ]
    )
    small = jnp.dot(order.astype(BF), small, preferred_element_type=F32)
    full = [part.reshape(1, -1) for part in split_vectors(small)]
    qv_full, out_shift, first_gain, first_shift, up_full, down_shift, second_gain, second_shift = full
    blank = jnp.zeros((2, 1024), F32)
    vectors = jnp.concatenate([out_shift, first_gain, first_shift, down_shift, second_gain, second_shift, blank])
    qv_mine = pick(qv_full.reshape(2, 4, 2, 128), c, 2).reshape(2, 512)
    qkv_shift = jnp.stack([qv_mine[0], jnp.zeros((512,), F32), qv_mine[1]])
    up_shift = pick(up_full.reshape(4, 2, 512), c, 1).reshape(1, 2048)

    hidden, qkv = project_qkv(meta, own_tokens, other_tokens, embedded, qkv_shift, qkv_pieces)
    up_first = jnp.stack([after(up_shard, qkv), up_far])
    mixed_one, lse_one = attend(meta, 0, after(qkv, up_first), seg_column, seg_row)
    up_second = after(send(up_first, ALONG_Z[1]), mixed_one)
    up_near = after(gather_near(up_first), mixed_one)
    mixed_two, lse_two = attend(meta, 1, after(qkv, up_second, up_near), seg_column, seg_row)
    up_more = after(gather_near(up_second), mixed_two)
    down_first = jnp.stack([after(down_shard, mixed_two), send(after(down_shard, up_second), ALONG_Z[2])])
    down_second = send(down_first, ALONG_Z[1])
    up_pieces = gather_far(up_first, up_near, up_second, up_more)
    mixed = mixed_one, after(mixed_two, down_second, up_pieces)
    away, mine = project_out(meta, mixed, qkv_pieces)
    down_pieces = gather_plane(down_first, down_second, mine)
    away = after(away, down_pieces[0], down_pieces[2])
    normal_one, inverse_one, normed = first_norm(meta, own_tokens, embedded, mine, send(away, PAIR), vectors)
    normed_other = send(normed, PAIR)
    normed_other = after(normed_other, down_pieces[0], down_pieces[2])
    activated, slope = expand(meta, normed, normed_other, up_shift, up_pieces)
    own_cotangent = take_rows(after(cotangent, normed), activated).reshape(512, 1024)
    away, mine = contract(meta, after(activated, own_cotangent), down_pieces)
    result, resid_two, df, sums_two = second_norm(meta, normal_one, mine, send(away, PAIR), own_cotangent, vectors)

    df_other = send(df, PAIR)
    down_terms = weigh_down(meta, activated, df, df_other)
    du, away, mine, bias_sums = feed_back(meta, after(df, down_terms), df_other, slope, down_pieces, up_pieces)
    received = send(away, PAIR)
    up_terms = weigh_up(meta, normed, normed_other, du)
    output = give_rows(after(result, down_terms), up_terms)
    down_sums = add_one(*scatter_one(*down_terms), up_terms)
    resid_one, da, sums_one = first_norm_back(
        meta, after(resid_two, down_sums, output), mine, received, normal_one, inverse_one, vectors
    )
    da_other = send(da, PAIR)
    down_sums = scatter_two(*down_sums)
    up_sums = scatter_one(*after(up_terms, da))
    heads = lambda part, mixed, lse, own: attend_back_part(
        meta, part, qkv, mixed, lse, seg_column, seg_row, own, da_other, qkv_pieces
    )
    dqkv_one, qv_sums_one = heads(0, mixed_one, lse_one, da)
    down_sums = add_two(*down_sums, dqkv_one)
    dqkv_one = after(dqkv_one, down_sums)
    qkv_terms_one = weigh_qkv(meta, hidden, dqkv_one, (mixed_one, mixed_two, da, da_other))
    up_sums = add_one(*up_sums, qkv_terms_one)
    dqkv_two, qv_sums_two = heads(1, mixed_two, lse_two, after(da, qkv_terms_one, up_sums))
    down_sums = add_three(*scatter_three(*down_sums), dqkv_two)
    up_sums = add_two(*scatter_two(*up_sums), dqkv_two)
    qkv_sums_one = add_one(*scatter_one(*qkv_terms_one), dqkv_two)
    dqkv_two = after(dqkv_two, up_sums, qkv_sums_one, down_sums)
    away, mine = qkv_back(meta, (dqkv_one, dqkv_two), qkv_pieces)
    received = send(away, PAIR)
    qkv_sums_one = add_two(*scatter_two(*qkv_sums_one), mine)
    up_sums = add_three(*scatter_three(*up_sums), mine)
    down_share = scatter_four(*down_sums, mine)
    qkv_terms_two = weigh_qkv(meta, hidden, after(dqkv_two, mine, qkv_sums_one))
    qkv_sums_one = add_three(*scatter_three(*qkv_sums_one), qkv_terms_two)
    input_low, embed_sums = last_sum(meta, resid_one, after(mine, qkv_terms_two), received)
    input_grad = give_rows(input_low)
    up_share = scatter_four(*up_sums, input_low)
    qkv_sums_two = add_two(*scatter_two(*add_one(*scatter_one(*qkv_terms_two), input_low)))
    qkv_sums_two = add_three(*scatter_three(*qkv_sums_two))
    qkv_share_one = scatter_four(*after(qkv_sums_one, input_grad))
    qkv_share_two = scatter_four(*after(qkv_sums_two, input_grad))
    qkv_share = jnp.concatenate([qkv_share_one[:6], qkv_share_two], axis=2)
    qv_sums = jnp.concatenate([qv_sums_one[0:2], qv_sums_two[0:2]], axis=1)

    def both_halves(own, received):
        return jnp.where(c == 0, jnp.stack([own, received], axis=-2), jnp.stack([received, own], axis=-2))

    grad_down = down_share.transpose(1, 0, 2).reshape(128, 1024)
    grad_out = qkv_share_one[6:].transpose(1, 0, 2).reshape(32, 1024)
    grad_up = both_halves(up_share[:4], send(up_share[4:], PAIR))
    grad_up = grad_up.transpose(1, 0, 2, 3).reshape(32, 4096)
    split = lambda share: share.reshape(3, 32, 4, 128)
    grad_qkv = both_halves(split(qkv_share[:3]), split(send(qkv_share[3:], PAIR)))
    grad_qkv = grad_qkv.transpose(1, 0, 2, 3, 4).reshape(32, 3072)

    qv_sums, bias_sums, sums_one, sums_two = after((qv_sums, bias_sums, sums_one, sums_two), input_low)
    core_lane = (jnp.arange(2) == c).astype(F32)
    spread = lambda sums, width: (sums.reshape(-1, 1, width) * core_lane[None, :, None]).reshape(32, -1)
    grads = jnp.concatenate(
        [
            spread(qv_sums, 128),
            sums_one[2].reshape(32, 32),
            sums_one[0].reshape(32, 32),
            sums_one[1].reshape(32, 32),
            spread(bias_sums[0:1], 512),
            sums_two[2].reshape(32, 32),
            sums_two[0].reshape(32, 32),
            sums_two[1].reshape(32, 32),
        ],
        axis=1,
    )
    total = jnp.dot(order.astype(F32), grads, precision=lax.Precision.HIGHEST)
    total = total.reshape(4, 2, 4, 3, 128).transpose(1, 0, 2, 3, 4).reshape(96, 128)
    sums = embed_sums[0:1].reshape(8, 128)
    received = send(jnp.concatenate([total[48:], sums]), PAIR)
    total, sums = total[:48] + received[:48], sums + received[48:]
    for width, pairs in ((24, ALONG_Y), (12, ALONG_X), (6, ALONG_Z[2]), (3, ALONG_Z[1])):
        message = jnp.concatenate([total[width:], sums])
        received = send(after(message, input_grad) if width == 6 else message, pairs)
        total, sums = total[:width] + received[:width], jnp.concatenate([sums, received[width:]])
    small_grads = [part.reshape(-1) for part in split_vectors(total.reshape(1, 384))]
    sums = sums.reshape(2, 2, 2, 2, 1024).transpose(3, 2, 1, 0, 4).reshape(16, 1024)
    grad_time = jnp.dot(features.astype(F32).T, sums, precision=lax.Precision.HIGHEST)

    return (
        output,
        input_grad,
        grad_time,
        grad_qkv,
        small_grads[0],
        grad_out,
        *small_grads[1:4],
        grad_up,
        small_grads[4],
        grad_down,
        *small_grads[5:],
    )


def solution(mesh):
    in_specs = (
        P("dp", "sp", None),
        P("dp"),
        P("dp", "sp"),
        P("dp", "sp", None),
        P(("dp", "sp"), None),
        P(("dp", "sp"), None),
        P(("dp", "sp")),
        P(("dp", "sp"), None),
        P(("dp", "sp")),
        P(("dp", "sp")),
        P(("dp", "sp")),
        P(("dp", "sp"), None),
        P(("dp", "sp")),
        P(("dp", "sp"), None),
        P(("dp", "sp")),
        P(("dp", "sp")),
        P(("dp", "sp")),
    )
    out_specs = (
        P("dp", "sp", None),
        P("dp", "sp", None),
        P(("dp", "sp"), None),
        P(("dp", "sp"), None),
        P(("dp", "sp")),
        P(("dp", "sp"), None),
        P(("dp", "sp")),
        P(("dp", "sp")),
        P(("dp", "sp")),
        P(("dp", "sp"), None),
        P(("dp", "sp")),
        P(("dp", "sp"), None),
        P(("dp", "sp")),
        P(("dp", "sp")),
        P(("dp", "sp")),
    )
    plan = chip_body if dict(mesh.shape) == {"dp": 8, "sp": 4} else body
    return jax.shard_map(plan, mesh=mesh, in_specs=in_specs, out_specs=out_specs, check_vma=False)
```
